128 devices in a mesh: dp: 4 (over y), retr: 32 (over z, x, core).
Axes of the slice: x: 4, y: 4, z: 4, core: 2. Of those that a mesh axis runs over, the one named last changes fastest.
Arguments:
- query: bfloat16 [1024, 64, 2048], P(('dp', 'retr')), may hold values from -20 to 20
- grad_out: bfloat16 [1024, 64, 2048], P(('dp', 'retr')), may hold values from -12 to 12
- keys: bfloat16 [192, 128, 2048], P('retr'), may hold values from -4 to 4
- values: bfloat16 [192, 128, 2048], P('retr'), may hold values from -4 to 4
- owner_list: int32 [1024, 2], P(('dp', 'retr')), may hold values from 0 to 31, as said below
- row_list: int32 [1024, 2], P(('dp', 'retr')), may hold values from 0 to 5
Outputs:
- grad_query: bfloat16 [1024, 64, 2048], P(('dp', 'retr'))
- grad_keys: bfloat16 [192, 128, 2048], P('retr', 'dp')
- grad_values: bfloat16 [192, 128, 2048], P('retr', 'dp')
The draws below stay inside these ranges and needn't reach their ends.
Inputs may be any that keep to these rules, and one draw needn't show every extreme that they name: `owner_list`: spans lie on devices in blocks of 8; the 16 entries of one block name any one owner at most 1 times, and in every draw some owners are named exactly 1 times by every block. Owners are indices along retr within the span's own dp group.
All inputs are finite; a program needn't handle non-finite values.
Results may differ from the reference program's by a relative error of at most 0.0076.
Values may be sent and summed in bfloat16 or wider, within the bound.
A program may use at most 256 MiB of HBM per device.

```python
import jax
import jax.numpy as jnp
from jax import lax

HEADS = 16
HD = 128
SPAN = 64
NTOK = 128
CH_DEV = 8
NB_DEV = 6
HW = 2048
SPANS = 1024
ROWS = 192
N_RETR = 32


def draw_query(key, part):
    key = jax.random.fold_in(key, 21)
    drawn = jnp.clip(jax.random.normal(key, (SPANS, SPAN, HW), jnp.float32), -6.0, 6.0)
    return drawn.astype(jnp.bfloat16)


def draw_keys(key, part):
    key = jax.random.fold_in(key, 22)
    noise = jnp.clip(jax.random.normal(key, (ROWS, NTOK, HW), jnp.float32), -4.0, 4.0)
    return noise.astype(jnp.bfloat16)


def draw_owner_list(key, part):
    key = jax.random.fold_in(key, 23)
    capacity = 4 * CH_DEV // N_RETR
    favourite_count = max(1, N_RETR // 8)
    shuffled = jax.random.permutation(jax.random.fold_in(key, 1), N_RETR)
    standing = jnp.argsort(shuffled)
    favoured = (standing < favourite_count).astype(jnp.int32)
    positions = jnp.arange(N_RETR * capacity, dtype=jnp.int32)
    uplift = favoured[positions // capacity] * (N_RETR * capacity)

    def block_owners(index):
        shuffle = jax.random.permutation(jax.random.fold_in(key, index + 2), N_RETR * capacity).astype(jnp.int32)
        chosen = jax.lax.top_k(shuffle + uplift, 2 * CH_DEV)[1]
        return (chosen // capacity).astype(jnp.int32)
    owners = jax.vmap(block_owners)(jnp.arange(SPANS // CH_DEV, dtype=jnp.int32))
    return owners.reshape(SPANS, 2).astype(jnp.int32)


def place_ends(values, rng, least, largest):
    longest = values.shape.index(max(values.shape))
    spots = []
    for shift in (0, 1):
        where = [jax.random.randint(jax.random.fold_in(rng, axis), (), 0, length) for axis, length in enumerate(values.shape)]
        where[longest] = (where[longest] + shift) % values.shape[longest]
        spots.append(tuple(where))
    return values.at[spots[0]].set(least).at[spots[1]].set(largest)


def level_of(key, dims, cuts, smallest, high):
    factor_of = 1.0
    for dim, shards_of in cuts:
        heights = jax.random.uniform(jax.random.fold_in(jax.random.fold_in(key, 6), dim), (shards_of,), jnp.float32, smallest / len(cuts), high / len(cuts))
        factor_of = factor_of * jnp.repeat(jnp.exp(heights), dims[dim] // shards_of).reshape((-1,) + (1,) * (len(dims) - 1 - dim))
    return factor_of


def scatter_about(key, extent, width, bound, cuts=(), kind=jnp.bfloat16):
    values = jax.random.normal(key, extent, jnp.float32) * width
    if len(cuts) > 0:
        values = level_of(key, extent, cuts, -0.22, 0.18) * values
    return jnp.clip(values, min=-bound, max=bound).astype(kind)


def setup_inputs(seed: int = 0) -> dict:
    arg_keys = jax.random.split(jax.random.key(seed), 7)
    query = draw_query(jax.random.fold_in(arg_keys[6], 71), 0)
    grad_out = scatter_about(arg_keys[1], (SPANS, SPAN, HW), 2.0, 12.0, ((0, 128),))
    keys = draw_keys(jax.random.fold_in(arg_keys[6], 71), 0)
    values = scatter_about(arg_keys[3], (ROWS, NTOK, HW), 1.0, 4.0, ((0, 32),))
    owner_list = draw_owner_list(jax.random.fold_in(arg_keys[6], 71), 0)
    row_list = place_ends(jax.random.randint(arg_keys[5], (SPANS, 2), 0, NB_DEV), jax.random.fold_in(arg_keys[5], 1), 0, NB_DEV - 1).astype(jnp.int32)
    return dict(query=query, grad_out=grad_out, keys=keys, values=values, owner_list=owner_list, row_list=row_list)


def reference(query, grad_out, keys, values, owner_list, row_list):
    scaling = HD ** -0.5
    row_index = (owner_list * NB_DEV + row_list).astype(jnp.int32)
    per_block = CH_DEV
    blocks_total = SPANS // per_block

    def advance(carry, pieces):
        key_acc, value_acc = carry
        query_part, grad_part, index_part = pieces
        flat_index = index_part.reshape(-1)
        key_rows = jnp.take(keys, flat_index, axis=0).astype(jnp.float32).reshape(per_block, 2, NTOK, HEADS, HD)
        value_rows = jnp.take(values, flat_index, axis=0).astype(jnp.float32).reshape(per_block, 2, NTOK, HEADS, HD)
        queries = query_part.astype(jnp.float32).reshape(per_block, SPAN, HEADS, HD)
        grads = grad_part.astype(jnp.float32).reshape(per_block, SPAN, HEADS, HD)
        scores = jnp.einsum('cqhd,cnkhd->chqnk', queries, key_rows) * scaling
        flattened = scores.reshape(per_block, HEADS, SPAN, 2 * NTOK)
        log_norm = jax.nn.logsumexp(flattened, axis=-1)
        dprob = jnp.einsum('cqhd,cnkhd->chqnk', grads, value_rows)
        chance = jnp.exp(scores - log_norm[..., None, None])
        deltas = jnp.sum(chance * dprob, axis=(3, 4))
        chance_low = lax.optimization_barrier(chance.astype(jnp.bfloat16)).astype(jnp.float32)
        dscore = lax.optimization_barrier((scaling * chance * (dprob - deltas[..., None, None])).astype(jnp.bfloat16)).astype(jnp.float32)
        value_terms = jnp.einsum('chqnk,cqhd->cnkhd', chance_low, grads).reshape(per_block * 2, NTOK, HW)
        key_terms = jnp.einsum('chqnk,cqhd->cnkhd', dscore, queries).reshape(per_block * 2, NTOK, HW)
        query_terms = jnp.einsum('chqnk,cnkhd->cnqhd', dscore, key_rows)
        query_low = lax.optimization_barrier(query_terms.astype(jnp.bfloat16)).astype(jnp.float32)
        grad_query = (query_low[:, 0] + query_low[:, 1]).reshape(per_block, SPAN, HW).astype(jnp.bfloat16)
        key_acc = key_acc.at[flat_index].add(key_terms)
        value_acc = value_acc.at[flat_index].add(value_terms)
        return (key_acc, value_acc), grad_query

    initial = jnp.zeros((ROWS, NTOK, HW), jnp.float32)
    (key_acc, value_acc), grads_query = lax.scan(
        advance, (initial, initial),
        (query.reshape(blocks_total, per_block, SPAN, HW),
         grad_out.reshape(blocks_total, per_block, SPAN, HW),
         row_index.reshape(blocks_total, per_block, 2)))
    return grads_query.reshape(SPANS, SPAN, HW), key_acc.astype(jnp.bfloat16), value_acc.astype(jnp.bfloat16)
```

```python
import functools

import jax
import jax.numpy as jnp
import numpy as np
from jax import lax
from jax.experimental import pallas as pl
from jax.experimental.pallas import tpu as pltpu
from jax.sharding import Mesh
from jax.sharding import PartitionSpec as P

HD = 128
MiB = 1024 * 1024
ANY = pl.BlockSpec(memory_space=pl.ANY)
VMEM = pl.BlockSpec(memory_space=pltpu.VMEM)
SMEM = pl.BlockSpec(memory_space=pltpu.SMEM)


def place():
    return tuple(lax.axis_index(name) for name in ("y", "z", "x", "c"))


def remote(src, dst, send, recv, where):
    return pltpu.make_async_remote_copy(
        src_ref=src,
        dst_ref=dst,
        send_sem=send,
        recv_sem=recv,
        device_id=where,
        device_id_type=pl.DeviceIdType.MESH,
    )


def greet(nz, nx):
    y, z, x, c = place()
    barrier = pltpu.get_barrier_semaphore()

    def hello(where):
        pl.semaphore_signal(barrier, inc=1, device_id=where, device_id_type=pl.DeviceIdType.MESH)

    @pl.loop(1, nz * nx)
    def _(d):
        hello((y, lax.rem(z + d // nx, nz), lax.rem(x + lax.rem(d, nx), nx), c))

    hello((lax.rem(y + 1, 4), z, x, c))
    hello((lax.rem(y + 3, 4), z, x, c))
    hello((y, z, x, 1 - c))
    pl.semaphore_wait(barrier, nz * nx - 1 + 3)


def bring_kernel(
    nz, nx,
    q_ref, g_ref, k_ref, v_ref, i_ref,
    qh, gh, ka, va, ih,
    s_in, r_in, s_y, r_y, s_c, r_c, own,
):
    y, z, x, c = place()
    chips = nz * nx
    rows = k_ref.shape[0]
    part = chips * rows
    quarter = k_ref.shape[1] // 4
    me = z * nx + x
    up, down, far = lax.rem(y + 1, 4), lax.rem(y + 3, 4), lax.rem(y + 2, 4)
    greet(nz, nx)

    def columns(head):
        return pl.ds(pl.multiple_of(head * HD, HD), HD)

    def token_part(ref, head):
        return ref.at[:, pl.ds(pl.multiple_of(y * quarter, quarter), quarter), columns(head)]

    def landing(ref):
        return ref.at[y, pl.ds(c * part + me * rows, rows)]

    def to_chip(d):
        pz, px = lax.rem(z + d // nx, nz), lax.rem(x + lax.rem(d, nx), nx)
        head = pz * nx + px
        where = (y, pz, px, c)
        return (
            remote(token_part(k_ref, head), landing(ka), s_in.at[0, d], r_in.at[0, d], where),
            remote(token_part(v_ref, head), landing(va), s_in.at[1, d], r_in.at[1, d], where),
            remote(q_ref.at[:, :, columns(head)], qh.at[me], s_in.at[2, d], r_in.at[2, d], where),
            remote(g_ref.at[:, :, columns(head)], gh.at[me], s_in.at[3, d], r_in.at[3, d], where),
            remote(i_ref, ih.at[me], s_in.at[4, d], r_in.at[4, d], where),
        )

    mine = (
        pltpu.make_async_copy(token_part(k_ref, me), landing(ka), own.at[0]),
        pltpu.make_async_copy(token_part(v_ref, me), landing(va), own.at[1]),
        pltpu.make_async_copy(q_ref.at[:, :, columns(me)], qh.at[me], own.at[2]),
        pltpu.make_async_copy(g_ref.at[:, :, columns(me)], gh.at[me], own.at[3]),
        pltpu.make_async_copy(i_ref, ih.at[me], own.at[4]),
    )

    @pl.loop(1, chips)
    def _(d):
        copies = to_chip(d)
        copies[0].start()
        copies[1].start()

    for copy in mine:
        copy.start()

    def chunk(ref, at, core):
        return ref.at[at, pl.ds(core * part, part)]

    def along_y(ref, t, at, slot, where):
        return remote(
            chunk(ref, at, c), chunk(ref, at, c), s_y.at[t, slot], r_y.at[t, slot], (where, z, x, c)
        )

    def across(ref, t, at, slot):
        return remote(
            chunk(ref, at, c), chunk(ref, at, c), s_c.at[t, slot], r_c.at[t, slot], (y, z, x, 1 - c)
        )

    pair = (ka, va)
    for t in (0, 1):

        @pl.loop(1, chips)
        def _(d):
            to_chip(d)[t].wait_recv()

        mine[t].wait()
        along_y(pair[t], t, y, 0, up).start()
        along_y(pair[t], t, y, 1, down).start()
        across(pair[t], t, y, 0).start()

    @pl.loop(1, chips)
    def _(d):
        for copy in to_chip(d)[2:]:
            copy.start()

    for t in (0, 1):
        along_y(pair[t], t, down, 0, up).wait_recv()
        if t == 0:
            along_y(pair[t], t, down, 2, up).start()
        across(pair[t], t, down, 1).start()
        along_y(pair[t], t, up, 1, down).wait_recv()
        if t == 1:
            along_y(pair[t], t, up, 2, down).start()
        across(pair[t], t, up, 2).start()
    for t in (0, 1):
        along_y(pair[t], t, far, 2, up).wait_recv()
        across(pair[t], t, far, 3).start()

    @pl.loop(1, chips)
    def _(d):
        copies = to_chip(d)
        for copy in copies[2:]:
            copy.wait_recv()
        for copy in copies:
            copy.wait_send()

    for copy in mine[2:]:
        copy.wait()
    for t in (0, 1):
        for slot in range(3):
            along_y(pair[t], t, y, slot, up).wait_send()
        for slot in range(4):
            across(pair[t], t, y, slot).wait()


def bring(nz, nx, query, grad_out, keys, values, entry):
    chips = nz * nx
    rows, tokens, _ = keys.shape
    spans, span_len, _ = query.shape
    bf16 = jnp.bfloat16
    held = jax.ShapeDtypeStruct((4, 2 * chips * rows, tokens // 4, HD), bf16)
    heads = jax.ShapeDtypeStruct((chips, spans, span_len, HD), bf16)
    dma = pltpu.SemaphoreType.DMA
    return pl.pallas_call(
        functools.partial(bring_kernel, nz, nx),
        name="bring",
        out_shape=(heads, heads, held, held, jax.ShapeDtypeStruct((chips,) + entry.shape, jnp.int32)),
        in_specs=[ANY] * 5,
        out_specs=(ANY,) * 5,
        scratch_shapes=[
            dma((5, chips)), dma((5, chips)), dma((2, 3)), dma((2, 3)), dma((2, 4)), dma((2, 4)), dma((5,)),
        ],
        compiler_params=pltpu.CompilerParams(collective_id=0, has_side_effects=True),
    )(query, grad_out, keys, values, entry)


def attend_kernel(
    unroll, i_ref, q_ref, g_ref, k_hbm, v_hbm, dq_ref, dk_hbm, dv_hbm, ka, va, dk, dv, sems
):
    fill = (
        pltpu.make_async_copy(k_hbm, ka, sems.at[0]),
        pltpu.make_async_copy(v_hbm, va, sems.at[1]),
    )
    for copy in fill:
        copy.start()
    quarters, rows, tok, _ = ka.shape
    spans = q_ref.shape[0]
    per = i_ref.shape[1]
    scaling = HD ** -0.5
    to_base2 = scaling * float(np.log2(np.e))

    @pl.loop(0, rows)
    def _(r):
        dk[:, r] = jnp.zeros((quarters, tok, HD), jnp.float32)
        dv[:, r] = jnp.zeros((quarters, tok, HD), jnp.float32)

    for copy in fill:
        copy.wait()

    def contract(a, b, da, db):
        return lax.dot_general(
            a, b, (((da,), (db,)), ((), ())), preferred_element_type=jnp.float32
        )

    def row_of(ref, e):
        return ref[:, e].reshape(quarters * tok, HD)

    @pl.loop(0, spans // unroll)
    def _(step):
        results = []
        for u in range(unroll):
            s = step * unroll + u
            e0 = i_ref[s // per, lax.rem(s, per), 0]
            e1 = i_ref[s // per, lax.rem(s, per), 1]
            q, g = q_ref[s], g_ref[s]
            keys = jnp.concatenate([row_of(ka, e0), row_of(ka, e1)], axis=0)
            values = jnp.concatenate([row_of(va, e0), row_of(va, e1)], axis=0)
            scores = contract(q, keys, 1, 1)
            dprob = contract(g, values, 1, 1)
            top = jnp.max(scores, axis=-1, keepdims=True)
            lifted = jnp.exp2((scores - top) * to_base2)
            inverse = 1.0 / jnp.sum(lifted, axis=-1, keepdims=True)
            delta = jnp.sum(lifted * dprob, axis=-1, keepdims=True) * inverse
            chance = lifted * inverse
            chance_low = chance.astype(jnp.bfloat16)
            dscore = ((chance * scaling) * (dprob - delta)).astype(jnp.bfloat16)
            dq_ref[s] = contract(dscore, keys, 1, 0).astype(jnp.bfloat16)
            results.append((e0, e1, contract(dscore, q, 0, 0), contract(chance_low, g, 0, 0)))
        half = quarters * tok
        for e0, e1, key_terms, value_terms in results:
            dk[:, e0] += key_terms[:half].reshape(quarters, tok, HD)
            dk[:, e1] += key_terms[half:].reshape(quarters, tok, HD)
            dv[:, e0] += value_terms[:half].reshape(quarters, tok, HD)
            dv[:, e1] += value_terms[half:].reshape(quarters, tok, HD)

    drain = (
        pltpu.make_async_copy(ka, dk_hbm, sems.at[0]),
        pltpu.make_async_copy(va, dv_hbm, sems.at[1]),
    )
    for low, total, copy in ((ka, dk, drain[0]), (va, dv, drain[1])):

        @pl.loop(0, rows)
        def _(r):
            low[:, r] = total[:, r].astype(jnp.bfloat16)

        copy.start()
    for copy in drain:
        copy.wait()


def attend(entry, qh, gh, ka, va):
    spans = qh.shape[0] * qh.shape[1]
    flat = (spans,) + qh.shape[2:]
    bf16 = jnp.bfloat16
    held = jax.ShapeDtypeStruct(ka.shape, bf16)
    return pl.pallas_call(
        functools.partial(attend_kernel, 2),
        name="attend",
        out_shape=(jax.ShapeDtypeStruct(flat, bf16), held, held),
        in_specs=[SMEM, VMEM, VMEM, ANY, ANY],
        out_specs=(VMEM, ANY, ANY),
        scratch_shapes=[
            pltpu.VMEM(ka.shape, bf16),
            pltpu.VMEM(ka.shape, bf16),
            pltpu.VMEM(ka.shape, jnp.float32),
            pltpu.VMEM(ka.shape, jnp.float32),
            pltpu.SemaphoreType.DMA((2,)),
        ],
        compiler_params=pltpu.CompilerParams(vmem_limit_bytes=56 * MiB),
        cost_estimate=pl.CostEstimate(
            flops=spans * 10 * 64 * 256 * HD, bytes_accessed=32 * MiB, transcendentals=spans * 64 * 256
        ),
    )(entry, qh.reshape(flat), gh.reshape(flat), ka, va)


def give_kernel(
    nz, nx,
    dq_ref, dk_ref, dv_ref,
    gq, gk, gv,
    mine, other, total, passed, arrived,
    s_q, r_q, s_out, r_out, s_c, r_c, s_f, r_f, s_y, r_y, own_q, own_out, own,
):
    y, z, x, c = place()
    chips = nz * nx
    part = mine.shape[2]
    rows = part // chips
    me = z * nx + x
    up, down, far = lax.rem(y + 1, 4), lax.rem(y + 3, 4), lax.rem(y + 2, 4)
    pair = (dk_ref, dv_ref)
    outs = (gk, gv)
    greet(nz, nx)

    at = (far, up, down, y)

    def across(t, slot):
        return remote(
            pair[t].at[at[slot], pl.ds((1 - c) * part, part)], other.at[slot, t],
            s_c.at[slot, t], r_c.at[slot, t], (y, z, x, 1 - c),
        )

    def fetch(t, slot):
        return pltpu.make_async_copy(
            pair[t].at[at[slot], pl.ds(c * part, part)], mine.at[slot, t], own.at[slot, t]
        )

    for slot in range(4):
        for t in (0, 1):
            across(t, slot).start()
            fetch(t, slot).start()

    def columns(head):
        return pl.ds(pl.multiple_of(head * HD, HD), HD)

    def chip(d):
        pz, px = lax.rem(z + d // nx, nz), lax.rem(x + lax.rem(d, nx), nx)
        return pz * nx + px, (y, pz, px, c)

    def query_out(d):
        head, where = chip(d)
        return remote(dq_ref.at[head], gq.at[:, :, columns(me)], s_q.at[d], r_q.at[d], where)

    def key_out(d, t):
        head, where = chip(d)
        return remote(
            total.at[3, t, pl.ds(head * rows, rows)], outs[t].at[:, :, columns(me)],
            s_out.at[t, d], r_out.at[t, d], where,
        )

    query_own = pltpu.make_async_copy(dq_ref.at[me], gq.at[:, :, columns(me)], own_q)
    query_own.start()

    @pl.loop(1, chips)
    def _(d):
        query_out(d).start()

    def f32(a):
        return a.astype(jnp.float32)

    def add(dst, t, slot, *terms):
        @pl.loop(0, part // rows)
        def _(i):
            rs = pl.ds(i * rows, rows)
            sums = f32(terms[0][rs])
            for term in terms[1:]:
                sums = sums + f32(term[rs])
            dst[rs] = sums.astype(jnp.bfloat16)

    def chip_sum(t, slot):
        across(t, slot).wait_recv()
        fetch(t, slot).wait()
        add(total.at[slot, t], t, slot, mine.at[slot, t], other.at[slot, t])

    def far_copy(t):
        return remote(
            total.at[0, t], passed.at[t], s_f.at[t], r_f.at[t], ((up, down)[t], z, x, c)
        )

    def near_copy(t, slot):
        return remote(
            total.at[slot, t], arrived.at[slot - 1, t], s_y.at[slot - 1, t], r_y.at[slot - 1, t],
            ((up, down)[slot - 1], z, x, c),
        )

    for t in (0, 1):
        chip_sum(t, 0)
        far_copy(t).start()
    chip_sum(1, 1)
    near_copy(1, 1).start()
    chip_sum(0, 2)
    near_copy(0, 2).start()
    for t, slot in ((0, 1), (1, 2)):
        across(t, slot).wait_recv()
        fetch(t, slot).wait()
        far_copy(t).wait_recv()
        add(total.at[slot, t], t, slot, mine.at[slot, t], other.at[slot, t], passed.at[t])
        near_copy(t, slot).start()
    for t in (0, 1):
        across(t, 3).wait_recv()
        fetch(t, 3).wait()
    for t in (0, 1):
        near_copy(t, 1).wait_recv()
        near_copy(t, 2).wait_recv()
        add(
            total.at[3, t], t, 3,
            mine.at[3, t], other.at[3, t], arrived.at[0, t], arrived.at[1, t],
        )

        @pl.loop(1, chips)
        def _(d):
            key_out(d, t).start()

        pltpu.make_async_copy(
            total.at[3, t, pl.ds(me * rows, rows)], outs[t].at[:, :, columns(me)], own_out.at[t]
        ).start()

    @pl.loop(1, chips)
    def _(d):
        query_out(d).wait()
        for t in (0, 1):
            key_out(d, t).wait()

    query_own.wait()
    for t in (0, 1):
        pltpu.make_async_copy(
            total.at[3, t, pl.ds(me * rows, rows)], outs[t].at[:, :, columns(me)], own_out.at[t]
        ).wait()
        far_copy(t).wait_send()
        for slot in range(4):
            across(t, slot).wait_send()
        for slot in (1, 2):
            near_copy(t, slot).wait_send()


def give(nz, nx, dq, dk, dv):
    chips = nz * nx
    _, all_rows, tok, _ = dk.shape
    part = all_rows // 2
    _, spans, span_len, _ = dq.shape
    bf16 = jnp.bfloat16
    dma = pltpu.SemaphoreType.DMA
    row_out = jax.ShapeDtypeStruct((part // chips, tok, chips * HD), bf16)
    return pl.pallas_call(
        functools.partial(give_kernel, nz, nx),
        name="give",
        out_shape=(jax.ShapeDtypeStruct((spans, span_len, chips * HD), bf16), row_out, row_out),
        in_specs=[ANY] * 3,
        out_specs=(ANY,) * 3,
        scratch_shapes=[
            pltpu.VMEM((4, 2, part, tok, HD), bf16),
            pltpu.VMEM((4, 2, part, tok, HD), bf16),
            pltpu.VMEM((4, 2, part, tok, HD), bf16),
            pltpu.VMEM((2, part, tok, HD), bf16),
            pltpu.VMEM((2, 2, part, tok, HD), bf16),
            dma((chips,)), dma((chips,)), dma((2, chips)), dma((2, chips)),
            dma((4, 2)), dma((4, 2)), dma((2,)), dma((2,)), dma((2, 2)), dma((2, 2)),
            dma, dma((2,)), dma((4, 2)),
        ],
        compiler_params=pltpu.CompilerParams(
            collective_id=1, has_side_effects=True, vmem_limit_bytes=48 * MiB
        ),
    )(dq, dk, dv)


def on_device(nz, nx, query, grad_out, keys, values, owner_list, row_list):
    chips = nz * nx
    rows = keys.shape[0]
    entry = lax.rem(owner_list, 2) * (chips * rows) + (owner_list // 2) * rows + row_list
    entry = jnp.pad(entry, ((0, 0), (0, HD - entry.shape[1])))
    qh, gh, ka, va, ih = bring(nz, nx, query, grad_out, keys, values, entry)
    dq, dk, dv = attend(ih, qh, gh, ka, va)
    return give(nz, nx, dq.reshape(qh.shape), dk, dv)


def solution(mesh):
    groups, retr = mesh.devices.shape
    nx = 4 if retr == 32 else 2
    nz = retr // (2 * nx)
    fine = Mesh(mesh.devices.reshape(groups, nz, nx, 2), ("y", "z", "x", "c"))
    all_axes = ("y", "z", "x", "c")
    owner = ("z", "x", "c")
    return jax.shard_map(
        functools.partial(on_device, nz, nx),
        mesh=fine,
        in_specs=(
            P(all_axes, None, None),
            P(all_axes, None, None),
            P(owner, None, None),
            P(owner, None, None),
            P(all_axes, None),
            P(all_axes, None),
        ),
        out_specs=(P(all_axes, None, None), P(owner, "y", None), P(owner, "y", None)),
        check_vma=False,
    )
```

```python
import functools

import jax
import jax.numpy as jnp
import numpy as np
from jax import lax
from jax.experimental import pallas as pl
from jax.experimental.pallas import tpu as pltpu
from jax.sharding import Mesh
from jax.sharding import PartitionSpec as P

HD = 128
MiB = 1024 * 1024
ANY = pl.BlockSpec(memory_space=pl.ANY)
VMEM = pl.BlockSpec(memory_space=pltpu.VMEM)
SMEM = pl.BlockSpec(memory_space=pltpu.SMEM)


def place():
    return tuple(lax.axis_index(name) for name in ("y", "z", "x", "c"))


def remote(src, dst, send, recv, where):
    return pltpu.make_async_remote_copy(
        src_ref=src,
        dst_ref=dst,
        send_sem=send,
        recv_sem=recv,
        device_id=where,
        device_id_type=pl.DeviceIdType.MESH,
    )


def greet(nz, nx):
    y, z, x, c = place()
    barrier = pltpu.get_barrier_semaphore()

    def hello(where):
        pl.semaphore_signal(barrier, inc=1, device_id=where, device_id_type=pl.DeviceIdType.MESH)

    @pl.loop(1, nz * nx)
    def _(d):
        hello((y, lax.rem(z + d // nx, nz), lax.rem(x + lax.rem(d, nx), nx), c))

    hello((lax.rem(y + 1, 4), z, x, c))
    hello((lax.rem(y + 3, 4), z, x, c))
    hello((y, z, x, 1 - c))
    pl.semaphore_wait(barrier, nz * nx - 1 + 3)


def offsets(nz, nx):
    steps = [(dz, dx) for dz in range(nz) for dx in range(nx) if dz or dx]

    def hops(step):
        return min(step[0], nz - step[0]) + min(step[1], nx - step[1])

    return sorted(steps, key=hops)


def bring_kernel(
    nz, nx,
    q_ref, g_ref, k_ref, v_ref, i_ref,
    qh, gh, ka, va, ih,
    s_in, r_in, s_y, r_y, s_c, r_c, own,
):
    y, z, x, c = place()
    chips = nz * nx
    rows = k_ref.shape[0]
    part = chips * rows
    quarter = k_ref.shape[1] // 4
    me = z * nx + x
    up, down, far = lax.rem(y + 1, 4), lax.rem(y + 3, 4), lax.rem(y + 2, 4)
    greet(nz, nx)

    def columns(head):
        return pl.ds(pl.multiple_of(head * HD, HD), HD)

    def token_part(ref, head):
        return ref.at[:, pl.ds(pl.multiple_of(y * quarter, quarter), quarter), columns(head)]

    def landing(ref):
        return ref.at[y, pl.ds(c * part + me * rows, rows)]

    def sides(t, head):
        if t < 2:
            return token_part((k_ref, v_ref)[t], head), landing((ka, va)[t])
        if t < 4:
            return (q_ref, g_ref)[t - 2].at[:, :, columns(head)], (qh, gh)[t - 2].at[me]
        return i_ref, ih.at[me]

    def to_chip(t, d):
        pz, px = lax.rem(z + d // nx, nz), lax.rem(x + lax.rem(d, nx), nx)
        return remote(*sides(t, pz * nx + px), s_in.at[t, d], r_in.at[t, d], (y, pz, px, c))

    def keep(t):
        return pltpu.make_async_copy(*sides(t, me), own.at[t])

    def arrived(t):
        @pl.loop(1, chips)
        def _(d):
            to_chip(t, d).wait_recv()

        keep(t).wait()

    for t in (0, 1, 4, 2, 3):
        for dz, dx in offsets(nz, nx):
            to_chip(t, dz * nx + dx).start()
        keep(t).start()

    def chunk(t, at):
        return (ka, va)[t].at[at, pl.ds(c * part, part)]

    def along_y(t, at, slot, where):
        return remote(
            chunk(t, at), chunk(t, at), s_y.at[t, slot], r_y.at[t, slot], (where, z, x, c)
        )

    def across(t, at, slot):
        return remote(
            chunk(t, at), chunk(t, at), s_c.at[t, slot], r_c.at[t, slot], (y, z, x, 1 - c)
        )

    for t in (0, 1):
        arrived(t)
        along_y(t, y, 0, up).start()
        along_y(t, y, 1, down).start()
        across(t, y, 0).start()

    for t in (0, 1):
        along_y(t, down, 0, up).wait_recv()
        if t == 0:
            along_y(t, down, 2, up).start()
        across(t, down, 1).start()
        along_y(t, up, 1, down).wait_recv()
        if t == 1:
            along_y(t, up, 2, down).start()
        across(t, up, 2).start()
    for t in (0, 1):
        along_y(t, far, 2, up).wait_recv()
        across(t, far, 3).start()

    for t in (2, 3, 4):
        arrived(t)
    for t in range(5):

        @pl.loop(1, chips)
        def _(d):
            to_chip(t, d).wait_send()

    for t in (0, 1):
        for slot in range(3):
            along_y(t, y, slot, up).wait_send()
        for slot in range(4):
            across(t, y, slot).wait()


def bring(nz, nx, query, grad_out, keys, values, entry):
    chips = nz * nx
    rows, tokens, _ = keys.shape
    spans, span_len, _ = query.shape
    bf16 = jnp.bfloat16
    held = jax.ShapeDtypeStruct((4, 2 * chips * rows, tokens // 4, HD), bf16)
    heads = jax.ShapeDtypeStruct((chips, spans, span_len, HD), bf16)
    dma = pltpu.SemaphoreType.DMA
    return pl.pallas_call(
        functools.partial(bring_kernel, nz, nx),
        name="bring",
        out_shape=(heads, heads, held, held, jax.ShapeDtypeStruct((chips,) + entry.shape, jnp.int32)),
        in_specs=[ANY] * 5,
        out_specs=(ANY,) * 5,
        scratch_shapes=[
            dma((5, chips)), dma((5, chips)), dma((2, 3)), dma((2, 3)), dma((2, 4)), dma((2, 4)), dma((5,)),
        ],
        compiler_params=pltpu.CompilerParams(collective_id=0, has_side_effects=True),
    )(query, grad_out, keys, values, entry)


def attend_kernel(
    unroll, i_ref, q_ref, g_ref, k_hbm, v_hbm, dq_ref, dk_hbm, dv_hbm, ka, va, dk, dv, sems
):
    fill = (
        pltpu.make_async_copy(k_hbm, ka, sems.at[0]),
        pltpu.make_async_copy(v_hbm, va, sems.at[1]),
    )
    for copy in fill:
        copy.start()
    quarters, rows, tok, _ = ka.shape
    spans, span_len, _ = q_ref.shape
    tokens = quarters * tok
    per = i_ref.shape[1]
    scaling = HD ** -0.5
    to_base2 = scaling * float(np.log2(np.e))

    @pl.loop(0, rows)
    def _(r):
        dk[:, r] = jnp.zeros((quarters, tok, HD), jnp.float32)
        dv[:, r] = jnp.zeros((quarters, tok, HD), jnp.float32)

    for copy in fill:
        copy.wait()

    def contract(a, b, da, db):
        return lax.dot_general(
            a, b, (((da,), (db,)), ((), ())), preferred_element_type=jnp.float32
        )

    def rows_of(ref, ea, eb):
        return jnp.concatenate(
            [ref[:, ea].reshape(tokens, HD), ref[:, eb].reshape(tokens, HD)], axis=0
        )

    def diagonal(a, b):
        empty = jnp.zeros_like(a)
        return jnp.concatenate(
            [jnp.concatenate([a, empty], axis=1), jnp.concatenate([empty, b], axis=1)], axis=0
        )

    def gradients(sa):
        sb = sa + 1
        entries = [i_ref[s // per, lax.rem(s, per), n] for s in (sa, sb) for n in (0, 1)]
        queries = diagonal(q_ref[sa], q_ref[sb])
        grads = diagonal(g_ref[sa], g_ref[sb])
        keys = jnp.concatenate([rows_of(ka, *entries[:2]), rows_of(ka, *entries[2:])], axis=1)
        values = jnp.concatenate([rows_of(va, *entries[:2]), rows_of(va, *entries[2:])], axis=1)
        scores = contract(keys, queries, 1, 1)
        dprob = contract(values, grads, 1, 1)
        top = jnp.max(scores, axis=0, keepdims=True)
        lifted = jnp.exp2((scores - top) * to_base2)
        inverse = 1.0 / jnp.sum(lifted, axis=0, keepdims=True)
        delta = jnp.sum(lifted * dprob, axis=0, keepdims=True) * inverse
        chance_low = (lifted * inverse).astype(jnp.bfloat16)
        dscore = (lifted * (inverse * scaling) * (dprob - delta)).astype(jnp.bfloat16)
        both = contract(dscore, keys, 0, 0)
        dq_ref[sa] = both[:span_len, :HD].astype(jnp.bfloat16)
        dq_ref[sb] = both[span_len:, HD:].astype(jnp.bfloat16)
        return entries, contract(dscore, queries, 1, 0), contract(chance_low, grads, 1, 0)

    @pl.loop(0, spans // (2 * unroll))
    def _(step):
        results = [gradients(2 * (step * unroll + u)) for u in range(unroll)]
        for entries, key_terms, value_terms in results:
            for at, e in enumerate(entries):
                rs = slice(at % 2 * tokens, (at % 2 + 1) * tokens)
                cs = slice(at // 2 * HD, (at // 2 + 1) * HD)
                dk[:, e] += key_terms[rs, cs].reshape(quarters, tok, HD)
                dv[:, e] += value_terms[rs, cs].reshape(quarters, tok, HD)

    drain = (
        pltpu.make_async_copy(ka, dk_hbm, sems.at[0]),
        pltpu.make_async_copy(va, dv_hbm, sems.at[1]),
    )
    for low, total, copy in ((ka, dk, drain[0]), (va, dv, drain[1])):

        @pl.loop(0, rows)
        def _(r):
            low[:, r] = total[:, r].astype(jnp.bfloat16)

        copy.start()
    for copy in drain:
        copy.wait()


def attend(entry, qh, gh, ka, va):
    spans = qh.shape[0] * qh.shape[1]
    flat = (spans,) + qh.shape[2:]
    bf16 = jnp.bfloat16
    held = jax.ShapeDtypeStruct(ka.shape, bf16)
    return pl.pallas_call(
        functools.partial(attend_kernel, min(4, spans // 2)),
        name="attend",
        out_shape=(jax.ShapeDtypeStruct(flat, bf16), held, held),
        in_specs=[SMEM, VMEM, VMEM, ANY, ANY],
        out_specs=(VMEM, ANY, ANY),
        scratch_shapes=[
            pltpu.VMEM(ka.shape, bf16),
            pltpu.VMEM(ka.shape, bf16),
            pltpu.VMEM(ka.shape, jnp.float32),
            pltpu.VMEM(ka.shape, jnp.float32),
            pltpu.SemaphoreType.DMA((2,)),
        ],
        compiler_params=pltpu.CompilerParams(vmem_limit_bytes=56 * MiB),
        cost_estimate=pl.CostEstimate(
            flops=spans * 10 * 64 * 256 * HD, bytes_accessed=32 * MiB, transcendentals=spans * 64 * 256
        ),
    )(entry, qh.reshape(flat), gh.reshape(flat), ka, va)


def give_kernel(
    nz, nx,
    dq_ref, dk_ref, dv_ref,
    gq, gk, gv,
    mine, other, total, passed, arrived,
    s_q, r_q, s_out, r_out, s_c, r_c, s_f, r_f, s_y, r_y, own_q, own_out, own,
):
    y, z, x, c = place()
    chips = nz * nx
    part = chips * (gk.shape[0])
    rows = part // chips
    band = nx * rows
    me = z * nx + x
    up, down, far = lax.rem(y + 1, 4), lax.rem(y + 3, 4), lax.rem(y + 2, 4)
    pair = (dk_ref, dv_ref)
    outs = (gk, gv)
    greet(nz, nx)

    at = (far, up, down, y)
    bands = sorted(range(nz), key=lambda dz: -min(dz, nz - dz))

    def first_row(dz):
        return lax.rem(z + dz, nz) * band

    def across(t, slot, dz):
        return remote(
            pair[t].at[at[slot], pl.ds((1 - c) * part + first_row(dz), band)],
            other.at[slot, t, dz],
            s_c.at[slot, t, dz], r_c.at[slot, t, dz], (y, z, x, 1 - c),
        )

    def fetch(t, slot, dz):
        return pltpu.make_async_copy(
            pair[t].at[at[slot], pl.ds(c * part + first_row(dz), band)],
            mine.at[slot, t, dz],
            own.at[slot, t, dz],
        )

    for dz in bands:
        for slot in range(4):
            for t in (0, 1):
                across(t, slot, dz).start()
                fetch(t, slot, dz).start()

    def columns(head):
        return pl.ds(pl.multiple_of(head * HD, HD), HD)

    def chip(d):
        pz, px = lax.rem(z + d // nx, nz), lax.rem(x + lax.rem(d, nx), nx)
        return pz * nx + px, (y, pz, px, c)

    def query_out(d):
        head, where = chip(d)
        return remote(dq_ref.at[head], gq.at[:, :, columns(me)], s_q.at[d], r_q.at[d], where)

    def key_out(d, t):
        _, where = chip(d)
        px = lax.rem(x + lax.rem(d, nx), nx)
        return remote(
            total.at[3, t, d // nx, pl.ds(px * rows, rows)], outs[t].at[:, :, columns(me)],
            s_out.at[t, d], r_out.at[t, d], where,
        )

    def key_own(t):
        return pltpu.make_async_copy(
            total.at[3, t, 0, pl.ds(x * rows, rows)], outs[t].at[:, :, columns(me)], own_out.at[t]
        )

    query_own = pltpu.make_async_copy(dq_ref.at[me], gq.at[:, :, columns(me)], own_q)
    query_own.start()
    for dz, dx in offsets(nz, nx):
        query_out(dz * nx + dx).start()

    def f32(a):
        return a.astype(jnp.float32)

    def add(dst, *terms):
        @pl.loop(0, band // rows)
        def _(i):
            rs = pl.ds(i * rows, rows)
            sums = f32(terms[0][rs])
            for term in terms[1:]:
                sums = sums + f32(term[rs])
            dst[rs] = sums.astype(jnp.bfloat16)

    def both_cores(t, slot, dz):
        across(t, slot, dz).wait_recv()
        fetch(t, slot, dz).wait()
        return mine.at[slot, t, dz], other.at[slot, t, dz]

    def far_copy(t, dz):
        return remote(
            total.at[0, t, dz], passed.at[t, dz], s_f.at[t, dz], r_f.at[t, dz],
            ((up, down)[t], z, x, c),
        )

    def near_copy(t, slot, dz):
        return remote(
            total.at[slot, t, dz], arrived.at[slot - 1, t, dz],
            s_y.at[slot - 1, t, dz], r_y.at[slot - 1, t, dz],
            ((up, down)[slot - 1], z, x, c),
        )

    def direct(dz):
        for t in (0, 1):
            add(total.at[0, t, dz], *both_cores(t, 0, dz))
            far_copy(t, dz).start()
        for t, slot in ((1, 1), (0, 2)):
            add(total.at[slot, t, dz], *both_cores(t, slot, dz))
            near_copy(t, slot, dz).start()

    def merged(dz):
        for t, slot in ((0, 1), (1, 2)):
            terms = both_cores(t, slot, dz)
            far_copy(t, dz).wait_recv()
            add(total.at[slot, t, dz], *terms, passed.at[t, dz])
            near_copy(t, slot, dz).start()

    def final(dz):
        for t in (0, 1):
            terms = both_cores(t, 3, dz)
            near_copy(t, 1, dz).wait_recv()
            near_copy(t, 2, dz).wait_recv()
            add(total.at[3, t, dz], *terms, arrived.at[0, t, dz], arrived.at[1, t, dz])
            for dx in range(nx):
                if dz or dx:
                    key_out(dz * nx + dx, t).start()
                else:
                    key_own(t).start()

    for step in range(nz + 2):
        if step < nz:
            direct(bands[step])
        if 1 <= step < nz + 1:
            merged(bands[step - 1])
        if step >= 2:
            final(bands[step - 2])

    @pl.loop(1, chips)
    def _(d):
        query_out(d).wait()
        for t in (0, 1):
            key_out(d, t).wait()

    query_own.wait()
    for t in (0, 1):
        key_own(t).wait()

        @pl.loop(0, nz)
        def _(dz):
            far_copy(t, dz).wait_send()
            for slot in range(4):
                across(t, slot, dz).wait_send()
            for slot in (1, 2):
                near_copy(t, slot, dz).wait_send()


def give(nz, nx, dq, dk, dv):
    chips = nz * nx
    _, all_rows, tok, _ = dk.shape
    part = all_rows // 2
    band = part // nz
    _, spans, span_len, _ = dq.shape
    bf16 = jnp.bfloat16
    dma = pltpu.SemaphoreType.DMA
    row_out = jax.ShapeDtypeStruct((part // chips, tok, chips * HD), bf16)
    return pl.pallas_call(
        functools.partial(give_kernel, nz, nx),
        name="give",
        out_shape=(jax.ShapeDtypeStruct((spans, span_len, chips * HD), bf16), row_out, row_out),
        in_specs=[ANY] * 3,
        out_specs=(ANY,) * 3,
        scratch_shapes=[
            pltpu.VMEM((4, 2, nz, band, tok, HD), bf16),
            pltpu.VMEM((4, 2, nz, band, tok, HD), bf16),
            pltpu.VMEM((4, 2, nz, band, tok, HD), bf16),
            pltpu.VMEM((2, nz, band, tok, HD), bf16),
            pltpu.VMEM((2, 2, nz, band, tok, HD), bf16),
            dma((chips,)), dma((chips,)), dma((2, chips)), dma((2, chips)),
            dma((4, 2, nz)), dma((4, 2, nz)), dma((2, nz)), dma((2, nz)),
            dma((2, 2, nz)), dma((2, 2, nz)), dma, dma((2,)), dma((4, 2, nz)),
        ],
        compiler_params=pltpu.CompilerParams(
            collective_id=1, has_side_effects=True, vmem_limit_bytes=48 * MiB
        ),
    )(dq, dk, dv)


def on_device(nz, nx, query, grad_out, keys, values, owner_list, row_list):
    chips = nz * nx
    rows = keys.shape[0]
    entry = lax.rem(owner_list, 2) * (chips * rows) + (owner_list // 2) * rows + row_list
    entry = jnp.pad(entry, ((0, 0), (0, HD - entry.shape[1])))
    qh, gh, ka, va, ih = bring(nz, nx, query, grad_out, keys, values, entry)
    dq, dk, dv = attend(ih, qh, gh, ka, va)
    return give(nz, nx, dq.reshape(qh.shape), dk, dv)


def solution(mesh):
    groups, retr = mesh.devices.shape
    nx = 4 if retr == 32 else 2
    nz = retr // (2 * nx)
    fine = Mesh(mesh.devices.reshape(groups, nz, nx, 2), ("y", "z", "x", "c"))
    all_axes = ("y", "z", "x", "c")
    owner = ("z", "x", "c")
    return jax.shard_map(
        functools.partial(on_device, nz, nx),
        mesh=fine,
        in_specs=(
            P(all_axes, None, None),
            P(all_axes, None, None),
            P(owner, None, None),
            P(owner, None, None),
            P(all_axes, None),
            P(all_axes, None),
        ),
        out_specs=(P(all_axes, None, None), P(owner, "y", None), P(owner, "y", None)),
        check_vma=False,
    )
```

```python
import functools

import jax
import jax.numpy as jnp
import numpy as np
from jax import lax
from jax.experimental import pallas as pl
from jax.experimental.pallas import tpu as pltpu
from jax.sharding import Mesh
from jax.sharding import PartitionSpec as P

HD = 128
MiB = 1024 * 1024
ANY = pl.BlockSpec(memory_space=pl.ANY)
VMEM = pl.BlockSpec(memory_space=pltpu.VMEM)
SMEM = pl.BlockSpec(memory_space=pltpu.SMEM)
HBM = pl.BlockSpec(memory_space=pltpu.HBM)


def in_hbm(*arrays):
    return tuple(pltpu.with_memory_space_constraint(a, pltpu.HBM) for a in arrays)


def in_vmem(*arrays):
    return tuple(pltpu.with_memory_space_constraint(a, pltpu.VMEM) for a in arrays)


def place():
    return tuple(lax.axis_index(name) for name in ("y", "z", "x", "c"))


def remote(src, dst, send, recv, where):
    return pltpu.make_async_remote_copy(
        src_ref=src,
        dst_ref=dst,
        send_sem=send,
        recv_sem=recv,
        device_id=where,
        device_id_type=pl.DeviceIdType.MESH,
    )


def greet(nz, nx):
    y, z, x, c = place()
    barrier = pltpu.get_barrier_semaphore()

    def hello(where):
        pl.semaphore_signal(barrier, inc=1, device_id=where, device_id_type=pl.DeviceIdType.MESH)

    @pl.loop(1, nz * nx)
    def _(d):
        hello((y, lax.rem(z + d // nx, nz), lax.rem(x + lax.rem(d, nx), nx), c))

    hello((lax.rem(y + 1, 4), z, x, c))
    hello((lax.rem(y + 3, 4), z, x, c))
    hello((y, z, x, 1 - c))
    pl.semaphore_wait(barrier, nz * nx - 1 + 3)


def contract(a, b, da, db):
    return lax.dot_general(a, b, (((da,), (db,)), ((), ())), preferred_element_type=jnp.float32)


def diagonal(a, b):
    empty = jnp.zeros_like(a)
    return jnp.concatenate(
        [jnp.concatenate([a, empty], axis=1), jnp.concatenate([empty, b], axis=1)], axis=0
    )


def entries_of(i_ref, pair):
    per = i_ref.shape[1]
    return [
        i_ref[s // per, lax.rem(s, per), n] for s in (2 * pair, 2 * pair + 1) for n in (0, 1)
    ]


def rows_of(ref, entries):
    quarters, _, tok, _ = ref.shape
    taken = [ref[:, e].reshape(quarters * tok, HD) for e in entries]
    return jnp.concatenate(
        [jnp.concatenate(taken[:2], axis=0), jnp.concatenate(taken[2:], axis=0)], axis=1
    )


def tokens_of(ref, pair):
    per = ref.shape[1]
    sa, sb = 2 * pair, 2 * pair + 1
    return diagonal(ref[sa // per, lax.rem(sa, per)], ref[sb // per, lax.rem(sb, per)])


def offsets(nz, nx):
    steps = [(dz, dx) for dz in range(nz) for dx in range(nx) if dz or dx]

    def hops(step):
        return min(step[0], nz - step[0]) + min(step[1], nx - step[1])

    return sorted(steps, key=hops)


def bring_kernel(
    nz, nx,
    q_ref, g_ref, k_ref, v_ref, i_ref,
    qh, gh, va, ih, lifted_ref, inverse_ref, ka_hbm,
    ka, i_smem, s_in, r_in, s_y, r_y, s_c, r_c, own,
):
    y, z, x, c = place()
    chips = nz * nx
    rows = k_ref.shape[0]
    part = chips * rows
    quarter = k_ref.shape[1] // 4
    me = z * nx + x
    up, down, far = lax.rem(y + 1, 4), lax.rem(y + 3, 4), lax.rem(y + 2, 4)
    greet(nz, nx)

    def columns(head):
        return pl.ds(pl.multiple_of(head * HD, HD), HD)

    def token_part(ref, head):
        return ref.at[:, pl.ds(pl.multiple_of(y * quarter, quarter), quarter), columns(head)]

    def landing(ref):
        return ref.at[y, pl.ds(c * part + me * rows, rows)]

    def sides(t, head):
        if t < 2:
            return token_part((k_ref, v_ref)[t], head), landing((ka, va)[t])
        if t < 4:
            return (q_ref, g_ref)[t - 2].at[:, :, columns(head)], (qh, gh)[t - 2].at[me]
        return i_ref, ih.at[me]

    def to_chip(t, d):
        pz, px = lax.rem(z + d // nx, nz), lax.rem(x + lax.rem(d, nx), nx)
        return remote(*sides(t, pz * nx + px), s_in.at[t, d], r_in.at[t, d], (y, pz, px, c))

    def keep(t):
        return pltpu.make_async_copy(*sides(t, me), own.at[t])

    def arrived(t):
        @pl.loop(1, chips)
        def _(d):
            to_chip(t, d).wait_recv()

        keep(t).wait()

    def send(t):
        for dz, dx in offsets(nz, nx):
            to_chip(t, dz * nx + dx).start()
        keep(t).start()

    for t in (0, 1, 4, 2):
        send(t)

    def chunk(t, at):
        return (ka, va)[t].at[at, pl.ds(c * part, part)]

    def along_y(t, at, slot, where):
        return remote(
            chunk(t, at), chunk(t, at), s_y.at[t, slot], r_y.at[t, slot], (where, z, x, c)
        )

    def across(t, at, slot):
        return remote(
            chunk(t, at), chunk(t, at), s_c.at[t, slot], r_c.at[t, slot], (y, z, x, 1 - c)
        )

    arrived(0)
    along_y(0, y, 0, up).start()
    along_y(0, y, 1, down).start()
    across(0, y, 0).start()
    arrived(1)
    along_y(1, y, 1, down).start()
    across(1, y, 0).start()
    send(3)

    def all_across(t):
        along_y(t, far, 2, up).wait_recv()
        across(t, far, 3).start()
        for slot in range(4):
            across(t, y, slot).wait_recv()

    arrived(4)
    entry_copy = pltpu.make_async_copy(ih, i_smem, own.at[5])
    entry_copy.start()
    entry_copy.wait()
    along_y(0, down, 0, up).wait_recv()
    along_y(0, down, 2, up).start()
    along_y(1, y, 0, up).start()
    across(0, down, 1).start()
    along_y(0, up, 1, down).wait_recv()
    across(0, up, 2).start()
    along_y(1, up, 1, down).wait_recv()
    along_y(1, up, 2, down).start()
    across(1, up, 2).start()
    all_across(0)
    keep_keys = pltpu.make_async_copy(ka, ka_hbm, own.at[6])
    keep_keys.start()
    arrived(2)

    to_base2 = HD ** -0.5 * float(np.log2(np.e))
    pairs = lifted_ref.shape[0]
    unroll = min(4, pairs)

    def weigh(first, last):
        @pl.loop(first, last)
        def _(step):
            for u in range(unroll):
                p = step * unroll + u
                scores = contract(rows_of(ka, entries_of(i_smem, p)), tokens_of(qh, p), 1, 1)
                lifted = jnp.exp2((scores - jnp.max(scores, axis=0, keepdims=True)) * to_base2)
                inverse_ref[p] = 1.0 / jnp.sum(lifted, axis=0, keepdims=True)
                lifted_ref[p] = lifted.astype(jnp.bfloat16)

    steps = pairs // unroll
    weigh(0, steps // 2)
    along_y(1, down, 0, up).wait_recv()
    across(1, down, 1).start()
    weigh(steps // 2, steps)
    all_across(1)
    arrived(3)
    keep_keys.wait()
    for t in range(5):

        @pl.loop(1, chips)
        def _(d):
            to_chip(t, d).wait_send()

    for t in (0, 1):
        for slot in range(3):
            along_y(t, y, slot, up).wait_send()
        for slot in range(4):
            across(t, y, slot).wait_send()


def bring(nz, nx, query, grad_out, keys, values, entry):
    chips = nz * nx
    rows, tokens, _ = keys.shape
    spans, span_len, _ = query.shape
    bf16 = jnp.bfloat16
    held = pltpu.VMEM((4, 2 * chips * rows, tokens // 4, HD), bf16)
    heads = pltpu.VMEM((chips, spans, span_len, HD), bf16)
    pairs = chips * spans // 2
    dma = pltpu.SemaphoreType.DMA
    return pl.pallas_call(
        functools.partial(bring_kernel, nz, nx),
        name="bring",
        out_shape=(
            heads, heads, held,
            jax.ShapeDtypeStruct((chips,) + entry.shape, jnp.int32),
            pltpu.VMEM((pairs, 2 * tokens, 2 * span_len), bf16),
            pltpu.VMEM((pairs, 1, 2 * span_len), jnp.float32),
            pltpu.HBM(held.shape, bf16),
        ),
        in_specs=[HBM] * 4 + [ANY],
        out_specs=(VMEM,) * 3 + (ANY,) + (VMEM,) * 2 + (HBM,),
        scratch_shapes=[
            pltpu.VMEM(held.shape, bf16),
            pltpu.SMEM((chips,) + entry.shape, jnp.int32),
            dma((5, chips)), dma((5, chips)), dma((2, 3)), dma((2, 3)), dma((2, 4)), dma((2, 4)), dma((7,)),
        ],
        compiler_params=pltpu.CompilerParams(
            collective_id=0, has_side_effects=True, vmem_limit_bytes=14 * MiB
        ),
    )(*in_hbm(query, grad_out, keys, values), entry)


def attend_kernel(
    i_ref, qh, gh, va, lifted_ref, inverse_ref, dscore_ref, dk_low, dv_low, dk, dv
):
    quarters, rows, tok, _ = va.shape
    tokens = quarters * tok
    scaling = HD ** -0.5
    pairs = lifted_ref.shape[0]
    unroll = min(4, pairs)

    def gradients(p):
        entries = entries_of(i_ref, p)
        grads = tokens_of(gh, p)
        dprob = contract(rows_of(va, entries), grads, 1, 1)
        inverse = inverse_ref[p]
        lifted = lifted_ref[p].astype(jnp.float32)
        delta = jnp.sum(lifted * dprob, axis=0, keepdims=True) * inverse
        chance_low = (lifted * inverse).astype(jnp.bfloat16)
        dscore = (lifted * (inverse * scaling) * (dprob - delta)).astype(jnp.bfloat16)
        dscore_ref[p] = dscore
        return entries, contract(dscore, tokens_of(qh, p), 1, 0), contract(chance_low, grads, 1, 0)

    @pl.loop(0, rows)
    def _(r):
        dk[:, r] = jnp.zeros((quarters, tok, HD), jnp.float32)
        dv[:, r] = jnp.zeros((quarters, tok, HD), jnp.float32)

    @pl.loop(0, pairs // unroll)
    def _(step):
        results = [gradients(step * unroll + u) for u in range(unroll)]
        for entries, key_terms, value_terms in results:
            for at, e in enumerate(entries):
                rs = slice(at % 2 * tokens, (at % 2 + 1) * tokens)
                cs = slice(at // 2 * HD, (at // 2 + 1) * HD)
                dk[:, e] += key_terms[rs, cs].reshape(quarters, tok, HD)
                dv[:, e] += value_terms[rs, cs].reshape(quarters, tok, HD)

    @pl.loop(0, rows)
    def _(r):
        dk_low[:, r] = dk[:, r].astype(jnp.bfloat16)
        dv_low[:, r] = dv[:, r].astype(jnp.bfloat16)


def attend(ih, qh, gh, va, lifted, inverse):
    held = pltpu.VMEM(va.shape, jnp.bfloat16)
    work = lifted.size * HD * 2
    return pl.pallas_call(
        attend_kernel,
        name="attend",
        out_shape=(pltpu.VMEM(lifted.shape, jnp.bfloat16), held, held),
        in_specs=[SMEM] + [VMEM] * 5,
        out_specs=(VMEM,) * 3,
        scratch_shapes=[pltpu.VMEM(va.shape, jnp.float32)] * 2,
        input_output_aliases={4: 0, 3: 2},
        compiler_params=pltpu.CompilerParams(vmem_limit_bytes=28 * MiB),
        cost_estimate=pl.CostEstimate(flops=3 * work, bytes_accessed=4 * MiB, transcendentals=0),
    )(ih, *in_vmem(qh, gh, va, lifted, inverse))


def give_kernel(
    nz, nx,
    i_ref, ka_hbm, dscore_ref, dk_ref, dv_ref,
    gq, gk, gv,
    ka, dq_ref, other, total, passed, arrived,
    s_q, r_q, s_out, r_out, s_c, r_c, s_f, r_f, s_y, r_y, own_q, own_out, own_k,
):
    y, z, x, c = place()
    chips = nz * nx
    part = chips * (gk.shape[0])
    rows = part // chips
    band = nx * rows
    me = z * nx + x
    up, down, far = lax.rem(y + 1, 4), lax.rem(y + 3, 4), lax.rem(y + 2, 4)
    pair = (dk_ref, dv_ref)
    outs = (gk, gv)
    greet(nz, nx)

    at = (far, up, down, y)
    bands = sorted(range(nz), key=lambda dz: -min(dz, nz - dz))

    def first_row(dz):
        return lax.rem(z + dz, nz) * band

    def across(t, slot, dz):
        return remote(
            pair[t].at[at[slot], pl.ds((1 - c) * part + first_row(dz), band)],
            other.at[slot, t, dz],
            s_c.at[slot, t, dz], r_c.at[slot, t, dz], (y, z, x, 1 - c),
        )

    def mine(t, slot, dz):
        return pair[t].at[at[slot], pl.ds(c * part + first_row(dz), band)]

    for dz in bands:
        for slot in range(4):
            for t in (0, 1):
                across(t, slot, dz).start()

    def columns(head):
        return pl.ds(pl.multiple_of(head * HD, HD), HD)

    def chip(d):
        pz, px = lax.rem(z + d // nx, nz), lax.rem(x + lax.rem(d, nx), nx)
        return pz * nx + px, (y, pz, px, c)

    def query_out(d):
        head, where = chip(d)
        return remote(dq_ref.at[head], gq.at[:, :, columns(me)], s_q.at[d], r_q.at[d], where)

    def key_out(d, t):
        _, where = chip(d)
        px = lax.rem(x + lax.rem(d, nx), nx)
        return remote(
            total.at[3, t, d // nx, pl.ds(px * rows, rows)], outs[t].at[:, :, columns(me)],
            s_out.at[t, d], r_out.at[t, d], where,
        )

    def key_own(t):
        return pltpu.make_async_copy(
            total.at[3, t, 0, pl.ds(x * rows, rows)], outs[t].at[:, :, columns(me)], own_out.at[t]
        )

    query_own = pltpu.make_async_copy(dq_ref.at[me], gq.at[:, :, columns(me)], own_q)
    keys_in = pltpu.make_async_copy(ka_hbm, ka, own_k)
    keys_in.start()
    pairs = dscore_ref.shape[0]
    per = dq_ref.shape[1]
    span_len = dq_ref.shape[2]
    unroll = min(4, pairs)

    def queries():
        keys_in.wait()

        @pl.loop(0, pairs // unroll)
        def _(step):
            for u in range(unroll):
                p = step * unroll + u
                both = contract(dscore_ref[p], rows_of(ka, entries_of(i_ref, p)), 0, 0)
                sa, sb = 2 * p, 2 * p + 1
                dq_ref[sa // per, lax.rem(sa, per)] = both[:span_len, :HD].astype(jnp.bfloat16)
                dq_ref[sb // per, lax.rem(sb, per)] = both[span_len:, HD:].astype(jnp.bfloat16)

        query_own.start()
        for dz, dx in offsets(nz, nx):
            query_out(dz * nx + dx).start()

    def f32(a):
        return a.astype(jnp.float32)

    def add(dst, *terms):
        @pl.loop(0, band // rows)
        def _(i):
            rs = pl.ds(i * rows, rows)
            sums = f32(terms[0][rs])
            for term in terms[1:]:
                sums = sums + f32(term[rs])
            dst[rs] = sums.astype(jnp.bfloat16)

    def both_cores(t, slot, dz):
        across(t, slot, dz).wait_recv()
        return mine(t, slot, dz), other.at[slot, t, dz]

    def far_copy(t, dz):
        return remote(
            total.at[0, t, dz], passed.at[t, dz], s_f.at[t, dz], r_f.at[t, dz],
            ((up, down)[t], z, x, c),
        )

    def near_copy(t, slot, dz):
        return remote(
            total.at[slot, t, dz], arrived.at[slot - 1, t, dz],
            s_y.at[slot - 1, t, dz], r_y.at[slot - 1, t, dz],
            ((up, down)[slot - 1], z, x, c),
        )

    def direct(dz):
        for t in (0, 1):
            add(total.at[0, t, dz], *both_cores(t, 0, dz))
            far_copy(t, dz).start()
        for t, slot in ((1, 1), (0, 2)):
            add(total.at[slot, t, dz], *both_cores(t, slot, dz))
            near_copy(t, slot, dz).start()

    def merged(dz):
        for t, slot in ((0, 1), (1, 2)):
            terms = both_cores(t, slot, dz)
            far_copy(t, dz).wait_recv()
            add(total.at[slot, t, dz], *terms, passed.at[t, dz])
            near_copy(t, slot, dz).start()

    def final(dz):
        for t in (0, 1):
            terms = both_cores(t, 3, dz)
            near_copy(t, 1, dz).wait_recv()
            near_copy(t, 2, dz).wait_recv()
            add(total.at[3, t, dz], *terms, arrived.at[0, t, dz], arrived.at[1, t, dz])
            for dx in range(nx):
                if dz or dx:
                    key_out(dz * nx + dx, t).start()
                else:
                    key_own(t).start()

    for step in range(nz + 2):
        if step < nz:
            direct(bands[step])
        if step == min(1, nz - 1):
            queries()
        if 1 <= step < nz + 1:
            merged(bands[step - 1])
        if step >= 2:
            final(bands[step - 2])

    @pl.loop(1, chips)
    def _(d):
        query_out(d).wait()
        for t in (0, 1):
            key_out(d, t).wait()

    query_own.wait()
    for t in (0, 1):
        key_own(t).wait()

        @pl.loop(0, nz)
        def _(dz):
            far_copy(t, dz).wait_send()
            for slot in range(4):
                across(t, slot, dz).wait_send()
            for slot in (1, 2):
                near_copy(t, slot, dz).wait_send()


def give(nz, nx, spans, ih, ka, dscore, dk, dv):
    chips = nz * nx
    _, all_rows, tok, _ = dk.shape
    part = all_rows // 2
    band = part // nz
    span_len = dscore.shape[2] // 2
    bf16 = jnp.bfloat16
    dma = pltpu.SemaphoreType.DMA
    row_out = pltpu.VMEM((part // chips, tok, chips * HD), bf16)
    return pl.pallas_call(
        functools.partial(give_kernel, nz, nx),
        name="give",
        out_shape=(pltpu.VMEM((spans, span_len, chips * HD), bf16), row_out, row_out),
        in_specs=[SMEM, HBM] + [VMEM] * 3,
        out_specs=(ANY,) * 3,
        scratch_shapes=[
            pltpu.VMEM(ka.shape, bf16),
            pltpu.VMEM((chips, spans, span_len, HD), bf16),
            pltpu.VMEM((4, 2, nz, band, tok, HD), bf16),
            pltpu.VMEM((4, 2, nz, band, tok, HD), bf16),
            pltpu.VMEM((2, nz, band, tok, HD), bf16),
            pltpu.VMEM((2, 2, nz, band, tok, HD), bf16),
            dma((chips,)), dma((chips,)), dma((2, chips)), dma((2, chips)),
            dma((4, 2, nz)), dma((4, 2, nz)), dma((2, nz)), dma((2, nz)),
            dma((2, 2, nz)), dma((2, 2, nz)), dma, dma((2,)), dma,
        ],
        compiler_params=pltpu.CompilerParams(
            collective_id=1, has_side_effects=True, vmem_limit_bytes=32 * MiB
        ),
    )(ih, *in_hbm(ka), *in_vmem(dscore, dk, dv))


def on_device(nz, nx, query, grad_out, keys, values, owner_list, row_list):
    chips = nz * nx
    rows = keys.shape[0]
    entry = lax.rem(owner_list, 2) * (chips * rows) + (owner_list // 2) * rows + row_list
    entry = jnp.pad(entry, ((0, 0), (0, HD - entry.shape[1])))
    qh, gh, va, ih, lifted, inverse, ka = bring(
        nz, nx, query, grad_out, keys, values, entry
    )
    dscore, dk, dv = attend(ih, qh, gh, va, lifted, inverse)
    return give(nz, nx, query.shape[0], ih, ka, dscore, dk, dv)


def solution(mesh):
    groups, retr = mesh.devices.shape
    nx = 4 if retr == 32 else 2
    nz = retr // (2 * nx)
    fine = Mesh(mesh.devices.reshape(groups, nz, nx, 2), ("y", "z", "x", "c"))
    all_axes = ("y", "z", "x", "c")
    owner = ("z", "x", "c")
    return jax.shard_map(
        functools.partial(on_device, nz, nx),
        mesh=fine,
        in_specs=(
            P(all_axes, None, None),
            P(all_axes, None, None),
            P(owner, None, None),
            P(owner, None, None),
            P(all_axes, None),
            P(all_axes, None),
        ),
        out_specs=(P(all_axes, None, None), P(owner, "y", None), P(owner, "y", None)),
        check_vma=False,
    )
```

```python
import functools

import jax
import jax.numpy as jnp
import numpy as np
from jax import lax
from jax.experimental import pallas as pl
from jax.experimental.pallas import tpu as pltpu
from jax.sharding import Mesh
from jax.sharding import PartitionSpec as P

HD = 128
MiB = 1024 * 1024
ANY = pl.BlockSpec(memory_space=pl.ANY)
VMEM = pl.BlockSpec(memory_space=pltpu.VMEM)
SMEM = pl.BlockSpec(memory_space=pltpu.SMEM)
HBM = pl.BlockSpec(memory_space=pltpu.HBM)


def in_hbm(*arrays):
    return tuple(pltpu.with_memory_space_constraint(a, pltpu.HBM) for a in arrays)


def in_vmem(*arrays):
    return tuple(pltpu.with_memory_space_constraint(a, pltpu.VMEM) for a in arrays)


def place():
    return tuple(lax.axis_index(name) for name in ("y", "z", "x", "c"))


def remote(src, dst, send, recv, where):
    return pltpu.make_async_remote_copy(
        src_ref=src,
        dst_ref=dst,
        send_sem=send,
        recv_sem=recv,
        device_id=where,
        device_id_type=pl.DeviceIdType.MESH,
    )


def greet(nz, nx):
    y, z, x, c = place()
    barrier = pltpu.get_barrier_semaphore()

    def hello(where):
        pl.semaphore_signal(barrier, inc=1, device_id=where, device_id_type=pl.DeviceIdType.MESH)

    @pl.loop(1, nz * nx)
    def _(d):
        hello((y, lax.rem(z + d // nx, nz), lax.rem(x + lax.rem(d, nx), nx), c))

    hello((lax.rem(y + 1, 4), z, x, c))
    hello((lax.rem(y + 3, 4), z, x, c))
    hello((y, z, x, 1 - c))
    pl.semaphore_wait(barrier, nz * nx - 1 + 3)


def contract(a, b, da, db):
    return lax.dot_general(a, b, (((da,), (db,)), ((), ())), preferred_element_type=jnp.float32)


def diagonal(a, b):
    empty = jnp.zeros_like(a)
    return jnp.concatenate(
        [jnp.concatenate([a, empty], axis=1), jnp.concatenate([empty, b], axis=1)], axis=0
    )


def entries_of(i_ref, pair):
    per = i_ref.shape[1]
    return [
        i_ref[s // per, lax.rem(s, per), n] for s in (2 * pair, 2 * pair + 1) for n in (0, 1)
    ]


def rows_of(ref, entries):
    quarters, _, tok, _ = ref.shape
    taken = [ref[:, e].reshape(quarters * tok, HD) for e in entries]
    return jnp.concatenate(
        [jnp.concatenate(taken[:2], axis=0), jnp.concatenate(taken[2:], axis=0)], axis=1
    )


def tokens_of(ref, pair):
    per = ref.shape[1]
    sa, sb = 2 * pair, 2 * pair + 1
    return diagonal(ref[sa // per, lax.rem(sa, per)], ref[sb // per, lax.rem(sb, per)])


def offsets(nz, nx):
    steps = [(dz, dx) for dz in range(nz) for dx in range(nx) if dz or dx]

    def hops(step):
        return min(step[0], nz - step[0]) + min(step[1], nx - step[1])

    return sorted(steps, key=hops)


def bring_kernel(
    nz, nx,
    q_ref, g_ref, k_ref, v_ref, i_ref,
    qh, gh, va, ih, lifted_ref, inverse_ref, ka_hbm,
    ka, i_smem, s_in, r_in, s_y, r_y, s_c, r_c, own,
):
    y, z, x, c = place()
    chips = nz * nx
    rows = k_ref.shape[0]
    part = chips * rows
    quarter = k_ref.shape[1] // 4
    me = z * nx + x
    up, down, far = lax.rem(y + 1, 4), lax.rem(y + 3, 4), lax.rem(y + 2, 4)
    greet(nz, nx)

    def columns(head):
        return pl.ds(pl.multiple_of(head * HD, HD), HD)

    def token_part(ref, head):
        return ref.at[:, pl.ds(pl.multiple_of(y * quarter, quarter), quarter), columns(head)]

    def landing(ref):
        return ref.at[y, pl.ds(c * part + me * rows, rows)]

    def sides(t, head):
        if t < 2:
            return token_part((k_ref, v_ref)[t], head), landing((ka, va)[t])
        if t < 4:
            return (q_ref, g_ref)[t - 2].at[:, :, columns(head)], (qh, gh)[t - 2].at[me]
        return i_ref, ih.at[me]

    def to_chip(t, d):
        pz, px = lax.rem(z + d // nx, nz), lax.rem(x + lax.rem(d, nx), nx)
        return remote(*sides(t, pz * nx + px), s_in.at[t, d], r_in.at[t, d], (y, pz, px, c))

    def keep(t):
        return pltpu.make_async_copy(*sides(t, me), own.at[t])

    def arrived(t):
        @pl.loop(1, chips)
        def _(d):
            to_chip(t, d).wait_recv()

        keep(t).wait()

    def send(t):
        for dz, dx in offsets(nz, nx):
            to_chip(t, dz * nx + dx).start()
        keep(t).start()

    for t in (0, 1, 4, 2):
        send(t)

    def chunk(t, at):
        return (ka, va)[t].at[at, pl.ds(c * part, part)]

    def along_y(t, at, slot, where):
        return remote(
            chunk(t, at), chunk(t, at), s_y.at[t, slot], r_y.at[t, slot], (where, z, x, c)
        )

    def across(t, at, slot):
        return remote(
            chunk(t, at), chunk(t, at), s_c.at[t, slot], r_c.at[t, slot], (y, z, x, 1 - c)
        )

    arrived(0)
    along_y(0, y, 0, up).start()
    along_y(0, y, 1, down).start()
    across(0, y, 0).start()
    arrived(1)
    along_y(1, y, 1, down).start()
    across(1, y, 0).start()
    send(3)

    def all_across(t):
        along_y(t, far, 2, up).wait_recv()
        across(t, far, 3).start()
        for slot in range(4):
            across(t, y, slot).wait_recv()

    arrived(4)
    entry_copy = pltpu.make_async_copy(ih, i_smem, own.at[5])
    entry_copy.start()
    entry_copy.wait()
    along_y(0, down, 0, up).wait_recv()
    along_y(0, down, 2, up).start()
    along_y(1, y, 0, up).start()
    across(0, down, 1).start()
    along_y(0, up, 1, down).wait_recv()
    across(0, up, 2).start()
    along_y(1, up, 1, down).wait_recv()
    along_y(1, up, 2, down).start()
    across(1, up, 2).start()
    all_across(0)
    keep_keys = pltpu.make_async_copy(ka, ka_hbm, own.at[6])
    keep_keys.start()
    arrived(2)

    to_base2 = HD ** -0.5 * float(np.log2(np.e))
    pairs = lifted_ref.shape[0]
    unroll = min(4, pairs)

    def weigh(first, last):
        @pl.loop(first, last)
        def _(step):
            for u in range(unroll):
                p = step * unroll + u
                scores = contract(rows_of(ka, entries_of(i_smem, p)), tokens_of(qh, p), 1, 1)
                lifted = jnp.exp2((scores - jnp.max(scores, axis=0, keepdims=True)) * to_base2)
                inverse_ref[p] = 1.0 / jnp.sum(lifted, axis=0, keepdims=True)
                lifted_ref[p] = lifted.astype(jnp.bfloat16)

    steps = pairs // unroll
    weigh(0, steps // 2)
    along_y(1, down, 0, up).wait_recv()
    across(1, down, 1).start()
    weigh(steps // 2, steps)
    all_across(1)
    arrived(3)
    keep_keys.wait()
    for t in range(5):

        @pl.loop(1, chips)
        def _(d):
            to_chip(t, d).wait_send()

    for t in (0, 1):
        for slot in range(3):
            along_y(t, y, slot, up).wait_send()
        for slot in range(4):
            across(t, y, slot).wait_send()


def bring(nz, nx, query, grad_out, keys, values, entry):
    chips = nz * nx
    rows, tokens, _ = keys.shape
    spans, span_len, _ = query.shape
    bf16 = jnp.bfloat16
    held = pltpu.VMEM((4, 2 * chips * rows, tokens // 4, HD), bf16)
    heads = pltpu.VMEM((chips, spans, span_len, HD), bf16)
    pairs = chips * spans // 2
    dma = pltpu.SemaphoreType.DMA
    return pl.pallas_call(
        functools.partial(bring_kernel, nz, nx),
        name="bring",
        out_shape=(
            heads, heads, held,
            jax.ShapeDtypeStruct((chips,) + entry.shape, jnp.int32),
            pltpu.VMEM((pairs, 2 * tokens, 2 * span_len), bf16),
            pltpu.VMEM((pairs, 1, 2 * span_len), jnp.float32),
            pltpu.HBM(held.shape, bf16),
        ),
        in_specs=[HBM] * 4 + [ANY],
        out_specs=(VMEM,) * 3 + (ANY,) + (VMEM,) * 2 + (HBM,),
        scratch_shapes=[
            pltpu.VMEM(held.shape, bf16),
            pltpu.SMEM((chips,) + entry.shape, jnp.int32),
            dma((5, chips)), dma((5, chips)), dma((2, 3)), dma((2, 3)), dma((2, 4)), dma((2, 4)), dma((7,)),
        ],
        compiler_params=pltpu.CompilerParams(
            collective_id=0, has_side_effects=True, vmem_limit_bytes=14 * MiB
        ),
    )(*in_hbm(query, grad_out, keys, values), entry)


def attend_kernel(
    i_ref, qh, gh, va, lifted_ref, inverse_ref, dscore_ref, dk_low, dv_low, dk, dv
):
    quarters, rows, tok, _ = va.shape
    tokens = quarters * tok
    scaling = HD ** -0.5
    pairs = lifted_ref.shape[0]
    unroll = min(8, pairs)

    def add(sums, entries, terms):
        for at, e in enumerate(entries):
            rs = slice(at % 2 * tokens, (at % 2 + 1) * tokens)
            cs = slice(at // 2 * HD, (at // 2 + 1) * HD)
            sums[:, e] += terms[rs, cs].reshape(quarters, tok, HD)

    def gradients(p):
        entries = entries_of(i_ref, p)
        grads = tokens_of(gh, p)
        dprob = contract(rows_of(va, entries), grads, 1, 1)
        inverse = inverse_ref[p]
        lifted = lifted_ref[p].astype(jnp.float32)
        delta = jnp.sum(lifted * dprob, axis=0, keepdims=True) * inverse
        chance_low = (lifted * inverse).astype(jnp.bfloat16)
        dscore = (lifted * (inverse * scaling) * (dprob - delta)).astype(jnp.bfloat16)
        dscore_ref[p] = dscore
        return entries, contract(chance_low, grads, 1, 0)

    @pl.loop(0, rows)
    def _(r):
        dk[:, r] = jnp.zeros((quarters, tok, HD), jnp.float32)
        dv[:, r] = jnp.zeros((quarters, tok, HD), jnp.float32)

    @pl.loop(0, pairs // unroll)
    def _(step):
        results = [gradients(step * unroll + u) for u in range(unroll)]
        for entries, value_terms in results:
            add(dv, entries, value_terms)

    @pl.loop(0, pairs // unroll)
    def _(step):
        results = []
        for u in range(unroll):
            p = step * unroll + u
            results.append(
                (entries_of(i_ref, p), contract(dscore_ref[p], tokens_of(qh, p), 1, 0))
            )
        for entries, key_terms in results:
            add(dk, entries, key_terms)

    @pl.loop(0, rows)
    def _(r):
        dk_low[:, r] = dk[:, r].astype(jnp.bfloat16)
        dv_low[:, r] = dv[:, r].astype(jnp.bfloat16)


def attend(ih, qh, gh, va, lifted, inverse):
    held = pltpu.VMEM(va.shape, jnp.bfloat16)
    work = lifted.size * HD * 2
    return pl.pallas_call(
        attend_kernel,
        name="attend",
        out_shape=(pltpu.VMEM(lifted.shape, jnp.bfloat16), held, held),
        in_specs=[SMEM] + [VMEM] * 5,
        out_specs=(VMEM,) * 3,
        scratch_shapes=[pltpu.VMEM(va.shape, jnp.float32)] * 2,
        input_output_aliases={4: 0, 3: 2},
        compiler_params=pltpu.CompilerParams(vmem_limit_bytes=28 * MiB),
        cost_estimate=pl.CostEstimate(flops=3 * work, bytes_accessed=4 * MiB, transcendentals=0),
    )(ih, *in_vmem(qh, gh, va, lifted, inverse))


def give_kernel(
    nz, nx,
    i_ref, ka_hbm, dscore_ref, dk_ref, dv_ref,
    gq, gk, gv,
    ka, dq_ref, other, total, passed, arrived,
    s_q, r_q, s_out, r_out, s_c, r_c, s_f, r_f, s_y, r_y, own_q, own_out, own_k,
):
    y, z, x, c = place()
    chips = nz * nx
    part = chips * (gk.shape[0])
    rows = part // chips
    band = nx * rows
    me = z * nx + x
    up, down, far = lax.rem(y + 1, 4), lax.rem(y + 3, 4), lax.rem(y + 2, 4)
    pair = (dk_ref, dv_ref)
    outs = (gk, gv)
    greet(nz, nx)

    at = (far, up, down, y)
    bands = sorted(range(nz), key=lambda dz: -min(dz, nz - dz))

    def first_row(dz):
        return lax.rem(z + dz, nz) * band

    def across(t, slot, dz):
        return remote(
            pair[t].at[at[slot], pl.ds((1 - c) * part + first_row(dz), band)],
            other.at[slot, t, dz],
            s_c.at[slot, t, dz], r_c.at[slot, t, dz], (y, z, x, 1 - c),
        )

    def mine(t, slot, dz):
        return pair[t].at[at[slot], pl.ds(c * part + first_row(dz), band)]

    for dz in bands:
        for slot in range(4):
            for t in (0, 1):
                across(t, slot, dz).start()

    def columns(head):
        return pl.ds(pl.multiple_of(head * HD, HD), HD)

    def chip(d):
        pz, px = lax.rem(z + d // nx, nz), lax.rem(x + lax.rem(d, nx), nx)
        return pz * nx + px, (y, pz, px, c)

    def query_out(d):
        head, where = chip(d)
        return remote(dq_ref.at[head], gq.at[:, :, columns(me)], s_q.at[d], r_q.at[d], where)

    def key_out(d, t):
        _, where = chip(d)
        px = lax.rem(x + lax.rem(d, nx), nx)
        return remote(
            total.at[3, t, d // nx, pl.ds(px * rows, rows)], outs[t].at[:, :, columns(me)],
            s_out.at[t, d], r_out.at[t, d], where,
        )

    def key_own(t):
        return pltpu.make_async_copy(
            total.at[3, t, 0, pl.ds(x * rows, rows)], outs[t].at[:, :, columns(me)], own_out.at[t]
        )

    query_own = pltpu.make_async_copy(dq_ref.at[me], gq.at[:, :, columns(me)], own_q)
    keys_in = pltpu.make_async_copy(ka_hbm, ka, own_k)
    keys_in.start()
    pairs = dscore_ref.shape[0]
    per = dq_ref.shape[1]
    span_len = dq_ref.shape[2]
    unroll = min(4, pairs)

    def queries():
        keys_in.wait()

        @pl.loop(0, pairs // unroll)
        def _(step):
            for u in range(unroll):
                p = step * unroll + u
                both = contract(dscore_ref[p], rows_of(ka, entries_of(i_ref, p)), 0, 0)
                sa, sb = 2 * p, 2 * p + 1
                dq_ref[sa // per, lax.rem(sa, per)] = both[:span_len, :HD].astype(jnp.bfloat16)
                dq_ref[sb // per, lax.rem(sb, per)] = both[span_len:, HD:].astype(jnp.bfloat16)

        query_own.start()
        for dz, dx in offsets(nz, nx):
            query_out(dz * nx + dx).start()

    def f32(a):
        return a.astype(jnp.float32)

    def add(dst, *terms):
        @pl.loop(0, band // rows)
        def _(i):
            rs = pl.ds(i * rows, rows)
            sums = f32(terms[0][rs])
            for term in terms[1:]:
                sums = sums + f32(term[rs])
            dst[rs] = sums.astype(jnp.bfloat16)

    def both_cores(t, slot, dz):
        across(t, slot, dz).wait_recv()
        return mine(t, slot, dz), other.at[slot, t, dz]

    def far_copy(t, dz):
        return remote(
            total.at[0, t, dz], passed.at[t, dz], s_f.at[t, dz], r_f.at[t, dz],
            ((up, down)[t], z, x, c),
        )

    def near_copy(t, slot, dz):
        return remote(
            total.at[slot, t, dz], arrived.at[slot - 1, t, dz],
            s_y.at[slot - 1, t, dz], r_y.at[slot - 1, t, dz],
            ((up, down)[slot - 1], z, x, c),
        )

    def direct(dz):
        for t in (0, 1):
            add(total.at[0, t, dz], *both_cores(t, 0, dz))
            far_copy(t, dz).start()
        for t, slot in ((1, 1), (0, 2)):
            add(total.at[slot, t, dz], *both_cores(t, slot, dz))
            near_copy(t, slot, dz).start()

    def merged(dz):
        for t, slot in ((0, 1), (1, 2)):
            terms = both_cores(t, slot, dz)
            far_copy(t, dz).wait_recv()
            add(total.at[slot, t, dz], *terms, passed.at[t, dz])
            near_copy(t, slot, dz).start()

    def final(dz):
        for t in (0, 1):
            terms = both_cores(t, 3, dz)
            near_copy(t, 1, dz).wait_recv()
            near_copy(t, 2, dz).wait_recv()
            add(total.at[3, t, dz], *terms, arrived.at[0, t, dz], arrived.at[1, t, dz])
            for dx in range(nx):
                if dz or dx:
                    key_out(dz * nx + dx, t).start()
                else:
                    key_own(t).start()

    for step in range(nz + 2):
        if step < nz:
            direct(bands[step])
        if step == min(1, nz - 1):
            queries()
        if 1 <= step < nz + 1:
            merged(bands[step - 1])
        if step >= 2:
            final(bands[step - 2])

    @pl.loop(1, chips)
    def _(d):
        query_out(d).wait()
        for t in (0, 1):
            key_out(d, t).wait()

    query_own.wait()
    for t in (0, 1):
        key_own(t).wait()

        @pl.loop(0, nz)
        def _(dz):
            far_copy(t, dz).wait_send()
            for slot in range(4):
                across(t, slot, dz).wait_send()
            for slot in (1, 2):
                near_copy(t, slot, dz).wait_send()


def give(nz, nx, spans, ih, ka, dscore, dk, dv):
    chips = nz * nx
    _, all_rows, tok, _ = dk.shape
    part = all_rows // 2
    band = part // nz
    span_len = dscore.shape[2] // 2
    bf16 = jnp.bfloat16
    dma = pltpu.SemaphoreType.DMA
    row_out = pltpu.VMEM((part // chips, tok, chips * HD), bf16)
    return pl.pallas_call(
        functools.partial(give_kernel, nz, nx),
        name="give",
        out_shape=(pltpu.VMEM((spans, span_len, chips * HD), bf16), row_out, row_out),
        in_specs=[SMEM, HBM] + [VMEM] * 3,
        out_specs=(ANY,) * 3,
        scratch_shapes=[
            pltpu.VMEM(ka.shape, bf16),
            pltpu.VMEM((chips, spans, span_len, HD), bf16),
            pltpu.VMEM((4, 2, nz, band, tok, HD), bf16),
            pltpu.VMEM((4, 2, nz, band, tok, HD), bf16),
            pltpu.VMEM((2, nz, band, tok, HD), bf16),
            pltpu.VMEM((2, 2, nz, band, tok, HD), bf16),
            dma((chips,)), dma((chips,)), dma((2, chips)), dma((2, chips)),
            dma((4, 2, nz)), dma((4, 2, nz)), dma((2, nz)), dma((2, nz)),
            dma((2, 2, nz)), dma((2, 2, nz)), dma, dma((2,)), dma,
        ],
        compiler_params=pltpu.CompilerParams(
            collective_id=1, has_side_effects=True, vmem_limit_bytes=32 * MiB
        ),
    )(ih, *in_hbm(ka), *in_vmem(dscore, dk, dv))


def on_device(nz, nx, query, grad_out, keys, values, owner_list, row_list):
    chips = nz * nx
    rows = keys.shape[0]
    entry = lax.rem(owner_list, 2) * (chips * rows) + (owner_list // 2) * rows + row_list
    entry = jnp.pad(entry, ((0, 0), (0, HD - entry.shape[1])))
    qh, gh, va, ih, lifted, inverse, ka = bring(
        nz, nx, query, grad_out, keys, values, entry
    )
    dscore, dk, dv = attend(ih, qh, gh, va, lifted, inverse)
    return give(nz, nx, query.shape[0], ih, ka, dscore, dk, dv)


def solution(mesh):
    groups, retr = mesh.devices.shape
    nx = 4 if retr == 32 else 2
    nz = retr // (2 * nx)
    fine = Mesh(mesh.devices.reshape(groups, nz, nx, 2), ("y", "z", "x", "c"))
    all_axes = ("y", "z", "x", "c")
    owner = ("z", "x", "c")
    return jax.shard_map(
        functools.partial(on_device, nz, nx),
        mesh=fine,
        in_specs=(
            P(all_axes, None, None),
            P(all_axes, None, None),
            P(owner, None, None),
            P(owner, None, None),
            P(all_axes, None),
            P(all_axes, None),
        ),
        out_specs=(P(all_axes, None, None), P(owner, "y", None), P(owner, "y", None)),
        check_vma=False,
    )
```

```python
import functools

import jax
import jax.numpy as jnp
import numpy as np
from jax import lax
from jax.experimental import pallas as pl
from jax.experimental.pallas import tpu as pltpu
from jax.sharding import Mesh
from jax.sharding import PartitionSpec as P

HD = 128
MiB = 1024 * 1024
ANY = pl.BlockSpec(memory_space=pl.ANY)
VMEM = pl.BlockSpec(memory_space=pltpu.VMEM)
SMEM = pl.BlockSpec(memory_space=pltpu.SMEM)
HBM = pl.BlockSpec(memory_space=pltpu.HBM)


def in_hbm(*arrays):
    return tuple(pltpu.with_memory_space_constraint(a, pltpu.HBM) for a in arrays)


def in_vmem(*arrays):
    return tuple(pltpu.with_memory_space_constraint(a, pltpu.VMEM) for a in arrays)


def place():
    return tuple(lax.axis_index(name) for name in ("y", "z", "x", "c"))


def remote(src, dst, send, recv, where):
    return pltpu.make_async_remote_copy(
        src_ref=src,
        dst_ref=dst,
        send_sem=send,
        recv_sem=recv,
        device_id=where,
        device_id_type=pl.DeviceIdType.MESH,
    )


def greet(nz, nx):
    y, z, x, c = place()
    barrier = pltpu.get_barrier_semaphore()

    def hello(where):
        pl.semaphore_signal(barrier, inc=1, device_id=where, device_id_type=pl.DeviceIdType.MESH)

    @pl.loop(1, nz * nx)
    def _(d):
        hello((y, lax.rem(z + d // nx, nz), lax.rem(x + lax.rem(d, nx), nx), c))

    hello((lax.rem(y + 1, 4), z, x, c))
    hello((lax.rem(y + 3, 4), z, x, c))
    hello((y, z, x, 1 - c))
    pl.semaphore_wait(barrier, nz * nx - 1 + 3)


def contract(a, b, da, db):
    return lax.dot_general(a, b, (((da,), (db,)), ((), ())), preferred_element_type=jnp.float32)


def diagonal(a, b):
    empty = jnp.zeros_like(a)
    return jnp.concatenate(
        [jnp.concatenate([a, empty], axis=1), jnp.concatenate([empty, b], axis=1)], axis=0
    )


def entries_of(i_ref, pair, per):
    return [
        i_ref[s // per, n, lax.rem(s, per)] for s in (2 * pair, 2 * pair + 1) for n in (0, 1)
    ]


def rows_of(ref, entries):
    quarters, _, tok, _ = ref.shape
    taken = [ref[:, e].reshape(quarters * tok, HD) for e in entries]
    return jnp.concatenate(
        [jnp.concatenate(taken[:2], axis=0), jnp.concatenate(taken[2:], axis=0)], axis=1
    )


def tokens_of(ref, pair):
    per = ref.shape[1]
    sa, sb = 2 * pair, 2 * pair + 1
    return diagonal(ref[sa // per, lax.rem(sa, per)], ref[sb // per, lax.rem(sb, per)])


def offsets(nz, nx):
    steps = [(dz, dx) for dz in range(nz) for dx in range(nx) if dz or dx]

    def hops(step):
        return min(step[0], nz - step[0]) + min(step[1], nx - step[1])

    return sorted(steps, key=hops)


def bring_kernel(
    nz, nx,
    q_ref, g_ref, k_ref, v_ref, owner_ref, row_ref,
    qh, gh, va, ih, lifted_ref, inverse_ref, ka_hbm,
    ka, i_ref, i_smem, s_in, r_in, s_y, r_y, s_c, r_c, own,
):
    y, z, x, c = place()
    chips = nz * nx
    rows = k_ref.shape[0]
    part = chips * rows
    quarter = k_ref.shape[1] // 4
    me = z * nx + x
    up, down, far = lax.rem(y + 1, 4), lax.rem(y + 3, 4), lax.rem(y + 2, 4)
    greet(nz, nx)

    owners = owner_ref[...]
    entries = (owners & 1) * part + (owners >> 1) * rows + row_ref[...]
    i_ref[...] = jnp.zeros_like(i_ref)
    i_ref[: entries.shape[0], : entries.shape[1]] = entries

    def columns(head):
        return pl.ds(pl.multiple_of(head * HD, HD), HD)

    def token_part(ref, head):
        return ref.at[:, pl.ds(pl.multiple_of(y * quarter, quarter), quarter), columns(head)]

    def landing(ref):
        return ref.at[y, pl.ds(c * part + me * rows, rows)]

    def sides(t, head):
        if t < 2:
            return token_part((k_ref, v_ref)[t], head), landing((ka, va)[t])
        if t < 4:
            return (q_ref, g_ref)[t - 2].at[:, :, columns(head)], (qh, gh)[t - 2].at[me]
        return i_ref, ih.at[me]

    def to_chip(t, d):
        pz, px = lax.rem(z + d // nx, nz), lax.rem(x + lax.rem(d, nx), nx)
        return remote(*sides(t, pz * nx + px), s_in.at[t, d], r_in.at[t, d], (y, pz, px, c))

    def keep(t):
        return pltpu.make_async_copy(*sides(t, me), own.at[t])

    def arrived(t):
        @pl.loop(1, chips)
        def _(d):
            to_chip(t, d).wait_recv()

        keep(t).wait()

    def send(t):
        for dz, dx in offsets(nz, nx):
            to_chip(t, dz * nx + dx).start()
        keep(t).start()

    for t in (0, 1, 4, 2):
        send(t)

    def chunk(t, at):
        return (ka, va)[t].at[at, pl.ds(c * part, part)]

    def along_y(t, at, slot, where):
        return remote(
            chunk(t, at), chunk(t, at), s_y.at[t, slot], r_y.at[t, slot], (where, z, x, c)
        )

    def across(t, at, slot):
        return remote(
            chunk(t, at), chunk(t, at), s_c.at[t, slot], r_c.at[t, slot], (y, z, x, 1 - c)
        )

    arrived(0)
    along_y(0, y, 0, up).start()
    along_y(0, y, 1, down).start()
    across(0, y, 0).start()
    arrived(1)
    along_y(1, y, 1, down).start()
    across(1, y, 0).start()
    send(3)

    def all_across(t):
        along_y(t, far, 2, up).wait_recv()
        across(t, far, 3).start()
        for slot in range(4):
            across(t, y, slot).wait_recv()

    arrived(4)
    entry_copy = pltpu.make_async_copy(ih, i_smem, own.at[5])
    entry_copy.start()
    entry_copy.wait()
    along_y(0, down, 0, up).wait_recv()
    along_y(0, down, 2, up).start()
    along_y(1, y, 0, up).start()
    across(0, down, 1).start()
    along_y(0, up, 1, down).wait_recv()
    across(0, up, 2).start()
    along_y(1, up, 1, down).wait_recv()
    along_y(1, up, 2, down).start()
    across(1, up, 2).start()
    all_across(0)
    keep_keys = pltpu.make_async_copy(ka, ka_hbm, own.at[6])
    keep_keys.start()
    arrived(2)

    to_base2 = HD ** -0.5 * float(np.log2(np.e))
    pairs = lifted_ref.shape[0]
    unroll = min(4, pairs)

    def weigh(first, last):
        @pl.loop(first, last)
        def _(step):
            for u in range(unroll):
                p = step * unroll + u
                scores = contract(rows_of(ka, entries_of(i_smem, p, qh.shape[1])), tokens_of(qh, p), 1, 1)
                lifted = jnp.exp2((scores - jnp.max(scores, axis=0, keepdims=True)) * to_base2)
                inverse_ref[p] = 1.0 / jnp.sum(lifted, axis=0, keepdims=True)
                lifted_ref[p] = lifted.astype(jnp.bfloat16)

    steps = pairs // unroll
    weigh(0, steps // 2)
    along_y(1, down, 0, up).wait_recv()
    across(1, down, 1).start()
    weigh(steps // 2, steps)
    all_across(1)
    arrived(3)
    keep_keys.wait()
    for t in range(5):

        @pl.loop(1, chips)
        def _(d):
            to_chip(t, d).wait_send()

    for t in (0, 1):
        for slot in range(3):
            along_y(t, y, slot, up).wait_send()
        for slot in range(4):
            across(t, y, slot).wait_send()


def bring(nz, nx, query, grad_out, keys, values, owner_list, row_list):
    chips = nz * nx
    rows, tokens, _ = keys.shape
    spans, span_len, _ = query.shape
    bf16 = jnp.bfloat16
    held = pltpu.VMEM((4, 2 * chips * rows, tokens // 4, HD), bf16)
    heads = pltpu.VMEM((chips, spans, span_len, HD), bf16)
    pairs = chips * spans // 2
    listed = (8, HD)
    dma = pltpu.SemaphoreType.DMA
    return pl.pallas_call(
        functools.partial(bring_kernel, nz, nx),
        name="bring",
        out_shape=(
            heads, heads, held,
            jax.ShapeDtypeStruct((chips,) + listed, jnp.int32),
            pltpu.VMEM((pairs, 2 * tokens, 2 * span_len), bf16),
            pltpu.VMEM((pairs, 1, 2 * span_len), jnp.float32),
            pltpu.HBM(held.shape, bf16),
        ),
        in_specs=[HBM] * 4 + [VMEM] * 2,
        out_specs=(VMEM,) * 3 + (ANY,) + (VMEM,) * 2 + (HBM,),
        scratch_shapes=[
            pltpu.VMEM(held.shape, bf16),
            pltpu.VMEM(listed, jnp.int32),
            pltpu.SMEM((chips,) + listed, jnp.int32),
            dma((5, chips)), dma((5, chips)), dma((2, 3)), dma((2, 3)), dma((2, 4)), dma((2, 4)), dma((7,)),
        ],
        compiler_params=pltpu.CompilerParams(
            collective_id=0, has_side_effects=True, vmem_limit_bytes=14 * MiB
        ),
    )(*in_hbm(query, grad_out, keys, values), owner_list.T, row_list.T)


def attend_kernel(
    i_ref, qh, gh, va, lifted_ref, inverse_ref, dscore_ref, dk_low, dv_low, dk, dv
):
    quarters, rows, tok, _ = va.shape
    tokens = quarters * tok
    scaling = HD ** -0.5
    pairs = lifted_ref.shape[0]
    unroll = min(8, pairs)

    def add(sums, entries, terms):
        for at, e in enumerate(entries):
            rs = slice(at % 2 * tokens, (at % 2 + 1) * tokens)
            cs = slice(at // 2 * HD, (at // 2 + 1) * HD)
            sums[:, e] += terms[rs, cs].reshape(quarters, tok, HD)

    def gradients(p):
        entries = entries_of(i_ref, p, qh.shape[1])
        grads = tokens_of(gh, p)
        dprob = contract(rows_of(va, entries), grads, 1, 1)
        inverse = inverse_ref[p]
        lifted = lifted_ref[p].astype(jnp.float32)
        delta = jnp.sum(lifted * dprob, axis=0, keepdims=True) * inverse
        chance_low = (lifted * inverse).astype(jnp.bfloat16)
        dscore = (lifted * (inverse * scaling) * (dprob - delta)).astype(jnp.bfloat16)
        dscore_ref[p] = dscore
        return entries, contract(chance_low, grads, 1, 0)

    @pl.loop(0, rows)
    def _(r):
        dk[:, r] = jnp.zeros((quarters, tok, HD), jnp.float32)
        dv[:, r] = jnp.zeros((quarters, tok, HD), jnp.float32)

    @pl.loop(0, pairs // unroll)
    def _(step):
        results = [gradients(step * unroll + u) for u in range(unroll)]
        for entries, value_terms in results:
            add(dv, entries, value_terms)

    @pl.loop(0, pairs // unroll)
    def _(step):
        results = []
        for u in range(unroll):
            p = step * unroll + u
            results.append(
                (entries_of(i_ref, p, qh.shape[1]), contract(dscore_ref[p], tokens_of(qh, p), 1, 0))
            )
        for entries, key_terms in results:
            add(dk, entries, key_terms)

    @pl.loop(0, rows)
    def _(r):
        dk_low[:, r] = dk[:, r].astype(jnp.bfloat16)
        dv_low[:, r] = dv[:, r].astype(jnp.bfloat16)


def attend(ih, qh, gh, va, lifted, inverse):
    held = pltpu.VMEM(va.shape, jnp.bfloat16)
    work = lifted.size * HD * 2
    return pl.pallas_call(
        attend_kernel,
        name="attend",
        out_shape=(pltpu.VMEM(lifted.shape, jnp.bfloat16), held, held),
        in_specs=[SMEM] + [VMEM] * 5,
        out_specs=(VMEM,) * 3,
        scratch_shapes=[pltpu.VMEM(va.shape, jnp.float32)] * 2,
        input_output_aliases={4: 0, 3: 2},
        compiler_params=pltpu.CompilerParams(vmem_limit_bytes=28 * MiB),
        cost_estimate=pl.CostEstimate(flops=3 * work, bytes_accessed=4 * MiB, transcendentals=0),
    )(ih, *in_vmem(qh, gh, va, lifted, inverse))


def give_kernel(
    nz, nx,
    i_ref, ka_hbm, dscore_ref, dk_ref, dv_ref,
    gq, gk, gv,
    ka, dq_ref, other, total, passed, arrived,
    s_q, r_q, s_out, r_out, s_c, r_c, s_f, r_f, s_y, r_y, own_q, own_out, own_k,
):
    y, z, x, c = place()
    chips = nz * nx
    rows = gk.shape[0]
    half = rows // 2
    me = z * nx + x
    up, down, far = lax.rem(y + 1, 4), lax.rem(y + 3, 4), lax.rem(y + 2, 4)
    pair = (dk_ref, dv_ref)
    outs = (gk, gv)
    greet(nz, nx)

    at = (far, up, down, y)
    bands = [(dz, h) for dz in sorted(range(nz), key=lambda dz: -min(dz, nz - dz)) for h in (0, 1)]

    def rows_at(t, slot, dz, h, core):
        first = core * chips + lax.rem(z + dz, nz) * nx
        return pair[t].at[at[slot], pl.ds(first, nx), pl.ds(h * half, half)]

    def across(t, slot, dz, h):
        return remote(
            rows_at(t, slot, dz, h, 1 - c), other.at[slot, t, dz, h],
            s_c.at[slot, t, dz, h], r_c.at[slot, t, dz, h], (y, z, x, 1 - c),
        )

    for dz, h in bands:
        for slot in range(4):
            for t in (0, 1):
                across(t, slot, dz, h).start()

    def columns(head):
        return pl.ds(pl.multiple_of(head * HD, HD), HD)

    def chip(d):
        pz, px = lax.rem(z + d // nx, nz), lax.rem(x + lax.rem(d, nx), nx)
        return pz * nx + px, (y, pz, px, c)

    def query_out(d):
        head, where = chip(d)
        return remote(dq_ref.at[head], gq.at[:, :, columns(me)], s_q.at[d], r_q.at[d], where)

    def key_out(d, t, h):
        _, where = chip(d)
        px = lax.rem(x + lax.rem(d, nx), nx)
        return remote(
            total.at[3, t, d // nx, h, px], outs[t].at[pl.ds(h * half, half), :, columns(me)],
            s_out.at[t, h, d], r_out.at[t, h, d], where,
        )

    def key_own(t, h):
        return pltpu.make_async_copy(
            total.at[3, t, 0, h, x], outs[t].at[pl.ds(h * half, half), :, columns(me)],
            own_out.at[t, h],
        )

    query_own = pltpu.make_async_copy(dq_ref.at[me], gq.at[:, :, columns(me)], own_q)
    keys_in = pltpu.make_async_copy(ka_hbm, ka, own_k)
    keys_in.start()
    pairs = dscore_ref.shape[0]
    per = dq_ref.shape[1]
    span_len = dq_ref.shape[2]
    unroll = min(4, pairs)

    def queries():
        keys_in.wait()

        @pl.loop(0, pairs // unroll)
        def _(step):
            for u in range(unroll):
                p = step * unroll + u
                both = contract(dscore_ref[p], rows_of(ka, entries_of(i_ref, p, per)), 0, 0)
                sa, sb = 2 * p, 2 * p + 1
                dq_ref[sa // per, lax.rem(sa, per)] = both[:span_len, :HD].astype(jnp.bfloat16)
                dq_ref[sb // per, lax.rem(sb, per)] = both[span_len:, HD:].astype(jnp.bfloat16)

        query_own.start()
        for dz, dx in offsets(nz, nx):
            query_out(dz * nx + dx).start()

    def f32(a):
        return a.astype(jnp.float32)

    def add(dst, *terms):
        @pl.loop(0, nx)
        def _(i):
            sums = f32(terms[0][i])
            for term in terms[1:]:
                sums = sums + f32(term[i])
            dst[i] = sums.astype(jnp.bfloat16)

    def both_cores(t, slot, dz, h):
        across(t, slot, dz, h).wait_recv()
        return rows_at(t, slot, dz, h, c), other.at[slot, t, dz, h]

    def far_copy(t, dz, h):
        return remote(
            total.at[0, t, dz, h], passed.at[t, dz, h], s_f.at[t, dz, h], r_f.at[t, dz, h],
            ((up, down)[t], z, x, c),
        )

    def near_copy(t, slot, dz, h):
        return remote(
            total.at[slot, t, dz, h], arrived.at[slot - 1, t, dz, h],
            s_y.at[slot - 1, t, dz, h], r_y.at[slot - 1, t, dz, h],
            ((up, down)[slot - 1], z, x, c),
        )

    def direct(dz, h):
        for t in (0, 1):
            add(total.at[0, t, dz, h], *both_cores(t, 0, dz, h))
            far_copy(t, dz, h).start()
        for t, slot in ((1, 1), (0, 2)):
            add(total.at[slot, t, dz, h], *both_cores(t, slot, dz, h))
            near_copy(t, slot, dz, h).start()

    def merged(dz, h):
        for t, slot in ((0, 1), (1, 2)):
            terms = both_cores(t, slot, dz, h)
            far_copy(t, dz, h).wait_recv()
            add(total.at[slot, t, dz, h], *terms, passed.at[t, dz, h])
            near_copy(t, slot, dz, h).start()

    def final(dz, h):
        for t in (0, 1):
            terms = both_cores(t, 3, dz, h)
            near_copy(t, 1, dz, h).wait_recv()
            near_copy(t, 2, dz, h).wait_recv()
            add(total.at[3, t, dz, h], *terms, arrived.at[0, t, dz, h], arrived.at[1, t, dz, h])
            for dx in range(nx):
                if dz or dx:
                    key_out(dz * nx + dx, t, h).start()
                else:
                    key_own(t, h).start()

    lag = 2
    for step in range(len(bands) + 2 * lag):
        if step < len(bands):
            direct(*bands[step])
        if step == 2:
            queries()
        if lag <= step < len(bands) + lag:
            merged(*bands[step - lag])
        if step >= 2 * lag:
            final(*bands[step - 2 * lag])

    @pl.loop(1, chips)
    def _(d):
        query_out(d).wait()
        for t in (0, 1):
            for h in (0, 1):
                key_out(d, t, h).wait()

    query_own.wait()
    for t in (0, 1):
        for h in (0, 1):
            key_own(t, h).wait()

            @pl.loop(0, nz)
            def _(dz):
                far_copy(t, dz, h).wait_send()
                for slot in range(4):
                    across(t, slot, dz, h).wait_send()
                for slot in (1, 2):
                    near_copy(t, slot, dz, h).wait_send()


def give(nz, nx, spans, ih, ka, dscore, dk, dv):
    chips = nz * nx
    _, all_rows, tok, _ = dk.shape
    part = all_rows // 2
    rows = part // chips
    piece = (nz, 2, nx, rows // 2, tok, HD)
    span_len = dscore.shape[2] // 2
    bf16 = jnp.bfloat16
    dma = pltpu.SemaphoreType.DMA
    def split(sums):
        return sums.reshape(4, 2 * chips, rows, tok, HD)

    row_out = pltpu.VMEM((part // chips, tok, chips * HD), bf16)
    return pl.pallas_call(
        functools.partial(give_kernel, nz, nx),
        name="give",
        out_shape=(pltpu.VMEM((spans, span_len, chips * HD), bf16), row_out, row_out),
        in_specs=[SMEM, HBM] + [VMEM] * 3,
        out_specs=(ANY,) * 3,
        scratch_shapes=[
            pltpu.VMEM(ka.shape, bf16),
            pltpu.VMEM((chips, spans, span_len, HD), bf16),
            pltpu.VMEM((4, 2) + piece, bf16),
            pltpu.VMEM((4, 2) + piece, bf16),
            pltpu.VMEM((2,) + piece, bf16),
            pltpu.VMEM((2, 2) + piece, bf16),
            dma((chips,)), dma((chips,)), dma((2, 2, chips)), dma((2, 2, chips)),
            dma((4, 2, nz, 2)), dma((4, 2, nz, 2)), dma((2, nz, 2)), dma((2, nz, 2)),
            dma((2, 2, nz, 2)), dma((2, 2, nz, 2)), dma, dma((2, 2)), dma,
        ],
        compiler_params=pltpu.CompilerParams(
            collective_id=1, has_side_effects=True, vmem_limit_bytes=32 * MiB
        ),
    )(ih, *in_hbm(ka), *in_vmem(dscore, split(dk), split(dv)))


def write_kernel(*refs):
    count = (len(refs) - 1) // 2
    copies = [
        pltpu.make_async_copy(refs[i], refs[count + i], refs[-1].at[i]) for i in range(count)
    ]
    for copy in copies:
        copy.start()
    for copy in copies:
        copy.wait()


def write(*arrays):
    return pl.pallas_call(
        write_kernel,
        name="write",
        out_shape=tuple(pltpu.HBM(a.shape, a.dtype) for a in arrays),
        in_specs=[VMEM] * len(arrays),
        out_specs=(HBM,) * len(arrays),
        scratch_shapes=[pltpu.SemaphoreType.DMA((len(arrays),))],
        compiler_params=pltpu.CompilerParams(vmem_limit_bytes=8 * MiB),
    )(*in_vmem(*arrays))


def on_device(nz, nx, query, grad_out, keys, values, owner_list, row_list):
    qh, gh, va, ih, lifted, inverse, ka = bring(
        nz, nx, query, grad_out, keys, values, owner_list, row_list
    )
    dscore, dk, dv = attend(ih, qh, gh, va, lifted, inverse)
    return write(*give(nz, nx, query.shape[0], ih, ka, dscore, dk, dv))


def solution(mesh):
    groups, retr = mesh.devices.shape
    nx = 4 if retr == 32 else 2
    nz = retr // (2 * nx)
    fine = Mesh(mesh.devices.reshape(groups, nz, nx, 2), ("y", "z", "x", "c"))
    all_axes = ("y", "z", "x", "c")
    owner = ("z", "x", "c")
    return jax.shard_map(
        functools.partial(on_device, nz, nx),
        mesh=fine,
        in_specs=(
            P(all_axes, None, None),
            P(all_axes, None, None),
            P(owner, None, None),
            P(owner, None, None),
            P(all_axes, None),
            P(all_axes, None),
        ),
        out_specs=(P(all_axes, None, None), P(owner, "y", None), P(owner, "y", None)),
        check_vma=False,
    )
```

```python
import functools

import jax
import jax.numpy as jnp
import numpy as np
from jax import lax
from jax.experimental import pallas as pl
from jax.experimental.pallas import tpu as pltpu
from jax.sharding import Mesh
from jax.sharding import PartitionSpec as P

HD = 128
MiB = 1024 * 1024
ANY = pl.BlockSpec(memory_space=pl.ANY)
VMEM = pl.BlockSpec(memory_space=pltpu.VMEM)
SMEM = pl.BlockSpec(memory_space=pltpu.SMEM)
HBM = pl.BlockSpec(memory_space=pltpu.HBM)


def in_hbm(*arrays):
    return tuple(pltpu.with_memory_space_constraint(a, pltpu.HBM) for a in arrays)


def in_vmem(*arrays):
    return tuple(pltpu.with_memory_space_constraint(a, pltpu.VMEM) for a in arrays)


def place():
    return tuple(lax.axis_index(name) for name in ("y", "z", "x", "c"))


def remote(src, dst, send, recv, where):
    return pltpu.make_async_remote_copy(
        src_ref=src,
        dst_ref=dst,
        send_sem=send,
        recv_sem=recv,
        device_id=where,
        device_id_type=pl.DeviceIdType.MESH,
    )


def greet(nz, nx):
    y, z, x, c = place()
    barrier = pltpu.get_barrier_semaphore()

    def hello(where):
        pl.semaphore_signal(barrier, inc=1, device_id=where, device_id_type=pl.DeviceIdType.MESH)

    @pl.loop(1, nz * nx)
    def _(d):
        hello((y, lax.rem(z + d // nx, nz), lax.rem(x + lax.rem(d, nx), nx), c))

    hello((lax.rem(y + 1, 4), z, x, c))
    hello((lax.rem(y + 3, 4), z, x, c))
    hello((y, z, x, 1 - c))
    pl.semaphore_wait(barrier, nz * nx - 1 + 3)


def contract(a, b, da, db):
    return lax.dot_general(a, b, (((da,), (db,)), ((), ())), preferred_element_type=jnp.float32)


def diagonal(a, b):
    empty = jnp.zeros_like(a)
    return jnp.concatenate(
        [jnp.concatenate([a, empty], axis=1), jnp.concatenate([empty, b], axis=1)], axis=0
    )


def entries_of(i_ref, pair, per):
    return [
        i_ref[s // per, n, lax.rem(s, per)] for s in (2 * pair, 2 * pair + 1) for n in (0, 1)
    ]


def rows_of(ref, entries):
    quarters, _, tok, _ = ref.shape
    taken = [ref[:, e].reshape(quarters * tok, HD) for e in entries]
    return jnp.concatenate(
        [jnp.concatenate(taken[:2], axis=0), jnp.concatenate(taken[2:], axis=0)], axis=1
    )


def tokens_of(ref, pair):
    per = ref.shape[1]
    sa, sb = 2 * pair, 2 * pair + 1
    return diagonal(ref[sa // per, lax.rem(sa, per)], ref[sb // per, lax.rem(sb, per)])


def offsets(nz, nx):
    steps = [(dz, dx) for dz in range(nz) for dx in range(nx) if dz or dx]

    def hops(step):
        return min(step[0], nz - step[0]) + min(step[1], nx - step[1])

    return sorted(steps, key=hops)


def bring_kernel(
    nz, nx,
    q_ref, g_ref, k_ref, v_ref, owner_ref, row_ref,
    qh, gh, va, ih, lifted_ref, inverse_ref, ka_hbm,
    ka, i_ref, i_smem, o_vmem, w_vmem, s_in, r_in, s_y, r_y, s_c, r_c, own,
):
    y, z, x, c = place()
    chips = nz * nx
    rows = k_ref.shape[0]
    part = chips * rows
    quarter = k_ref.shape[1] // 4
    me = z * nx + x
    up, down, far = lax.rem(y + 1, 4), lax.rem(y + 3, 4), lax.rem(y + 2, 4)
    lists = (
        pltpu.make_async_copy(owner_ref, o_vmem, own.at[7]),
        pltpu.make_async_copy(row_ref, w_vmem, own.at[8]),
    )
    for copy in lists:
        copy.start()
    greet(nz, nx)
    for copy in lists:
        copy.wait()

    owners = o_vmem[...]
    entries = (owners & 1) * part + (owners >> 1) * rows + w_vmem[...]
    i_ref[...] = jnp.zeros_like(i_ref)
    i_ref[: entries.shape[0], : entries.shape[1]] = entries

    def columns(head):
        return pl.ds(pl.multiple_of(head * HD, HD), HD)

    def token_part(ref, head):
        return ref.at[:, pl.ds(pl.multiple_of(y * quarter, quarter), quarter), columns(head)]

    def landing(ref):
        return ref.at[y, pl.ds(c * part + me * rows, rows)]

    def sides(t, head):
        if t < 2:
            return token_part((k_ref, v_ref)[t], head), landing((ka, va)[t])
        if t < 4:
            return (q_ref, g_ref)[t - 2].at[:, :, columns(head)], (qh, gh)[t - 2].at[me]
        return i_ref, ih.at[me]

    def to_chip(t, d):
        pz, px = lax.rem(z + d // nx, nz), lax.rem(x + lax.rem(d, nx), nx)
        return remote(*sides(t, pz * nx + px), s_in.at[t, d], r_in.at[t, d], (y, pz, px, c))

    def keep(t):
        return pltpu.make_async_copy(*sides(t, me), own.at[t])

    def arrived(t):
        @pl.loop(1, chips)
        def _(d):
            to_chip(t, d).wait_recv()

        keep(t).wait()

    def send(t):
        for dz, dx in offsets(nz, nx):
            to_chip(t, dz * nx + dx).start()
        keep(t).start()

    for t in (0, 1, 4, 2):
        send(t)

    def chunk(t, at):
        return (ka, va)[t].at[at, pl.ds(c * part, part)]

    def along_y(t, at, slot, where):
        return remote(
            chunk(t, at), chunk(t, at), s_y.at[t, slot], r_y.at[t, slot], (where, z, x, c)
        )

    def across(t, at, slot):
        return remote(
            chunk(t, at), chunk(t, at), s_c.at[t, slot], r_c.at[t, slot], (y, z, x, 1 - c)
        )

    arrived(0)
    along_y(0, y, 0, up).start()
    along_y(0, y, 1, down).start()
    across(0, y, 0).start()
    arrived(1)
    along_y(1, y, 1, down).start()
    across(1, y, 0).start()
    send(3)

    def all_across(t):
        along_y(t, far, 2, up).wait_recv()
        across(t, far, 3).start()
        for slot in range(4):
            across(t, y, slot).wait_recv()

    arrived(4)
    entry_copy = pltpu.make_async_copy(ih, i_smem, own.at[5])
    entry_copy.start()
    entry_copy.wait()
    along_y(0, down, 0, up).wait_recv()
    along_y(0, down, 2, up).start()
    along_y(1, y, 0, up).start()
    across(0, down, 1).start()
    along_y(0, up, 1, down).wait_recv()
    across(0, up, 2).start()
    along_y(1, up, 1, down).wait_recv()
    along_y(1, up, 2, down).start()
    across(1, up, 2).start()
    all_across(0)
    keep_keys = pltpu.make_async_copy(ka, ka_hbm, own.at[6])
    keep_keys.start()
    arrived(2)

    to_base2 = HD ** -0.5 * float(np.log2(np.e))
    pairs = lifted_ref.shape[0]
    unroll = min(4, pairs)

    def weigh(first, last):
        @pl.loop(first, last)
        def _(step):
            for u in range(unroll):
                p = step * unroll + u
                scores = contract(rows_of(ka, entries_of(i_smem, p, qh.shape[1])), tokens_of(qh, p), 1, 1)
                lifted = jnp.exp2((scores - jnp.max(scores, axis=0, keepdims=True)) * to_base2)
                inverse_ref[p] = 1.0 / jnp.sum(lifted, axis=0, keepdims=True)
                lifted_ref[p] = lifted.astype(jnp.bfloat16)

    steps = pairs // unroll
    weigh(0, steps // 2)
    along_y(1, down, 0, up).wait_recv()
    across(1, down, 1).start()
    weigh(steps // 2, steps)
    all_across(1)
    arrived(3)
    keep_keys.wait()
    for t in range(5):

        @pl.loop(1, chips)
        def _(d):
            to_chip(t, d).wait_send()

    for t in (0, 1):
        for slot in range(3):
            along_y(t, y, slot, up).wait_send()
        for slot in range(4):
            across(t, y, slot).wait_send()


def bring(nz, nx, query, grad_out, keys, values, owner_list, row_list):
    chips = nz * nx
    rows, tokens, _ = keys.shape
    spans, span_len, _ = query.shape
    bf16 = jnp.bfloat16
    held = pltpu.VMEM((4, 2 * chips * rows, tokens // 4, HD), bf16)
    heads = pltpu.VMEM((chips, spans, span_len, HD), bf16)
    pairs = chips * spans // 2
    listed = (8, HD)
    dma = pltpu.SemaphoreType.DMA
    return pl.pallas_call(
        functools.partial(bring_kernel, nz, nx),
        name="bring",
        out_shape=(
            heads, heads, held,
            jax.ShapeDtypeStruct((chips,) + listed, jnp.int32),
            pltpu.VMEM((pairs, 2 * tokens, 2 * span_len), bf16),
            pltpu.VMEM((pairs, 1, 2 * span_len), jnp.float32),
            pltpu.HBM(held.shape, bf16),
        ),
        in_specs=[HBM] * 6,
        out_specs=(VMEM,) * 3 + (ANY,) + (VMEM,) * 2 + (HBM,),
        scratch_shapes=[
            pltpu.VMEM(held.shape, bf16),
            pltpu.VMEM(listed, jnp.int32),
            pltpu.SMEM((chips,) + listed, jnp.int32),
            pltpu.VMEM((2, spans), jnp.int32),
            pltpu.VMEM((2, spans), jnp.int32),
            dma((5, chips)), dma((5, chips)), dma((2, 3)), dma((2, 3)), dma((2, 4)), dma((2, 4)), dma((9,)),
        ],
        compiler_params=pltpu.CompilerParams(
            collective_id=0, has_side_effects=True, vmem_limit_bytes=14 * MiB
        ),
    )(*in_hbm(query, grad_out, keys, values, owner_list.T, row_list.T))


def attend_kernel(
    i_hbm, qh, gh, va, lifted_ref, inverse_ref, dscore_ref, dk_low, dv_low, dk, dv, i_ref, sem
):
    quarters, rows, tok, _ = va.shape
    tokens = quarters * tok
    scaling = HD ** -0.5
    pairs = lifted_ref.shape[0]
    unroll = min(8, pairs)

    def add(sums, entries, terms):
        for at, e in enumerate(entries):
            rs = slice(at % 2 * tokens, (at % 2 + 1) * tokens)
            cs = slice(at // 2 * HD, (at // 2 + 1) * HD)
            sums[:, e] += terms[rs, cs].reshape(quarters, tok, HD)

    def gradients(p):
        entries = entries_of(i_ref, p, qh.shape[1])
        grads = tokens_of(gh, p)
        dprob = contract(rows_of(va, entries), grads, 1, 1)
        inverse = inverse_ref[p]
        lifted = lifted_ref[p].astype(jnp.float32)
        delta = jnp.sum(lifted * dprob, axis=0, keepdims=True) * inverse
        chance_low = (lifted * inverse).astype(jnp.bfloat16)
        dscore = (lifted * (inverse * scaling) * (dprob - delta)).astype(jnp.bfloat16)
        dscore_ref[p] = dscore
        return entries, contract(chance_low, grads, 1, 0)

    lists = pltpu.make_async_copy(i_hbm, i_ref, sem)
    lists.start()

    @pl.loop(0, rows)
    def _(r):
        dk[:, r] = jnp.zeros((quarters, tok, HD), jnp.float32)
        dv[:, r] = jnp.zeros((quarters, tok, HD), jnp.float32)

    lists.wait()

    @pl.loop(0, pairs // unroll)
    def _(step):
        results = [gradients(step * unroll + u) for u in range(unroll)]
        for entries, value_terms in results:
            add(dv, entries, value_terms)

    @pl.loop(0, pairs // unroll)
    def _(step):
        results = []
        for u in range(unroll):
            p = step * unroll + u
            results.append(
                (entries_of(i_ref, p, qh.shape[1]), contract(dscore_ref[p], tokens_of(qh, p), 1, 0))
            )
        for entries, key_terms in results:
            add(dk, entries, key_terms)

    @pl.loop(0, rows)
    def _(r):
        dk_low[:, r] = dk[:, r].astype(jnp.bfloat16)
        dv_low[:, r] = dv[:, r].astype(jnp.bfloat16)


def attend(ih, qh, gh, va, lifted, inverse):
    held = pltpu.VMEM(va.shape, jnp.bfloat16)
    work = lifted.size * HD * 2
    return pl.pallas_call(
        attend_kernel,
        name="attend",
        out_shape=(pltpu.VMEM(lifted.shape, jnp.bfloat16), held, held),
        in_specs=[ANY] + [VMEM] * 5,
        out_specs=(VMEM,) * 3,
        scratch_shapes=[
            pltpu.VMEM(va.shape, jnp.float32),
            pltpu.VMEM(va.shape, jnp.float32),
            pltpu.SMEM(ih.shape, jnp.int32),
            pltpu.SemaphoreType.DMA,
        ],
        input_output_aliases={4: 0, 3: 2},
        compiler_params=pltpu.CompilerParams(vmem_limit_bytes=28 * MiB),
        cost_estimate=pl.CostEstimate(flops=3 * work, bytes_accessed=4 * MiB, transcendentals=0),
    )(ih, *in_vmem(qh, gh, va, lifted, inverse))


def give_kernel(
    nz, nx,
    i_hbm, ka_hbm, dscore_ref, dk_ref, dv_ref,
    gq, gk, gv,
    i_ref, ka, dq_ref, other, total, passed, arrived,
    s_q, r_q, s_out, r_out, s_c, r_c, s_f, r_f, s_y, r_y, own_q, own_out, own_k, own_i,
):
    y, z, x, c = place()
    chips = nz * nx
    rows = gk.shape[0]
    half = rows // 2
    me = z * nx + x
    up, down, far = lax.rem(y + 1, 4), lax.rem(y + 3, 4), lax.rem(y + 2, 4)
    pair = (dk_ref, dv_ref)
    outs = (gk, gv)
    greet(nz, nx)

    at = (far, up, down, y)
    bands = [(dz, h) for dz in sorted(range(nz), key=lambda dz: -min(dz, nz - dz)) for h in (0, 1)]

    def rows_at(t, slot, dz, h, core):
        first = core * chips + lax.rem(z + dz, nz) * nx
        return pair[t].at[at[slot], pl.ds(first, nx), pl.ds(h * half, half)]

    def across(t, slot, dz, h):
        return remote(
            rows_at(t, slot, dz, h, 1 - c), other.at[slot, t, dz, h],
            s_c.at[slot, t, dz, h], r_c.at[slot, t, dz, h], (y, z, x, 1 - c),
        )

    for dz, h in bands:
        for slot in range(4):
            for t in (0, 1):
                across(t, slot, dz, h).start()

    def columns(head):
        return pl.ds(pl.multiple_of(head * HD, HD), HD)

    def chip(d):
        pz, px = lax.rem(z + d // nx, nz), lax.rem(x + lax.rem(d, nx), nx)
        return pz * nx + px, (y, pz, px, c)

    def query_out(d):
        head, where = chip(d)
        return remote(dq_ref.at[head], gq.at[:, :, columns(me)], s_q.at[d], r_q.at[d], where)

    def key_out(d, t, h):
        _, where = chip(d)
        px = lax.rem(x + lax.rem(d, nx), nx)
        return remote(
            total.at[3, t, d // nx, h, px], outs[t].at[pl.ds(h * half, half), :, columns(me)],
            s_out.at[t, h, d], r_out.at[t, h, d], where,
        )

    def key_own(t, h):
        return pltpu.make_async_copy(
            total.at[3, t, 0, h, x], outs[t].at[pl.ds(h * half, half), :, columns(me)],
            own_out.at[t, h],
        )

    query_own = pltpu.make_async_copy(dq_ref.at[me], gq.at[:, :, columns(me)], own_q)
    keys_in = pltpu.make_async_copy(ka_hbm, ka, own_k)
    keys_in.start()
    lists = pltpu.make_async_copy(i_hbm, i_ref, own_i)
    lists.start()
    pairs = dscore_ref.shape[0]
    per = dq_ref.shape[1]
    span_len = dq_ref.shape[2]
    unroll = min(4, pairs)

    def queries():
        keys_in.wait()
        lists.wait()

        @pl.loop(0, pairs // unroll)
        def _(step):
            for u in range(unroll):
                p = step * unroll + u
                both = contract(dscore_ref[p], rows_of(ka, entries_of(i_ref, p, per)), 0, 0)
                sa, sb = 2 * p, 2 * p + 1
                dq_ref[sa // per, lax.rem(sa, per)] = both[:span_len, :HD].astype(jnp.bfloat16)
                dq_ref[sb // per, lax.rem(sb, per)] = both[span_len:, HD:].astype(jnp.bfloat16)

        query_own.start()
        for dz, dx in offsets(nz, nx):
            query_out(dz * nx + dx).start()

    def f32(a):
        return a.astype(jnp.float32)

    def add(dst, *terms):
        @pl.loop(0, nx)
        def _(i):
            sums = f32(terms[0][i])
            for term in terms[1:]:
                sums = sums + f32(term[i])
            dst[i] = sums.astype(jnp.bfloat16)

    def both_cores(t, slot, dz, h):
        across(t, slot, dz, h).wait_recv()
        return rows_at(t, slot, dz, h, c), other.at[slot, t, dz, h]

    def far_copy(t, dz, h):
        return remote(
            total.at[0, t, dz, h], passed.at[t, dz, h], s_f.at[t, dz, h], r_f.at[t, dz, h],
            ((up, down)[t], z, x, c),
        )

    def near_copy(t, slot, dz, h):
        return remote(
            total.at[slot, t, dz, h], arrived.at[slot - 1, t, dz, h],
            s_y.at[slot - 1, t, dz, h], r_y.at[slot - 1, t, dz, h],
            ((up, down)[slot - 1], z, x, c),
        )

    def direct(dz, h):
        for t in (0, 1):
            add(total.at[0, t, dz, h], *both_cores(t, 0, dz, h))
            far_copy(t, dz, h).start()
        for t, slot in ((1, 1), (0, 2)):
            add(total.at[slot, t, dz, h], *both_cores(t, slot, dz, h))
            near_copy(t, slot, dz, h).start()

    def merged(dz, h):
        for t, slot in ((0, 1), (1, 2)):
            terms = both_cores(t, slot, dz, h)
            far_copy(t, dz, h).wait_recv()
            add(total.at[slot, t, dz, h], *terms, passed.at[t, dz, h])
            near_copy(t, slot, dz, h).start()

    def final(dz, h):
        for t in (0, 1):
            terms = both_cores(t, 3, dz, h)
            near_copy(t, 1, dz, h).wait_recv()
            near_copy(t, 2, dz, h).wait_recv()
            add(total.at[3, t, dz, h], *terms, arrived.at[0, t, dz, h], arrived.at[1, t, dz, h])
            for dx in range(nx):
                if dz or dx:
                    key_out(dz * nx + dx, t, h).start()
                else:
                    key_own(t, h).start()

    lag = 2
    for step in range(len(bands) + 2 * lag):
        if step < len(bands):
            direct(*bands[step])
        if step == 2:
            queries()
        if lag <= step < len(bands) + lag:
            merged(*bands[step - lag])
        if step >= 2 * lag:
            final(*bands[step - 2 * lag])

    @pl.loop(1, chips)
    def _(d):
        query_out(d).wait()
        for t in (0, 1):
            for h in (0, 1):
                key_out(d, t, h).wait()

    query_own.wait()
    for t in (0, 1):
        for h in (0, 1):
            key_own(t, h).wait()

            @pl.loop(0, nz)
            def _(dz):
                far_copy(t, dz, h).wait_send()
                for slot in range(4):
                    across(t, slot, dz, h).wait_send()
                for slot in (1, 2):
                    near_copy(t, slot, dz, h).wait_send()


def give(nz, nx, spans, ih, ka, dscore, dk, dv):
    chips = nz * nx
    _, all_rows, tok, _ = dk.shape
    part = all_rows // 2
    rows = part // chips
    piece = (nz, 2, nx, rows // 2, tok, HD)
    span_len = dscore.shape[2] // 2
    bf16 = jnp.bfloat16
    dma = pltpu.SemaphoreType.DMA
    def split(sums):
        return sums.reshape(4, 2 * chips, rows, tok, HD)

    row_out = pltpu.VMEM((part // chips, tok, chips * HD), bf16)
    return pl.pallas_call(
        functools.partial(give_kernel, nz, nx),
        name="give",
        out_shape=(pltpu.VMEM((spans, span_len, chips * HD), bf16), row_out, row_out),
        in_specs=[ANY, HBM] + [VMEM] * 3,
        out_specs=(ANY,) * 3,
        scratch_shapes=[
            pltpu.SMEM(ih.shape, jnp.int32),
            pltpu.VMEM(ka.shape, bf16),
            pltpu.VMEM((chips, spans, span_len, HD), bf16),
            pltpu.VMEM((4, 2) + piece, bf16),
            pltpu.VMEM((4, 2) + piece, bf16),
            pltpu.VMEM((2,) + piece, bf16),
            pltpu.VMEM((2, 2) + piece, bf16),
            dma((chips,)), dma((chips,)), dma((2, 2, chips)), dma((2, 2, chips)),
            dma((4, 2, nz, 2)), dma((4, 2, nz, 2)), dma((2, nz, 2)), dma((2, nz, 2)),
            dma((2, 2, nz, 2)), dma((2, 2, nz, 2)), dma, dma((2, 2)), dma, dma,
        ],
        compiler_params=pltpu.CompilerParams(
            collective_id=1, has_side_effects=True, vmem_limit_bytes=32 * MiB
        ),
    )(ih, *in_hbm(ka), *in_vmem(dscore, split(dk), split(dv)))


def write_kernel(*refs):
    count = (len(refs) - 1) // 2
    copies = [
        pltpu.make_async_copy(refs[i], refs[count + i], refs[-1].at[i]) for i in range(count)
    ]
    for copy in copies:
        copy.start()
    for copy in copies:
        copy.wait()


def write(*arrays):
    return pl.pallas_call(
        write_kernel,
        name="write",
        out_shape=tuple(pltpu.HBM(a.shape, a.dtype) for a in arrays),
        in_specs=[VMEM] * len(arrays),
        out_specs=(HBM,) * len(arrays),
        scratch_shapes=[pltpu.SemaphoreType.DMA((len(arrays),))],
        compiler_params=pltpu.CompilerParams(vmem_limit_bytes=8 * MiB),
    )(*in_vmem(*arrays))


def on_device(nz, nx, query, grad_out, keys, values, owner_list, row_list):
    qh, gh, va, ih, lifted, inverse, ka = bring(
        nz, nx, query, grad_out, keys, values, owner_list, row_list
    )
    dscore, dk, dv = attend(ih, qh, gh, va, lifted, inverse)
    return write(*give(nz, nx, query.shape[0], ih, ka, dscore, dk, dv))


def solution(mesh):
    groups, retr = mesh.devices.shape
    nx = 4 if retr == 32 else 2
    nz = retr // (2 * nx)
    fine = Mesh(mesh.devices.reshape(groups, nz, nx, 2), ("y", "z", "x", "c"))
    all_axes = ("y", "z", "x", "c")
    owner = ("z", "x", "c")
    return jax.shard_map(
        functools.partial(on_device, nz, nx),
        mesh=fine,
        in_specs=(
            P(all_axes, None, None),
            P(all_axes, None, None),
            P(owner, None, None),
            P(owner, None, None),
            P(all_axes, None),
            P(all_axes, None),
        ),
        out_specs=(P(all_axes, None, None), P(owner, "y", None), P(owner, "y", None)),
        check_vma=False,
    )
```

```python
import functools

import jax
import jax.numpy as jnp
import numpy as np
from jax import lax
from jax.experimental import pallas as pl
from jax.experimental.pallas import tpu as pltpu
from jax.sharding import Mesh
from jax.sharding import PartitionSpec as P

HD = 128
MiB = 1024 * 1024
ANY = pl.BlockSpec(memory_space=pl.ANY)
VMEM = pl.BlockSpec(memory_space=pltpu.VMEM)
SMEM = pl.BlockSpec(memory_space=pltpu.SMEM)
HBM = pl.BlockSpec(memory_space=pltpu.HBM)


def in_hbm(*arrays):
    return tuple(pltpu.with_memory_space_constraint(a, pltpu.HBM) for a in arrays)


def in_vmem(*arrays):
    return tuple(pltpu.with_memory_space_constraint(a, pltpu.VMEM) for a in arrays)


def place():
    return tuple(lax.axis_index(name) for name in ("y", "z", "x", "c"))


def remote(src, dst, send, recv, where):
    return pltpu.make_async_remote_copy(
        src_ref=src,
        dst_ref=dst,
        send_sem=send,
        recv_sem=recv,
        device_id=where,
        device_id_type=pl.DeviceIdType.MESH,
    )


def greet(nz, nx):
    y, z, x, c = place()
    barrier = pltpu.get_barrier_semaphore()

    def hello(where):
        pl.semaphore_signal(barrier, inc=1, device_id=where, device_id_type=pl.DeviceIdType.MESH)

    @pl.loop(1, nz * nx)
    def _(d):
        hello((y, lax.rem(z + d // nx, nz), lax.rem(x + lax.rem(d, nx), nx), c))

    hello((lax.rem(y + 1, 4), z, x, c))
    hello((lax.rem(y + 3, 4), z, x, c))
    hello((y, z, x, 1 - c))
    pl.semaphore_wait(barrier, nz * nx - 1 + 3)


def contract(a, b, da, db):
    return lax.dot_general(a, b, (((da,), (db,)), ((), ())), preferred_element_type=jnp.float32)


def diagonal(a, b):
    empty = jnp.zeros_like(a)
    return jnp.concatenate(
        [jnp.concatenate([a, empty], axis=1), jnp.concatenate([empty, b], axis=1)], axis=0
    )


def entries_of(i_ref, pair, per):
    return [
        i_ref[s // per, n, lax.rem(s, per)] for s in (2 * pair, 2 * pair + 1) for n in (0, 1)
    ]


def rows_of(ref, entries):
    quarters, _, tok, _ = ref.shape
    taken = [ref[:, e].reshape(quarters * tok, HD) for e in entries]
    return jnp.concatenate(
        [jnp.concatenate(taken[:2], axis=0), jnp.concatenate(taken[2:], axis=0)], axis=1
    )


def tokens_of(ref, pair):
    per = ref.shape[1]
    sa, sb = 2 * pair, 2 * pair + 1
    return diagonal(ref[sa // per, lax.rem(sa, per)], ref[sb // per, lax.rem(sb, per)])


def offsets(nz, nx):
    steps = [(dz, dx) for dz in range(nz) for dx in range(nx) if dz or dx]

    def hops(step):
        return min(step[0], nz - step[0]) + min(step[1], nx - step[1])

    return sorted(steps, key=hops)


def bring_kernel(
    nz, nx,
    q_ref, g_ref, k_ref, v_ref, owner_ref, row_ref,
    qh, gh, va, ih, lifted_ref, inverse_ref, ka_hbm,
    ka, i_ref, i_smem, o_vmem, w_vmem, s_in, r_in, s_y, r_y, s_c, r_c, own,
):
    y, z, x, c = place()
    chips = nz * nx
    rows = k_ref.shape[0]
    part = chips * rows
    quarter = k_ref.shape[1] // 4
    me = z * nx + x
    up, down, far = lax.rem(y + 1, 4), lax.rem(y + 3, 4), lax.rem(y + 2, 4)
    lists = (
        pltpu.make_async_copy(owner_ref, o_vmem, own.at[7]),
        pltpu.make_async_copy(row_ref, w_vmem, own.at[8]),
    )
    for copy in lists:
        copy.start()
    greet(nz, nx)
    for copy in lists:
        copy.wait()

    owners = o_vmem[...]
    entries = (owners & 1) * part + (owners >> 1) * rows + w_vmem[...]
    i_ref[...] = jnp.zeros_like(i_ref)
    i_ref[: entries.shape[0], : entries.shape[1]] = entries

    def columns(head):
        return pl.ds(pl.multiple_of(head * HD, HD), HD)

    def token_part(ref, head):
        return ref.at[:, pl.ds(pl.multiple_of(y * quarter, quarter), quarter), columns(head)]

    def landing(ref):
        return ref.at[y, pl.ds(c * part + me * rows, rows)]

    def sides(t, head):
        if t < 2:
            return token_part((k_ref, v_ref)[t], head), landing((ka, va)[t])
        if t < 4:
            return (q_ref, g_ref)[t - 2].at[:, :, columns(head)], (qh, gh)[t - 2].at[me]
        return i_ref, ih.at[me]

    def to_chip(t, d):
        pz, px = lax.rem(z + d // nx, nz), lax.rem(x + lax.rem(d, nx), nx)
        return remote(*sides(t, pz * nx + px), s_in.at[t, d], r_in.at[t, d], (y, pz, px, c))

    def keep(t):
        return pltpu.make_async_copy(*sides(t, me), own.at[t])

    def arrived(t):
        @pl.loop(1, chips)
        def _(d):
            to_chip(t, d).wait_recv()

        keep(t).wait()

    def send(t):
        for dz, dx in offsets(nz, nx):
            to_chip(t, dz * nx + dx).start()
        keep(t).start()

    for t in (0, 1, 4, 2):
        send(t)

    def chunk(t, at):
        return (ka, va)[t].at[at, pl.ds(c * part, part)]

    def along_y(t, at, slot, where):
        return remote(
            chunk(t, at), chunk(t, at), s_y.at[t, slot], r_y.at[t, slot], (where, z, x, c)
        )

    def across(t, at, slot):
        return remote(
            chunk(t, at), chunk(t, at), s_c.at[t, slot], r_c.at[t, slot], (y, z, x, 1 - c)
        )

    arrived(0)
    along_y(0, y, 0, up).start()
    along_y(0, y, 1, down).start()
    across(0, y, 0).start()
    arrived(1)
    along_y(1, y, 1, down).start()
    across(1, y, 0).start()
    send(3)

    def all_across(t):
        along_y(t, far, 2, up).wait_recv()
        across(t, far, 3).start()
        for slot in range(4):
            across(t, y, slot).wait_recv()

    arrived(4)
    entry_copy = pltpu.make_async_copy(ih, i_smem, own.at[5])
    entry_copy.start()
    entry_copy.wait()
    along_y(0, down, 0, up).wait_recv()
    along_y(0, down, 2, up).start()
    along_y(1, y, 0, up).start()
    across(0, down, 1).start()
    along_y(0, up, 1, down).wait_recv()
    across(0, up, 2).start()
    along_y(1, up, 1, down).wait_recv()
    along_y(1, up, 2, down).start()
    across(1, up, 2).start()
    all_across(0)
    keep_keys = pltpu.make_async_copy(ka, ka_hbm, own.at[6])
    keep_keys.start()
    arrived(2)

    to_base2 = HD ** -0.5 * float(np.log2(np.e))
    pairs = lifted_ref.shape[0]
    unroll = min(4, pairs)

    def weigh(first, last):
        @pl.loop(first, last)
        def _(step):
            for u in range(unroll):
                p = step * unroll + u
                scores = contract(rows_of(ka, entries_of(i_smem, p, qh.shape[1])), tokens_of(qh, p), 1, 1)
                lifted = jnp.exp2((scores - jnp.max(scores, axis=0, keepdims=True)) * to_base2)
                inverse_ref[p] = 1.0 / jnp.sum(lifted, axis=0, keepdims=True)
                lifted_ref[p] = lifted.astype(jnp.bfloat16)

    steps = pairs // unroll
    weigh(0, steps // 2)
    along_y(1, down, 0, up).wait_recv()
    across(1, down, 1).start()
    weigh(steps // 2, steps)
    all_across(1)
    arrived(3)
    keep_keys.wait()
    for t in range(5):

        @pl.loop(1, chips)
        def _(d):
            to_chip(t, d).wait_send()

    for t in (0, 1):
        for slot in range(3):
            along_y(t, y, slot, up).wait_send()
        for slot in range(4):
            across(t, y, slot).wait_send()


def bring(nz, nx, query, grad_out, keys, values, owner_list, row_list):
    chips = nz * nx
    rows, tokens, _ = keys.shape
    spans, span_len, _ = query.shape
    bf16 = jnp.bfloat16
    held = pltpu.VMEM((4, 2 * chips * rows, tokens // 4, HD), bf16)
    heads = pltpu.VMEM((chips, spans, span_len, HD), bf16)
    pairs = chips * spans // 2
    listed = (8, HD)
    dma = pltpu.SemaphoreType.DMA
    return pl.pallas_call(
        functools.partial(bring_kernel, nz, nx),
        name="bring",
        out_shape=(
            heads, heads, held,
            jax.ShapeDtypeStruct((chips,) + listed, jnp.int32),
            pltpu.VMEM((pairs, 2 * tokens, 2 * span_len), bf16),
            pltpu.VMEM((pairs, 1, 2 * span_len), jnp.float32),
            pltpu.HBM(held.shape, bf16),
        ),
        in_specs=[HBM] * 6,
        out_specs=(VMEM,) * 3 + (ANY,) + (VMEM,) * 2 + (HBM,),
        scratch_shapes=[
            pltpu.VMEM(held.shape, bf16),
            pltpu.VMEM(listed, jnp.int32),
            pltpu.SMEM((chips,) + listed, jnp.int32),
            pltpu.VMEM((2, spans), jnp.int32),
            pltpu.VMEM((2, spans), jnp.int32),
            dma((5, chips)), dma((5, chips)), dma((2, 3)), dma((2, 3)), dma((2, 4)), dma((2, 4)), dma((9,)),
        ],
        compiler_params=pltpu.CompilerParams(
            collective_id=0, has_side_effects=True, vmem_limit_bytes=14 * MiB
        ),
    )(*in_hbm(query, grad_out, keys, values, owner_list.T, row_list.T))


def attend_kernel(
    i_hbm, qh, gh, va, lifted_ref, inverse_ref, dscore_ref, dk_low, dv_low, dk, dv, i_ref, sem
):
    quarters, rows, tok, _ = va.shape
    tokens = quarters * tok
    scaling = HD ** -0.5
    pairs = lifted_ref.shape[0]
    unroll = min(8, pairs)

    def add(sums, entries, terms):
        for at, e in enumerate(entries):
            rs = slice(at % 2 * tokens, (at % 2 + 1) * tokens)
            cs = slice(at // 2 * HD, (at // 2 + 1) * HD)
            sums[:, e] += terms[rs, cs].reshape(quarters, tok, HD)

    def gradients(p):
        entries = entries_of(i_ref, p, qh.shape[1])
        grads = tokens_of(gh, p)
        dprob = contract(rows_of(va, entries), grads, 1, 1)
        inverse = inverse_ref[p]
        lifted = lifted_ref[p].astype(jnp.float32)
        delta = jnp.sum(lifted * dprob, axis=0, keepdims=True) * inverse
        chance_low = (lifted * inverse).astype(jnp.bfloat16)
        dscore = (lifted * (inverse * scaling) * (dprob - delta)).astype(jnp.bfloat16)
        dscore_ref[p] = dscore
        return entries, contract(chance_low, grads, 1, 0)

    lists = pltpu.make_async_copy(i_hbm, i_ref, sem)
    lists.start()

    @pl.loop(0, rows)
    def _(r):
        dk[:, r] = jnp.zeros((quarters, tok, HD), jnp.float32)
        dv[:, r] = jnp.zeros((quarters, tok, HD), jnp.float32)

    lists.wait()

    @pl.loop(0, pairs // unroll)
    def _(step):
        results = [gradients(step * unroll + u) for u in range(unroll)]
        for entries, value_terms in results:
            add(dv, entries, value_terms)

    @pl.loop(0, pairs // unroll)
    def _(step):
        results = []
        for u in range(unroll):
            p = step * unroll + u
            results.append(
                (entries_of(i_ref, p, qh.shape[1]), contract(dscore_ref[p], tokens_of(qh, p), 1, 0))
            )
        for entries, key_terms in results:
            add(dk, entries, key_terms)

    @pl.loop(0, rows // 4)
    def _(r):
        for u in range(4):
            dk_low[:, 4 * r + u] = dk[:, 4 * r + u].astype(jnp.bfloat16)
        for u in range(4):
            dv_low[:, 4 * r + u] = dv[:, 4 * r + u].astype(jnp.bfloat16)


def attend(ih, qh, gh, va, lifted, inverse):
    held = pltpu.VMEM(va.shape, jnp.bfloat16)
    work = lifted.size * HD * 2
    return pl.pallas_call(
        attend_kernel,
        name="attend",
        out_shape=(pltpu.VMEM(lifted.shape, jnp.bfloat16), held, held),
        in_specs=[ANY] + [VMEM] * 5,
        out_specs=(VMEM,) * 3,
        scratch_shapes=[
            pltpu.VMEM(va.shape, jnp.float32),
            pltpu.VMEM(va.shape, jnp.float32),
            pltpu.SMEM(ih.shape, jnp.int32),
            pltpu.SemaphoreType.DMA,
        ],
        input_output_aliases={4: 0, 3: 2},
        compiler_params=pltpu.CompilerParams(vmem_limit_bytes=28 * MiB),
        cost_estimate=pl.CostEstimate(flops=3 * work, bytes_accessed=4 * MiB, transcendentals=0),
    )(ih, *in_vmem(qh, gh, va, lifted, inverse))


def give_kernel(
    nz, nx,
    i_hbm, ka_hbm, dscore_ref, dk_ref, dv_ref,
    gq, gk, gv,
    i_ref, ka, dq_ref, other, total, passed, arrived,
    s_q, r_q, s_out, r_out, s_c, r_c, s_f, r_f, s_y, r_y, own_q, own_out, own_k, own_i,
):
    y, z, x, c = place()
    chips = nz * nx
    rows = gk.shape[0]
    half = rows // 2
    me = z * nx + x
    up, down, far = lax.rem(y + 1, 4), lax.rem(y + 3, 4), lax.rem(y + 2, 4)
    pair = (dk_ref, dv_ref)
    outs = (gk, gv)
    greet(nz, nx)

    at = (far, up, down, y)
    bands = [(dz, h) for dz in sorted(range(nz), key=lambda dz: -min(dz, nz - dz)) for h in (0, 1)]

    def rows_at(t, slot, dz, h, core):
        first = core * chips + lax.rem(z + dz, nz) * nx
        return pair[t].at[at[slot], pl.ds(first, nx), pl.ds(h * half, half)]

    def across(t, slot, dz, h):
        return remote(
            rows_at(t, slot, dz, h, 1 - c), other.at[slot, t, dz, h],
            s_c.at[slot, t, dz, h], r_c.at[slot, t, dz, h], (y, z, x, 1 - c),
        )

    for dz, h in bands:
        for slot in range(4):
            for t in (0, 1):
                across(t, slot, dz, h).start()

    def columns(head):
        return pl.ds(pl.multiple_of(head * HD, HD), HD)

    def chip(d):
        pz, px = lax.rem(z + d // nx, nz), lax.rem(x + lax.rem(d, nx), nx)
        return pz * nx + px, (y, pz, px, c)

    def query_out(d):
        head, where = chip(d)
        return remote(dq_ref.at[head], gq.at[:, :, columns(me)], s_q.at[d], r_q.at[d], where)

    def key_out(d, t, h):
        _, where = chip(d)
        px = lax.rem(x + lax.rem(d, nx), nx)
        return remote(
            total.at[3, t, d // nx, h, px], outs[t].at[pl.ds(h * half, half), :, columns(me)],
            s_out.at[t, h, d], r_out.at[t, h, d], where,
        )

    def key_own(t, h):
        return pltpu.make_async_copy(
            total.at[3, t, 0, h, x], outs[t].at[pl.ds(h * half, half), :, columns(me)],
            own_out.at[t, h],
        )

    query_own = pltpu.make_async_copy(dq_ref.at[me], gq.at[:, :, columns(me)], own_q)
    keys_in = pltpu.make_async_copy(ka_hbm, ka, own_k)
    keys_in.start()
    lists = pltpu.make_async_copy(i_hbm, i_ref, own_i)
    lists.start()
    pairs = dscore_ref.shape[0]
    per = dq_ref.shape[1]
    span_len = dq_ref.shape[2]
    unroll = min(4, pairs)

    def queries():
        keys_in.wait()
        lists.wait()

        @pl.loop(0, pairs // unroll)
        def _(step):
            for u in range(unroll):
                p = step * unroll + u
                both = contract(dscore_ref[p], rows_of(ka, entries_of(i_ref, p, per)), 0, 0)
                sa, sb = 2 * p, 2 * p + 1
                dq_ref[sa // per, lax.rem(sa, per)] = both[:span_len, :HD].astype(jnp.bfloat16)
                dq_ref[sb // per, lax.rem(sb, per)] = both[span_len:, HD:].astype(jnp.bfloat16)

        query_own.start()
        for dz, dx in offsets(nz, nx):
            query_out(dz * nx + dx).start()

    def f32(a):
        return a.astype(jnp.float32)

    def add(dst, *terms):
        @pl.loop(0, nx)
        def _(i):
            sums = f32(terms[0][i])
            for term in terms[1:]:
                sums = sums + f32(term[i])
            dst[i] = sums.astype(jnp.bfloat16)

    def both_cores(t, slot, dz, h):
        across(t, slot, dz, h).wait_recv()
        return rows_at(t, slot, dz, h, c), other.at[slot, t, dz, h]

    def far_copy(t, dz, h):
        return remote(
            total.at[0, t, dz, h], passed.at[t, dz, h], s_f.at[t, dz, h], r_f.at[t, dz, h],
            ((up, down)[t], z, x, c),
        )

    def near_copy(t, slot, dz, h):
        return remote(
            total.at[slot, t, dz, h], arrived.at[slot - 1, t, dz, h],
            s_y.at[slot - 1, t, dz, h], r_y.at[slot - 1, t, dz, h],
            ((up, down)[slot - 1], z, x, c),
        )

    def direct(dz, h):
        for t in (0, 1):
            add(total.at[0, t, dz, h], *both_cores(t, 0, dz, h))
            far_copy(t, dz, h).start()
        for t, slot in ((1, 1), (0, 2)):
            add(total.at[slot, t, dz, h], *both_cores(t, slot, dz, h))
            near_copy(t, slot, dz, h).start()

    def merged(dz, h):
        for t, slot in ((0, 1), (1, 2)):
            terms = both_cores(t, slot, dz, h)
            far_copy(t, dz, h).wait_recv()
            add(total.at[slot, t, dz, h], *terms, passed.at[t, dz, h])
            near_copy(t, slot, dz, h).start()

    def final(dz, h):
        for t in (0, 1):
            terms = both_cores(t, 3, dz, h)
            near_copy(t, 1, dz, h).wait_recv()
            near_copy(t, 2, dz, h).wait_recv()
            add(total.at[3, t, dz, h], *terms, arrived.at[0, t, dz, h], arrived.at[1, t, dz, h])
            for dx in range(nx):
                if dz or dx:
                    key_out(dz * nx + dx, t, h).start()
                else:
                    key_own(t, h).start()

    lag = 2
    for step in range(len(bands) + 2 * lag):
        if step < len(bands):
            direct(*bands[step])
        if step == 2:
            queries()
        if lag <= step < len(bands) + lag:
            merged(*bands[step - lag])
        if step >= 2 * lag:
            final(*bands[step - 2 * lag])

    @pl.loop(1, chips)
    def _(d):
        query_out(d).wait()
        for t in (0, 1):
            for h in (0, 1):
                key_out(d, t, h).wait()

    query_own.wait()
    for t in (0, 1):
        for h in (0, 1):
            key_own(t, h).wait()

            @pl.loop(0, nz)
            def _(dz):
                far_copy(t, dz, h).wait_send()
                for slot in range(4):
                    across(t, slot, dz, h).wait_send()
                for slot in (1, 2):
                    near_copy(t, slot, dz, h).wait_send()


def give(nz, nx, spans, ih, ka, dscore, dk, dv):
    chips = nz * nx
    _, all_rows, tok, _ = dk.shape
    part = all_rows // 2
    rows = part // chips
    piece = (nz, 2, nx, rows // 2, tok, HD)
    span_len = dscore.shape[2] // 2
    bf16 = jnp.bfloat16
    dma = pltpu.SemaphoreType.DMA
    def split(sums):
        return sums.reshape(4, 2 * chips, rows, tok, HD)

    row_out = pltpu.VMEM((part // chips, tok, chips * HD), bf16)
    return pl.pallas_call(
        functools.partial(give_kernel, nz, nx),
        name="give",
        out_shape=(pltpu.VMEM((spans, span_len, chips * HD), bf16), row_out, row_out),
        in_specs=[ANY, HBM] + [VMEM] * 3,
        out_specs=(ANY,) * 3,
        scratch_shapes=[
            pltpu.SMEM(ih.shape, jnp.int32),
            pltpu.VMEM(ka.shape, bf16),
            pltpu.VMEM((chips, spans, span_len, HD), bf16),
            pltpu.VMEM((4, 2) + piece, bf16),
            pltpu.VMEM((4, 2) + piece, bf16),
            pltpu.VMEM((2,) + piece, bf16),
            pltpu.VMEM((2, 2) + piece, bf16),
            dma((chips,)), dma((chips,)), dma((2, 2, chips)), dma((2, 2, chips)),
            dma((4, 2, nz, 2)), dma((4, 2, nz, 2)), dma((2, nz, 2)), dma((2, nz, 2)),
            dma((2, 2, nz, 2)), dma((2, 2, nz, 2)), dma, dma((2, 2)), dma, dma,
        ],
        compiler_params=pltpu.CompilerParams(
            collective_id=1, has_side_effects=True, vmem_limit_bytes=32 * MiB
        ),
    )(ih, *in_hbm(ka), *in_vmem(dscore, split(dk), split(dv)))


def write_kernel(*refs):
    count = (len(refs) - 1) // 2
    copies = [
        pltpu.make_async_copy(refs[i], refs[count + i], refs[-1].at[i]) for i in range(count)
    ]
    for copy in copies:
        copy.start()
    for copy in copies:
        copy.wait()


def write(*arrays):
    return pl.pallas_call(
        write_kernel,
        name="write",
        out_shape=tuple(pltpu.HBM(a.shape, a.dtype) for a in arrays),
        in_specs=[VMEM] * len(arrays),
        out_specs=(HBM,) * len(arrays),
        scratch_shapes=[pltpu.SemaphoreType.DMA((len(arrays),))],
        compiler_params=pltpu.CompilerParams(vmem_limit_bytes=8 * MiB),
    )(*in_vmem(*arrays))


def on_device(nz, nx, query, grad_out, keys, values, owner_list, row_list):
    qh, gh, va, ih, lifted, inverse, ka = bring(
        nz, nx, query, grad_out, keys, values, owner_list, row_list
    )
    dscore, dk, dv = attend(ih, qh, gh, va, lifted, inverse)
    return write(*give(nz, nx, query.shape[0], ih, ka, dscore, dk, dv))


def solution(mesh):
    groups, retr = mesh.devices.shape
    nx = 4 if retr == 32 else 2
    nz = retr // (2 * nx)
    fine = Mesh(mesh.devices.reshape(groups, nz, nx, 2), ("y", "z", "x", "c"))
    all_axes = ("y", "z", "x", "c")
    owner = ("z", "x", "c")
    return jax.shard_map(
        functools.partial(on_device, nz, nx),
        mesh=fine,
        in_specs=(
            P(all_axes, None, None),
            P(all_axes, None, None),
            P(owner, None, None),
            P(owner, None, None),
            P(all_axes, None),
            P(all_axes, None),
        ),
        out_specs=(P(all_axes, None, None), P(owner, "y", None), P(owner, "y", None)),
        check_vma=False,
    )
```

```python
import functools

import jax
import jax.numpy as jnp
import numpy as np
from jax import lax
from jax.experimental import pallas as pl
from jax.experimental.pallas import tpu as pltpu
from jax.sharding import Mesh
from jax.sharding import PartitionSpec as P

HD = 128
MiB = 1024 * 1024
ANY = pl.BlockSpec(memory_space=pl.ANY)
VMEM = pl.BlockSpec(memory_space=pltpu.VMEM)
SMEM = pl.BlockSpec(memory_space=pltpu.SMEM)
HBM = pl.BlockSpec(memory_space=pltpu.HBM)


def in_hbm(*arrays):
    return tuple(pltpu.with_memory_space_constraint(a, pltpu.HBM) for a in arrays)


def in_vmem(*arrays):
    return tuple(pltpu.with_memory_space_constraint(a, pltpu.VMEM) for a in arrays)


def place():
    return tuple(lax.axis_index(name) for name in ("y", "z", "x", "c"))


def remote(src, dst, send, recv, where):
    return pltpu.make_async_remote_copy(
        src_ref=src,
        dst_ref=dst,
        send_sem=send,
        recv_sem=recv,
        device_id=where,
        device_id_type=pl.DeviceIdType.MESH,
    )


def greet(nz, nx):
    y, z, x, c = place()
    barrier = pltpu.get_barrier_semaphore()

    def hello(where):
        pl.semaphore_signal(barrier, inc=1, device_id=where, device_id_type=pl.DeviceIdType.MESH)

    @pl.loop(1, nz * nx)
    def _(d):
        hello((y, lax.rem(z + d // nx, nz), lax.rem(x + lax.rem(d, nx), nx), c))

    hello((lax.rem(y + 1, 4), z, x, c))
    hello((lax.rem(y + 3, 4), z, x, c))
    hello((y, z, x, 1 - c))
    pl.semaphore_wait(barrier, nz * nx - 1 + 3)


def contract(a, b, da, db):
    return lax.dot_general(a, b, (((da,), (db,)), ((), ())), preferred_element_type=jnp.float32)


def diagonal(a, b):
    empty = jnp.zeros_like(a)
    return jnp.concatenate(
        [jnp.concatenate([a, empty], axis=1), jnp.concatenate([empty, b], axis=1)], axis=0
    )


def entries_of(i_ref, pair, per):
    return [
        i_ref[s // per, n, lax.rem(s, per)] for s in (2 * pair, 2 * pair + 1) for n in (0, 1)
    ]


def rows_of(ref, entries):
    quarters, _, tok, _ = ref.shape
    taken = [ref[:, e].reshape(quarters * tok, HD) for e in entries]
    return jnp.concatenate(
        [jnp.concatenate(taken[:2], axis=0), jnp.concatenate(taken[2:], axis=0)], axis=1
    )


def tokens_of(ref, pair):
    per = ref.shape[1]
    sa, sb = 2 * pair, 2 * pair + 1
    return diagonal(ref[sa // per, lax.rem(sa, per)], ref[sb // per, lax.rem(sb, per)])


def offsets(nz, nx):
    steps = [(dz, dx) for dz in range(nz) for dx in range(nx) if dz or dx]

    def hops(step):
        return min(step[0], nz - step[0]) + min(step[1], nx - step[1])

    return sorted(steps, key=hops)


def bring_kernel(
    nz, nx,
    q_ref, g_ref, k_ref, v_ref, owner_ref, row_ref,
    qh, gh, va, ih, lifted_ref, inverse_ref, ka_hbm,
    ka, i_ref, i_smem, o_vmem, w_vmem, s_in, r_in, s_y, r_y, s_c, r_c, own,
):
    y, z, x, c = place()
    chips = nz * nx
    rows = k_ref.shape[0]
    part = chips * rows
    quarter = k_ref.shape[1] // 4
    me = z * nx + x
    up, down, far = lax.rem(y + 1, 4), lax.rem(y + 3, 4), lax.rem(y + 2, 4)
    lists = (
        pltpu.make_async_copy(owner_ref, o_vmem, own.at[7]),
        pltpu.make_async_copy(row_ref, w_vmem, own.at[8]),
    )
    for copy in lists:
        copy.start()
    greet(nz, nx)
    for copy in lists:
        copy.wait()

    owners = o_vmem[...]
    entries = (owners & 1) * part + (owners >> 1) * rows + w_vmem[...]
    i_ref[...] = jnp.zeros_like(i_ref)
    i_ref[: entries.shape[0], : entries.shape[1]] = entries

    def columns(head):
        return pl.ds(pl.multiple_of(head * HD, HD), HD)

    def token_part(ref, head):
        return ref.at[:, pl.ds(pl.multiple_of(y * quarter, quarter), quarter), columns(head)]

    def landing(ref):
        return ref.at[y, pl.ds(c * part + me * rows, rows)]

    def sides(t, head):
        if t < 2:
            return token_part((k_ref, v_ref)[t], head), landing((ka, va)[t])
        if t < 4:
            return (q_ref, g_ref)[t - 2].at[:, :, columns(head)], (qh, gh)[t - 2].at[me]
        return i_ref, ih.at[me]

    def to_chip(t, d):
        pz, px = lax.rem(z + d // nx, nz), lax.rem(x + lax.rem(d, nx), nx)
        return remote(*sides(t, pz * nx + px), s_in.at[t, d], r_in.at[t, d], (y, pz, px, c))

    def keep(t):
        return pltpu.make_async_copy(*sides(t, me), own.at[t])

    def arrived(t):
        @pl.loop(1, chips)
        def _(d):
            to_chip(t, d).wait_recv()

        keep(t).wait()

    def send(t):
        for dz, dx in offsets(nz, nx):
            to_chip(t, dz * nx + dx).start()
        keep(t).start()

    for t in (0, 1, 4, 2):
        send(t)

    def chunk(t, at):
        return (ka, va)[t].at[at, pl.ds(c * part, part)]

    def along_y(t, at, slot, where):
        return remote(
            chunk(t, at), chunk(t, at), s_y.at[t, slot], r_y.at[t, slot], (where, z, x, c)
        )

    def across(t, at, slot):
        return remote(
            chunk(t, at), chunk(t, at), s_c.at[t, slot], r_c.at[t, slot], (y, z, x, 1 - c)
        )

    arrived(0)
    along_y(0, y, 0, up).start()
    along_y(0, y, 1, down).start()
    across(0, y, 0).start()
    arrived(1)
    along_y(1, y, 1, down).start()
    across(1, y, 0).start()
    send(3)

    def all_across(t):
        along_y(t, far, 2, up).wait_recv()
        across(t, far, 3).start()
        for slot in range(4):
            across(t, y, slot).wait_recv()

    arrived(4)
    entry_copy = pltpu.make_async_copy(ih, i_smem, own.at[5])
    entry_copy.start()
    entry_copy.wait()
    along_y(0, down, 0, up).wait_recv()
    along_y(0, down, 2, up).start()
    along_y(1, y, 0, up).start()
    across(0, down, 1).start()
    along_y(0, up, 1, down).wait_recv()
    across(0, up, 2).start()
    along_y(1, up, 1, down).wait_recv()
    along_y(1, up, 2, down).start()
    across(1, up, 2).start()
    all_across(0)
    keep_keys = pltpu.make_async_copy(ka, ka_hbm, own.at[6])
    keep_keys.start()
    arrived(2)

    to_base2 = HD ** -0.5 * float(np.log2(np.e))
    pairs = lifted_ref.shape[0]
    unroll = min(4, pairs)

    def weigh(first, last):
        @pl.loop(first, last)
        def _(step):
            for u in range(unroll):
                p = step * unroll + u
                scores = contract(rows_of(ka, entries_of(i_smem, p, qh.shape[1])), tokens_of(qh, p), 1, 1)
                lifted = jnp.exp2((scores - jnp.max(scores, axis=0, keepdims=True)) * to_base2)
                inverse_ref[p] = 1.0 / jnp.sum(lifted, axis=0, keepdims=True)
                lifted_ref[p] = lifted.astype(jnp.bfloat16)

    steps = pairs // unroll
    weigh(0, steps // 2)
    along_y(1, down, 0, up).wait_recv()
    across(1, down, 1).start()
    weigh(steps // 2, steps)
    all_across(1)
    arrived(3)
    keep_keys.wait()
    for t in range(5):

        @pl.loop(1, chips)
        def _(d):
            to_chip(t, d).wait_send()

    for t in (0, 1):
        for slot in range(3):
            along_y(t, y, slot, up).wait_send()
        for slot in range(4):
            across(t, y, slot).wait_send()


def bring(nz, nx, query, grad_out, keys, values, owner_list, row_list):
    chips = nz * nx
    rows, tokens, _ = keys.shape
    spans, span_len, _ = query.shape
    bf16 = jnp.bfloat16
    held = pltpu.VMEM((4, 2 * chips * rows, tokens // 4, HD), bf16)
    heads = pltpu.VMEM((chips, spans, span_len, HD), bf16)
    pairs = chips * spans // 2
    listed = (8, HD)
    dma = pltpu.SemaphoreType.DMA
    return pl.pallas_call(
        functools.partial(bring_kernel, nz, nx),
        name="bring",
        out_shape=(
            heads, heads, held,
            jax.ShapeDtypeStruct((chips,) + listed, jnp.int32),
            pltpu.VMEM((pairs, 2 * tokens, 2 * span_len), bf16),
            pltpu.VMEM((pairs, 1, 2 * span_len), jnp.float32),
            pltpu.HBM(held.shape, bf16),
        ),
        in_specs=[HBM] * 6,
        out_specs=(VMEM,) * 3 + (ANY,) + (VMEM,) * 2 + (HBM,),
        scratch_shapes=[
            pltpu.VMEM(held.shape, bf16),
            pltpu.VMEM(listed, jnp.int32),
            pltpu.SMEM((chips,) + listed, jnp.int32),
            pltpu.VMEM((2, spans), jnp.int32),
            pltpu.VMEM((2, spans), jnp.int32),
            dma((5, chips)), dma((5, chips)), dma((2, 3)), dma((2, 3)), dma((2, 4)), dma((2, 4)), dma((9,)),
        ],
        compiler_params=pltpu.CompilerParams(
            collective_id=0, has_side_effects=True, vmem_limit_bytes=14 * MiB
        ),
    )(*in_hbm(query, grad_out, keys, values, owner_list.T, row_list.T))


def attend_kernel(
    i_hbm, qh, gh, va, lifted_ref, inverse_ref, dscore_ref, dk_low, dv_low, dk, dv, i_ref, sem
):
    quarters, rows, tok, _ = va.shape
    tokens = quarters * tok
    scaling = HD ** -0.5
    pairs = lifted_ref.shape[0]
    unroll = min(8, pairs)

    def add(sums, entries, terms):
        for at, e in enumerate(entries):
            rs = slice(at % 2 * tokens, (at % 2 + 1) * tokens)
            cs = slice(at // 2 * HD, (at // 2 + 1) * HD)
            sums[:, e] += terms[rs, cs].reshape(quarters, tok, HD)

    def gradients(p):
        entries = entries_of(i_ref, p, qh.shape[1])
        grads = tokens_of(gh, p)
        dprob = contract(rows_of(va, entries), grads, 1, 1)
        inverse = inverse_ref[p]
        lifted = lifted_ref[p].astype(jnp.float32)
        delta = jnp.sum(lifted * dprob, axis=0, keepdims=True) * inverse
        chance_low = (lifted * inverse).astype(jnp.bfloat16)
        dscore = (lifted * (inverse * scaling) * (dprob - delta)).astype(jnp.bfloat16)
        dscore_ref[p] = dscore
        return entries, contract(chance_low, grads, 1, 0)

    lists = pltpu.make_async_copy(i_hbm, i_ref, sem)
    lists.start()

    @pl.loop(0, rows // 4)
    def _(r):
        dk[:, pl.ds(4 * r, 4)] = jnp.zeros((quarters, 4, tok, HD), jnp.float32)
        dv[:, pl.ds(4 * r, 4)] = jnp.zeros((quarters, 4, tok, HD), jnp.float32)

    lists.wait()

    @pl.loop(0, pairs // unroll)
    def _(step):
        results = [gradients(step * unroll + u) for u in range(unroll)]
        for entries, value_terms in results:
            add(dv, entries, value_terms)

    @pl.loop(0, pairs // unroll)
    def _(step):
        results = []
        for u in range(unroll):
            p = step * unroll + u
            results.append(
                (entries_of(i_ref, p, qh.shape[1]), contract(dscore_ref[p], tokens_of(qh, p), 1, 0))
            )
        for entries, key_terms in results:
            add(dk, entries, key_terms)

    @pl.loop(0, rows // 4)
    def _(r):
        for u in range(4):
            dk_low[:, 4 * r + u] = dk[:, 4 * r + u].astype(jnp.bfloat16)
        for u in range(4):
            dv_low[:, 4 * r + u] = dv[:, 4 * r + u].astype(jnp.bfloat16)


def attend(ih, qh, gh, va, lifted, inverse):
    held = pltpu.VMEM(va.shape, jnp.bfloat16)
    work = lifted.size * HD * 2
    return pl.pallas_call(
        attend_kernel,
        name="attend",
        out_shape=(pltpu.VMEM(lifted.shape, jnp.bfloat16), held, held),
        in_specs=[ANY] + [VMEM] * 5,
        out_specs=(VMEM,) * 3,
        scratch_shapes=[
            pltpu.VMEM(va.shape, jnp.float32),
            pltpu.VMEM(va.shape, jnp.float32),
            pltpu.SMEM(ih.shape, jnp.int32),
            pltpu.SemaphoreType.DMA,
        ],
        input_output_aliases={4: 0, 3: 2},
        compiler_params=pltpu.CompilerParams(vmem_limit_bytes=28 * MiB),
        cost_estimate=pl.CostEstimate(flops=3 * work, bytes_accessed=4 * MiB, transcendentals=0),
    )(ih, *in_vmem(qh, gh, va, lifted, inverse))


def give_kernel(
    nz, nx,
    i_hbm, ka_hbm, dscore_ref, dk_ref, dv_ref,
    gq, gk, gv,
    i_ref, ka, dq_ref, other, total, passed, arrived,
    s_q, r_q, s_out, r_out, s_c, r_c, s_f, r_f, s_y, r_y, own_q, own_out, own_k, own_i,
):
    y, z, x, c = place()
    chips = nz * nx
    rows = gk.shape[0]
    half = rows // 2
    me = z * nx + x
    up, down, far = lax.rem(y + 1, 4), lax.rem(y + 3, 4), lax.rem(y + 2, 4)
    pair = (dk_ref, dv_ref)
    outs = (gk, gv)
    greet(nz, nx)

    at = (far, up, down, y)
    bands = [(dz, h) for dz in sorted(range(nz), key=lambda dz: -min(dz, nz - dz)) for h in (0, 1)]

    def rows_at(t, slot, dz, h, core):
        first = core * chips + lax.rem(z + dz, nz) * nx
        return pair[t].at[at[slot], pl.ds(first, nx), pl.ds(h * half, half)]

    def across(t, slot, dz, h):
        return remote(
            rows_at(t, slot, dz, h, 1 - c), other.at[slot, t, dz, h],
            s_c.at[slot, t, dz, h], r_c.at[slot, t, dz, h], (y, z, x, 1 - c),
        )

    for dz, h in bands:
        for slot in range(4):
            for t in (0, 1):
                across(t, slot, dz, h).start()

    def columns(head):
        return pl.ds(pl.multiple_of(head * HD, HD), HD)

    def chip(d):
        pz, px = lax.rem(z + d // nx, nz), lax.rem(x + lax.rem(d, nx), nx)
        return pz * nx + px, (y, pz, px, c)

    def query_out(d):
        head, where = chip(d)
        return remote(dq_ref.at[head], gq.at[:, :, columns(me)], s_q.at[d], r_q.at[d], where)

    def key_out(d, t, h):
        _, where = chip(d)
        px = lax.rem(x + lax.rem(d, nx), nx)
        return remote(
            total.at[3, t, d // nx, h, px], outs[t].at[pl.ds(h * half, half), :, columns(me)],
            s_out.at[t, h, d], r_out.at[t, h, d], where,
        )

    def key_own(t, h):
        return pltpu.make_async_copy(
            total.at[3, t, 0, h, x], outs[t].at[pl.ds(h * half, half), :, columns(me)],
            own_out.at[t, h],
        )

    query_own = pltpu.make_async_copy(dq_ref.at[me], gq.at[:, :, columns(me)], own_q)
    keys_in = pltpu.make_async_copy(ka_hbm, ka, own_k)
    keys_in.start()
    lists = pltpu.make_async_copy(i_hbm, i_ref, own_i)
    lists.start()
    pairs = dscore_ref.shape[0]
    per = dq_ref.shape[1]
    span_len = dq_ref.shape[2]
    unroll = min(4, pairs)

    def queries():
        keys_in.wait()
        lists.wait()

        @pl.loop(0, pairs // unroll)
        def _(step):
            for u in range(unroll):
                p = step * unroll + u
                both = contract(dscore_ref[p], rows_of(ka, entries_of(i_ref, p, per)), 0, 0)
                sa, sb = 2 * p, 2 * p + 1
                dq_ref[sa // per, lax.rem(sa, per)] = both[:span_len, :HD].astype(jnp.bfloat16)
                dq_ref[sb // per, lax.rem(sb, per)] = both[span_len:, HD:].astype(jnp.bfloat16)

        query_own.start()
        for dz, dx in offsets(nz, nx):
            query_out(dz * nx + dx).start()

    def f32(a):
        return a.astype(jnp.float32)

    def add(dst, *terms):
        @pl.loop(0, nx)
        def _(i):
            sums = f32(terms[0][i])
            for term in terms[1:]:
                sums = sums + f32(term[i])
            dst[i] = sums.astype(jnp.bfloat16)

    def both_cores(t, slot, dz, h):
        across(t, slot, dz, h).wait_recv()
        return rows_at(t, slot, dz, h, c), other.at[slot, t, dz, h]

    def far_copy(t, dz, h):
        return remote(
            total.at[0, t, dz, h], passed.at[t, dz, h], s_f.at[t, dz, h], r_f.at[t, dz, h],
            ((up, down)[t], z, x, c),
        )

    def near_copy(t, slot, dz, h):
        return remote(
            total.at[slot, t, dz, h], arrived.at[slot - 1, t, dz, h],
            s_y.at[slot - 1, t, dz, h], r_y.at[slot - 1, t, dz, h],
            ((up, down)[slot - 1], z, x, c),
        )

    def direct(dz, h):
        for t in (0, 1):
            add(total.at[0, t, dz, h], *both_cores(t, 0, dz, h))
            far_copy(t, dz, h).start()
        for t, slot in ((1, 1), (0, 2)):
            add(total.at[slot, t, dz, h], *both_cores(t, slot, dz, h))
            near_copy(t, slot, dz, h).start()

    def merged(dz, h):
        for t, slot in ((0, 1), (1, 2)):
            terms = both_cores(t, slot, dz, h)
            far_copy(t, dz, h).wait_recv()
            add(total.at[slot, t, dz, h], *terms, passed.at[t, dz, h])
            near_copy(t, slot, dz, h).start()

    def final(dz, h):
        for t in (0, 1):
            terms = both_cores(t, 3, dz, h)
            near_copy(t, 1, dz, h).wait_recv()
            near_copy(t, 2, dz, h).wait_recv()
            add(total.at[3, t, dz, h], *terms, arrived.at[0, t, dz, h], arrived.at[1, t, dz, h])
            for dx in range(nx):
                if dz or dx:
                    key_out(dz * nx + dx, t, h).start()
                else:
                    key_own(t, h).start()

    lag = 2
    for step in range(len(bands) + 2 * lag):
        if step < len(bands):
            direct(*bands[step])
        if step == 2:
            queries()
        if lag <= step < len(bands) + lag:
            merged(*bands[step - lag])
        if step >= 2 * lag:
            final(*bands[step - 2 * lag])

    @pl.loop(1, chips)
    def _(d):
        query_out(d).wait()
        for t in (0, 1):
            for h in (0, 1):
                key_out(d, t, h).wait()

    query_own.wait()
    for t in (0, 1):
        for h in (0, 1):
            key_own(t, h).wait()

            @pl.loop(0, nz)
            def _(dz):
                far_copy(t, dz, h).wait_send()
                for slot in range(4):
                    across(t, slot, dz, h).wait_send()
                for slot in (1, 2):
                    near_copy(t, slot, dz, h).wait_send()


def give(nz, nx, spans, ih, ka, dscore, dk, dv):
    chips = nz * nx
    _, all_rows, tok, _ = dk.shape
    part = all_rows // 2
    rows = part // chips
    piece = (nz, 2, nx, rows // 2, tok, HD)
    span_len = dscore.shape[2] // 2
    bf16 = jnp.bfloat16
    dma = pltpu.SemaphoreType.DMA
    def split(sums):
        return sums.reshape(4, 2 * chips, rows, tok, HD)

    row_out = pltpu.VMEM((part // chips, tok, chips * HD), bf16)
    return pl.pallas_call(
        functools.partial(give_kernel, nz, nx),
        name="give",
        out_shape=(pltpu.VMEM((spans, span_len, chips * HD), bf16), row_out, row_out),
        in_specs=[ANY, HBM] + [VMEM] * 3,
        out_specs=(ANY,) * 3,
        scratch_shapes=[
            pltpu.SMEM(ih.shape, jnp.int32),
            pltpu.VMEM(ka.shape, bf16),
            pltpu.VMEM((chips, spans, span_len, HD), bf16),
            pltpu.VMEM((4, 2) + piece, bf16),
            pltpu.VMEM((4, 2) + piece, bf16),
            pltpu.VMEM((2,) + piece, bf16),
            pltpu.VMEM((2, 2) + piece, bf16),
            dma((chips,)), dma((chips,)), dma((2, 2, chips)), dma((2, 2, chips)),
            dma((4, 2, nz, 2)), dma((4, 2, nz, 2)), dma((2, nz, 2)), dma((2, nz, 2)),
            dma((2, 2, nz, 2)), dma((2, 2, nz, 2)), dma, dma((2, 2)), dma, dma,
        ],
        compiler_params=pltpu.CompilerParams(
            collective_id=1, has_side_effects=True, vmem_limit_bytes=32 * MiB
        ),
    )(ih, *in_hbm(ka), *in_vmem(dscore, split(dk), split(dv)))


def write_kernel(*refs):
    count = (len(refs) - 1) // 2
    copies = [
        pltpu.make_async_copy(refs[i], refs[count + i], refs[-1].at[i]) for i in range(count)
    ]
    for copy in copies:
        copy.start()
    for copy in copies:
        copy.wait()


def write(*arrays):
    return pl.pallas_call(
        write_kernel,
        name="write",
        out_shape=tuple(pltpu.HBM(a.shape, a.dtype) for a in arrays),
        in_specs=[VMEM] * len(arrays),
        out_specs=(HBM,) * len(arrays),
        scratch_shapes=[pltpu.SemaphoreType.DMA((len(arrays),))],
        compiler_params=pltpu.CompilerParams(vmem_limit_bytes=8 * MiB),
    )(*in_vmem(*arrays))


def on_device(nz, nx, query, grad_out, keys, values, owner_list, row_list):
    qh, gh, va, ih, lifted, inverse, ka = bring(
        nz, nx, query, grad_out, keys, values, owner_list, row_list
    )
    dscore, dk, dv = attend(ih, qh, gh, va, lifted, inverse)
    return write(*give(nz, nx, query.shape[0], ih, ka, dscore, dk, dv))


def solution(mesh):
    groups, retr = mesh.devices.shape
    nx = 4 if retr == 32 else 2
    nz = retr // (2 * nx)
    fine = Mesh(mesh.devices.reshape(groups, nz, nx, 2), ("y", "z", "x", "c"))
    all_axes = ("y", "z", "x", "c")
    owner = ("z", "x", "c")
    return jax.shard_map(
        functools.partial(on_device, nz, nx),
        mesh=fine,
        in_specs=(
            P(all_axes, None, None),
            P(all_axes, None, None),
            P(owner, None, None),
            P(owner, None, None),
            P(all_axes, None),
            P(all_axes, None),
        ),
        out_specs=(P(all_axes, None, None), P(owner, "y", None), P(owner, "y", None)),
        check_vma=False,
    )
```

```python
import functools

import jax
import jax.numpy as jnp
import numpy as np
from jax import lax
from jax.experimental import pallas as pl
from jax.experimental.pallas import tpu as pltpu
from jax.sharding import Mesh
from jax.sharding import PartitionSpec as P

HD = 128
MiB = 1024 * 1024
ANY = pl.BlockSpec(memory_space=pl.ANY)
VMEM = pl.BlockSpec(memory_space=pltpu.VMEM)
SMEM = pl.BlockSpec(memory_space=pltpu.SMEM)
HBM = pl.BlockSpec(memory_space=pltpu.HBM)


def in_hbm(*arrays):
    return tuple(pltpu.with_memory_space_constraint(a, pltpu.HBM) for a in arrays)


def in_vmem(*arrays):
    return tuple(pltpu.with_memory_space_constraint(a, pltpu.VMEM) for a in arrays)


def place():
    return tuple(lax.axis_index(name) for name in ("y", "z", "x", "c"))


def remote(src, dst, send, recv, where):
    return pltpu.make_async_remote_copy(
        src_ref=src,
        dst_ref=dst,
        send_sem=send,
        recv_sem=recv,
        device_id=where,
        device_id_type=pl.DeviceIdType.MESH,
    )


def greet(nz, nx):
    y, z, x, c = place()
    barrier = pltpu.get_barrier_semaphore()

    def hello(where):
        pl.semaphore_signal(barrier, inc=1, device_id=where, device_id_type=pl.DeviceIdType.MESH)

    @pl.loop(1, nz * nx)
    def _(d):
        hello((y, lax.rem(z + d // nx, nz), lax.rem(x + lax.rem(d, nx), nx), c))

    hello((lax.rem(y + 1, 4), z, x, c))
    hello((lax.rem(y + 3, 4), z, x, c))
    hello((y, z, x, 1 - c))
    pl.semaphore_wait(barrier, nz * nx - 1 + 3)


def contract(a, b, da, db):
    return lax.dot_general(a, b, (((da,), (db,)), ((), ())), preferred_element_type=jnp.float32)


def diagonal(a, b):
    empty = jnp.zeros_like(a)
    return jnp.concatenate(
        [jnp.concatenate([a, empty], axis=1), jnp.concatenate([empty, b], axis=1)], axis=0
    )


def entries_of(i_ref, pair, per):
    return [
        i_ref[s // per, n, lax.rem(s, per)] for s in (2 * pair, 2 * pair + 1) for n in (0, 1)
    ]


def rows_of(ref, entries):
    quarters, _, tok, _ = ref.shape
    taken = [ref[:, e].reshape(quarters * tok, HD) for e in entries]
    return jnp.concatenate(
        [jnp.concatenate(taken[:2], axis=0), jnp.concatenate(taken[2:], axis=0)], axis=1
    )


def tokens_of(ref, pair):
    per = ref.shape[1]
    sa, sb = 2 * pair, 2 * pair + 1
    return diagonal(ref[sa // per, lax.rem(sa, per)], ref[sb // per, lax.rem(sb, per)])


def offsets(nz, nx):
    steps = [(dz, dx) for dz in range(nz) for dx in range(nx) if dz or dx]

    def hops(step):
        return min(step[0], nz - step[0]) + min(step[1], nx - step[1])

    return sorted(steps, key=hops)


def bring_kernel(
    nz, nx,
    q_ref, g_ref, k_ref, v_ref, owner_ref, row_ref,
    qh, gh, va, ih, lifted_ref, inverse_ref, ka_hbm,
    ka, i_ref, i_smem, o_vmem, w_vmem, s_in, r_in, s_y, r_y, s_c, r_c, own,
):
    y, z, x, c = place()
    chips = nz * nx
    rows = k_ref.shape[0]
    part = chips * rows
    quarter = k_ref.shape[1] // 4
    me = z * nx + x
    up, down, far = lax.rem(y + 1, 4), lax.rem(y + 3, 4), lax.rem(y + 2, 4)
    lists = (
        pltpu.make_async_copy(owner_ref, o_vmem, own.at[7]),
        pltpu.make_async_copy(row_ref, w_vmem, own.at[8]),
    )
    for copy in lists:
        copy.start()
    greet(nz, nx)
    for copy in lists:
        copy.wait()

    owners = o_vmem[...]
    entries = (owners & 1) * part + (owners >> 1) * rows + w_vmem[...]
    i_ref[...] = jnp.zeros_like(i_ref)
    i_ref[: entries.shape[0], : entries.shape[1]] = entries

    def columns(head):
        return pl.ds(pl.multiple_of(head * HD, HD), HD)

    def token_part(ref, head):
        return ref.at[:, pl.ds(pl.multiple_of(y * quarter, quarter), quarter), columns(head)]

    def landing(ref):
        return ref.at[y, pl.ds(c * part + me * rows, rows)]

    def sides(t, head):
        if t < 2:
            return token_part((k_ref, v_ref)[t], head), landing((ka, va)[t])
        if t < 4:
            return (q_ref, g_ref)[t - 2].at[:, :, columns(head)], (qh, gh)[t - 2].at[me]
        return i_ref, ih.at[me]

    def to_chip(t, d):
        pz, px = lax.rem(z + d // nx, nz), lax.rem(x + lax.rem(d, nx), nx)
        return remote(*sides(t, pz * nx + px), s_in.at[t, d], r_in.at[t, d], (y, pz, px, c))

    def keep(t):
        return pltpu.make_async_copy(*sides(t, me), own.at[t])

    def arrived(t):
        @pl.loop(1, chips)
        def _(d):
            to_chip(t, d).wait_recv()

        keep(t).wait()

    def send(t):
        for dz, dx in offsets(nz, nx):
            to_chip(t, dz * nx + dx).start()
        keep(t).start()

    for t in (0, 1, 4, 2):
        send(t)

    def chunk(t, at):
        return (ka, va)[t].at[at, pl.ds(c * part, part)]

    def along_y(t, at, slot, where):
        return remote(
            chunk(t, at), chunk(t, at), s_y.at[t, slot], r_y.at[t, slot], (where, z, x, c)
        )

    def across(t, at, slot):
        return remote(
            chunk(t, at), chunk(t, at), s_c.at[t, slot], r_c.at[t, slot], (y, z, x, 1 - c)
        )

    arrived(0)
    along_y(0, y, 0, up).start()
    along_y(0, y, 1, down).start()
    across(0, y, 0).start()
    arrived(1)
    along_y(1, y, 1, down).start()
    across(1, y, 0).start()
    send(3)

    def all_across(t):
        along_y(t, far, 2, up).wait_recv()
        across(t, far, 3).start()
        for slot in range(4):
            across(t, y, slot).wait_recv()

    arrived(4)
    entry_copy = pltpu.make_async_copy(ih, i_smem, own.at[5])
    entry_copy.start()
    entry_copy.wait()
    along_y(0, down, 0, up).wait_recv()
    along_y(0, down, 2, up).start()
    along_y(1, y, 0, up).start()
    across(0, down, 1).start()
    along_y(0, up, 1, down).wait_recv()
    across(0, up, 2).start()
    along_y(1, up, 1, down).wait_recv()
    along_y(1, up, 2, down).start()
    across(1, up, 2).start()
    all_across(0)
    keep_keys = pltpu.make_async_copy(ka, ka_hbm, own.at[6])
    keep_keys.start()
    arrived(2)

    to_base2 = HD ** -0.5 * float(np.log2(np.e))
    pairs = lifted_ref.shape[0]
    unroll = min(8, pairs)

    def weigh(first, last):
        @pl.loop(first, last)
        def _(step):
            for u in range(unroll):
                p = step * unroll + u
                scores = contract(rows_of(ka, entries_of(i_smem, p, qh.shape[1])), tokens_of(qh, p), 1, 1)
                lifted = jnp.exp2((scores - jnp.max(scores, axis=0, keepdims=True)) * to_base2)
                inverse_ref[p] = 1.0 / jnp.sum(lifted, axis=0, keepdims=True)
                lifted_ref[p] = lifted.astype(jnp.bfloat16)

    steps = pairs // unroll
    weigh(0, steps // 2)
    along_y(1, down, 0, up).wait_recv()
    across(1, down, 1).start()
    weigh(steps // 2, steps)
    all_across(1)
    arrived(3)
    keep_keys.wait()
    for t in range(5):

        @pl.loop(1, chips)
        def _(d):
            to_chip(t, d).wait_send()

    for t in (0, 1):
        for slot in range(3):
            along_y(t, y, slot, up).wait_send()
        for slot in range(4):
            across(t, y, slot).wait_send()


def bring(nz, nx, query, grad_out, keys, values, owner_list, row_list):
    chips = nz * nx
    rows, tokens, _ = keys.shape
    spans, span_len, _ = query.shape
    bf16 = jnp.bfloat16
    held = pltpu.VMEM((4, 2 * chips * rows, tokens // 4, HD), bf16)
    heads = pltpu.VMEM((chips, spans, span_len, HD), bf16)
    pairs = chips * spans // 2
    listed = (8, HD)
    dma = pltpu.SemaphoreType.DMA
    return pl.pallas_call(
        functools.partial(bring_kernel, nz, nx),
        name="bring",
        out_shape=(
            heads, heads, held,
            jax.ShapeDtypeStruct((chips,) + listed, jnp.int32),
            pltpu.VMEM((pairs, 2 * tokens, 2 * span_len), bf16),
            pltpu.VMEM((pairs, 1, 2 * span_len), jnp.float32),
            pltpu.HBM(held.shape, bf16),
        ),
        in_specs=[HBM] * 6,
        out_specs=(VMEM,) * 3 + (ANY,) + (VMEM,) * 2 + (HBM,),
        scratch_shapes=[
            pltpu.VMEM(held.shape, bf16),
            pltpu.VMEM(listed, jnp.int32),
            pltpu.SMEM((chips,) + listed, jnp.int32),
            pltpu.VMEM((2, spans), jnp.int32),
            pltpu.VMEM((2, spans), jnp.int32),
            dma((5, chips)), dma((5, chips)), dma((2, 3)), dma((2, 3)), dma((2, 4)), dma((2, 4)), dma((9,)),
        ],
        compiler_params=pltpu.CompilerParams(
            collective_id=0, has_side_effects=True, vmem_limit_bytes=14 * MiB
        ),
    )(*in_hbm(query, grad_out, keys, values, owner_list.T, row_list.T))


def attend_kernel(
    i_hbm, qh, gh, va, lifted_ref, inverse_ref, dscore_ref, dk_low, dv_low, dk, dv, i_ref, sem
):
    quarters, rows, tok, _ = va.shape
    tokens = quarters * tok
    scaling = HD ** -0.5
    pairs = lifted_ref.shape[0]
    unroll = min(8, pairs)

    def add(sums, entries, terms):
        for at, e in enumerate(entries):
            rs = slice(at % 2 * tokens, (at % 2 + 1) * tokens)
            cs = slice(at // 2 * HD, (at // 2 + 1) * HD)
            sums[:, e] += terms[rs, cs].reshape(quarters, tok, HD)

    def gradients(p):
        entries = entries_of(i_ref, p, qh.shape[1])
        grads = tokens_of(gh, p)
        dprob = contract(rows_of(va, entries), grads, 1, 1)
        inverse = inverse_ref[p]
        lifted = lifted_ref[p].astype(jnp.float32)
        delta = jnp.sum(lifted * dprob, axis=0, keepdims=True) * inverse
        chance_low = (lifted * inverse).astype(jnp.bfloat16)
        dscore = (lifted * (inverse * scaling) * (dprob - delta)).astype(jnp.bfloat16)
        dscore_ref[p] = dscore
        return entries, contract(chance_low, grads, 1, 0)

    lists = pltpu.make_async_copy(i_hbm, i_ref, sem)
    lists.start()

    @pl.loop(0, rows // 4)
    def _(r):
        dk[:, pl.ds(4 * r, 4)] = jnp.zeros((quarters, 4, tok, HD), jnp.float32)
        dv[:, pl.ds(4 * r, 4)] = jnp.zeros((quarters, 4, tok, HD), jnp.float32)

    lists.wait()

    @pl.loop(0, pairs // unroll)
    def _(step):
        results = [gradients(step * unroll + u) for u in range(unroll)]
        for entries, value_terms in results:
            add(dv, entries, value_terms)

    @pl.loop(0, pairs // unroll)
    def _(step):
        results = []
        for u in range(unroll):
            p = step * unroll + u
            results.append(
                (entries_of(i_ref, p, qh.shape[1]), contract(dscore_ref[p], tokens_of(qh, p), 1, 0))
            )
        for entries, key_terms in results:
            add(dk, entries, key_terms)

    @pl.loop(0, rows // 4)
    def _(r):
        for u in range(4):
            dk_low[:, 4 * r + u] = dk[:, 4 * r + u].astype(jnp.bfloat16)
        for u in range(4):
            dv_low[:, 4 * r + u] = dv[:, 4 * r + u].astype(jnp.bfloat16)


def attend(ih, qh, gh, va, lifted, inverse):
    held = pltpu.VMEM(va.shape, jnp.bfloat16)
    work = lifted.size * HD * 2
    return pl.pallas_call(
        attend_kernel,
        name="attend",
        out_shape=(pltpu.VMEM(lifted.shape, jnp.bfloat16), held, held),
        in_specs=[ANY] + [VMEM] * 5,
        out_specs=(VMEM,) * 3,
        scratch_shapes=[
            pltpu.VMEM(va.shape, jnp.float32),
            pltpu.VMEM(va.shape, jnp.float32),
            pltpu.SMEM(ih.shape, jnp.int32),
            pltpu.SemaphoreType.DMA,
        ],
        input_output_aliases={4: 0, 3: 2},
        compiler_params=pltpu.CompilerParams(vmem_limit_bytes=28 * MiB),
        cost_estimate=pl.CostEstimate(flops=3 * work, bytes_accessed=4 * MiB, transcendentals=0),
    )(ih, *in_vmem(qh, gh, va, lifted, inverse))


def give_kernel(
    nz, nx,
    i_hbm, ka_hbm, dscore_ref, dk_ref, dv_ref,
    gq, gk, gv,
    i_ref, ka, dq_ref, other, total, passed, arrived,
    s_q, r_q, s_out, r_out, s_c, r_c, s_f, r_f, s_y, r_y, own_q, own_out, own_k, own_i,
):
    y, z, x, c = place()
    chips = nz * nx
    rows = gk.shape[0]
    half = rows // 2
    me = z * nx + x
    up, down, far = lax.rem(y + 1, 4), lax.rem(y + 3, 4), lax.rem(y + 2, 4)
    pair = (dk_ref, dv_ref)
    outs = (gk, gv)
    greet(nz, nx)

    at = (far, up, down, y)
    bands = [(dz, h) for dz in sorted(range(nz), key=lambda dz: -min(dz, nz - dz)) for h in (0, 1)]

    def rows_at(t, slot, dz, h, core):
        first = core * chips + lax.rem(z + dz, nz) * nx
        return pair[t].at[at[slot], pl.ds(first, nx), pl.ds(h * half, half)]

    def across(t, slot, dz, h):
        return remote(
            rows_at(t, slot, dz, h, 1 - c), other.at[slot, t, dz, h],
            s_c.at[slot, t, dz, h], r_c.at[slot, t, dz, h], (y, z, x, 1 - c),
        )

    for dz, h in bands:
        for slot in range(4):
            for t in (0, 1):
                across(t, slot, dz, h).start()

    def columns(head):
        return pl.ds(pl.multiple_of(head * HD, HD), HD)

    def chip(d):
        pz, px = lax.rem(z + d // nx, nz), lax.rem(x + lax.rem(d, nx), nx)
        return pz * nx + px, (y, pz, px, c)

    def query_out(d):
        head, where = chip(d)
        return remote(dq_ref.at[head], gq.at[:, :, columns(me)], s_q.at[d], r_q.at[d], where)

    def key_out(d, t, h):
        _, where = chip(d)
        px = lax.rem(x + lax.rem(d, nx), nx)
        return remote(
            total.at[3, t, d // nx, h, px], outs[t].at[pl.ds(h * half, half), :, columns(me)],
            s_out.at[t, h, d], r_out.at[t, h, d], where,
        )

    def key_own(t, h):
        return pltpu.make_async_copy(
            total.at[3, t, 0, h, x], outs[t].at[pl.ds(h * half, half), :, columns(me)],
            own_out.at[t, h],
        )

    query_own = pltpu.make_async_copy(dq_ref.at[me], gq.at[:, :, columns(me)], own_q)
    keys_in = pltpu.make_async_copy(ka_hbm, ka, own_k)
    keys_in.start()
    lists = pltpu.make_async_copy(i_hbm, i_ref, own_i)
    lists.start()
    pairs = dscore_ref.shape[0]
    per = dq_ref.shape[1]
    span_len = dq_ref.shape[2]
    unroll = min(4, pairs)

    def queries():
        keys_in.wait()
        lists.wait()

        @pl.loop(0, pairs // unroll)
        def _(step):
            for u in range(unroll):
                p = step * unroll + u
                both = contract(dscore_ref[p], rows_of(ka, entries_of(i_ref, p, per)), 0, 0)
                sa, sb = 2 * p, 2 * p + 1
                dq_ref[sa // per, lax.rem(sa, per)] = both[:span_len, :HD].astype(jnp.bfloat16)
                dq_ref[sb // per, lax.rem(sb, per)] = both[span_len:, HD:].astype(jnp.bfloat16)

        query_own.start()
        for dz, dx in offsets(nz, nx):
            query_out(dz * nx + dx).start()

    def f32(a):
        return a.astype(jnp.float32)

    def add(dst, *terms):
        @pl.loop(0, nx)
        def _(i):
            sums = f32(terms[0][i])
            for term in terms[1:]:
                sums = sums + f32(term[i])
            dst[i] = sums.astype(jnp.bfloat16)

    def both_cores(t, slot, dz, h):
        across(t, slot, dz, h).wait_recv()
        return rows_at(t, slot, dz, h, c), other.at[slot, t, dz, h]

    def far_copy(t, dz, h):
        return remote(
            total.at[0, t, dz, h], passed.at[t, dz, h], s_f.at[t, dz, h], r_f.at[t, dz, h],
            ((up, down)[t], z, x, c),
        )

    def near_copy(t, slot, dz, h):
        return remote(
            total.at[slot, t, dz, h], arrived.at[slot - 1, t, dz, h],
            s_y.at[slot - 1, t, dz, h], r_y.at[slot - 1, t, dz, h],
            ((up, down)[slot - 1], z, x, c),
        )

    def direct(dz, h):
        for t in (0, 1):
            add(total.at[0, t, dz, h], *both_cores(t, 0, dz, h))
            far_copy(t, dz, h).start()
        for t, slot in ((1, 1), (0, 2)):
            add(total.at[slot, t, dz, h], *both_cores(t, slot, dz, h))
            near_copy(t, slot, dz, h).start()

    def merged(dz, h):
        for t, slot in ((0, 1), (1, 2)):
            terms = both_cores(t, slot, dz, h)
            far_copy(t, dz, h).wait_recv()
            add(total.at[slot, t, dz, h], *terms, passed.at[t, dz, h])
            near_copy(t, slot, dz, h).start()

    def final(dz, h):
        for t in (0, 1):
            terms = both_cores(t, 3, dz, h)
            near_copy(t, 1, dz, h).wait_recv()
            near_copy(t, 2, dz, h).wait_recv()
            add(total.at[3, t, dz, h], *terms, arrived.at[0, t, dz, h], arrived.at[1, t, dz, h])
            for dx in range(nx):
                if dz or dx:
                    key_out(dz * nx + dx, t, h).start()
                else:
                    key_own(t, h).start()

    lag = 2
    for step in range(len(bands) + 2 * lag):
        if step < len(bands):
            direct(*bands[step])
        if step == 2:
            queries()
        if lag <= step < len(bands) + lag:
            merged(*bands[step - lag])
        if step >= 2 * lag:
            final(*bands[step - 2 * lag])

    @pl.loop(1, chips)
    def _(d):
        query_out(d).wait()
        for t in (0, 1):
            for h in (0, 1):
                key_out(d, t, h).wait()

    query_own.wait()
    for t in (0, 1):
        for h in (0, 1):
            key_own(t, h).wait()

            @pl.loop(0, nz)
            def _(dz):
                far_copy(t, dz, h).wait_send()
                for slot in range(4):
                    across(t, slot, dz, h).wait_send()
                for slot in (1, 2):
                    near_copy(t, slot, dz, h).wait_send()


def give(nz, nx, spans, ih, ka, dscore, dk, dv):
    chips = nz * nx
    _, all_rows, tok, _ = dk.shape
    part = all_rows // 2
    rows = part // chips
    piece = (nz, 2, nx, rows // 2, tok, HD)
    span_len = dscore.shape[2] // 2
    bf16 = jnp.bfloat16
    dma = pltpu.SemaphoreType.DMA
    def split(sums):
        return sums.reshape(4, 2 * chips, rows, tok, HD)

    row_out = pltpu.VMEM((part // chips, tok, chips * HD), bf16)
    return pl.pallas_call(
        functools.partial(give_kernel, nz, nx),
        name="give",
        out_shape=(pltpu.VMEM((spans, span_len, chips * HD), bf16), row_out, row_out),
        in_specs=[ANY, HBM] + [VMEM] * 3,
        out_specs=(ANY,) * 3,
        scratch_shapes=[
            pltpu.SMEM(ih.shape, jnp.int32),
            pltpu.VMEM(ka.shape, bf16),
            pltpu.VMEM((chips, spans, span_len, HD), bf16),
            pltpu.VMEM((4, 2) + piece, bf16),
            pltpu.VMEM((4, 2) + piece, bf16),
            pltpu.VMEM((2,) + piece, bf16),
            pltpu.VMEM((2, 2) + piece, bf16),
            dma((chips,)), dma((chips,)), dma((2, 2, chips)), dma((2, 2, chips)),
            dma((4, 2, nz, 2)), dma((4, 2, nz, 2)), dma((2, nz, 2)), dma((2, nz, 2)),
            dma((2, 2, nz, 2)), dma((2, 2, nz, 2)), dma, dma((2, 2)), dma, dma,
        ],
        compiler_params=pltpu.CompilerParams(
            collective_id=1, has_side_effects=True, vmem_limit_bytes=32 * MiB
        ),
    )(ih, *in_hbm(ka), *in_vmem(dscore, split(dk), split(dv)))


def write_kernel(*refs):
    count = (len(refs) - 1) // 2
    copies = [
        pltpu.make_async_copy(refs[i], refs[count + i], refs[-1].at[i]) for i in range(count)
    ]
    for copy in copies:
        copy.start()
    for copy in copies:
        copy.wait()


def write(*arrays):
    return pl.pallas_call(
        write_kernel,
        name="write",
        out_shape=tuple(pltpu.HBM(a.shape, a.dtype) for a in arrays),
        in_specs=[VMEM] * len(arrays),
        out_specs=(HBM,) * len(arrays),
        scratch_shapes=[pltpu.SemaphoreType.DMA((len(arrays),))],
        compiler_params=pltpu.CompilerParams(vmem_limit_bytes=8 * MiB),
    )(*in_vmem(*arrays))


def on_device(nz, nx, query, grad_out, keys, values, owner_list, row_list):
    qh, gh, va, ih, lifted, inverse, ka = bring(
        nz, nx, query, grad_out, keys, values, owner_list, row_list
    )
    dscore, dk, dv = attend(ih, qh, gh, va, lifted, inverse)
    return write(*give(nz, nx, query.shape[0], ih, ka, dscore, dk, dv))


def solution(mesh):
    groups, retr = mesh.devices.shape
    nx = 4 if retr == 32 else 2
    nz = retr // (2 * nx)
    fine = Mesh(mesh.devices.reshape(groups, nz, nx, 2), ("y", "z", "x", "c"))
    all_axes = ("y", "z", "x", "c")
    owner = ("z", "x", "c")
    return jax.shard_map(
        functools.partial(on_device, nz, nx),
        mesh=fine,
        in_specs=(
            P(all_axes, None, None),
            P(all_axes, None, None),
            P(owner, None, None),
            P(owner, None, None),
            P(all_axes, None),
            P(all_axes, None),
        ),
        out_specs=(P(all_axes, None, None), P(owner, "y", None), P(owner, "y", None)),
        check_vma=False,
    )
```
